32 devices in a mesh: clip: 4 (over z), tm: 2 (over y), height: 4 (over x, core).
Axes of the slice: x: 2, y: 2, z: 4, core: 2. Of those that a mesh axis runs over, the one named last changes fastest.
Arguments:
- clip_input: bfloat16 [4, 8, 24, 24, 384], P('clip', 'tm', 'height'), may hold values from -6 to 6
- memory: bfloat16 [4, 2, 2, 8, 24, 24, 768], P('clip', None, None, 'tm', 'height'), may hold values from -8 to 8
- mem_len: int32 [4], P('clip'), may hold values from 0 to 2, as said below
- res_id: int32 [4], P('clip'), may hold values 0 or 1
- norm1_gain: float32 [384], replicated, may hold values from 0.5 to 1.5
- norm1_bias: float32 [384], replicated, may hold values from -1.75 to 1.75
- w_qkv: bfloat16 [2304, 384], replicated, may hold values from -0.5 to 0.5
- b_qkv: float32 [2304], replicated, may hold values from -1.75 to 1.75
- conv_kv: float32 [2, 3, 3, 3, 768], replicated, may hold values from -1.25 to 1.25
- compress: float32 [2, 2, 2, 768], replicated, may hold values from -3 to 3
- rel_t: float32 [15, 96], replicated, may hold values from -0.75 to 0.75
- rel_h: float32 [47, 96], replicated, may hold values from -0.75 to 0.75
- rel_w: float32 [47, 96], replicated, may hold values from -0.75 to 0.75
- w_proj: bfloat16 [768, 768], replicated, may hold values from -0.21875 to 0.21875
- b_proj: float32 [768], replicated, may hold values from -1.75 to 1.75
- w_short: bfloat16 [768, 384], replicated, may hold values from -0.3125 to 0.3125
- b_short: float32 [768], replicated, may hold values from -1.75 to 1.75
- norm2_gain: float32 [768], replicated, may hold values from 0.5 to 1.5
- norm2_bias: float32 [768], replicated, may hold values from -1.75 to 1.75
- w_fc1: bfloat16 [3072, 768], replicated, may hold values from -0.21875 to 0.21875
- b_fc1: float32 [3072], replicated, may hold values from -1.75 to 1.75
- w_fc2: bfloat16 [768, 3072], replicated, may hold values from -0.109375 to 0.109375
- b_fc2: float32 [768], replicated, may hold values from -1.75 to 1.75
- cotangent: bfloat16 [4, 8, 12, 12, 768], P('clip', 'tm', 'height'), may hold values from -6 to 6
Outputs:
- output: bfloat16 [4, 8, 12, 12, 768], P('clip', 'tm', 'height')
- input_grad: bfloat16 [4, 8, 24, 24, 384], P('clip', 'tm', 'height')
- grad_norm1_gain: float32 [384], replicated
- grad_norm1_bias: float32 [384], replicated
- grad_w_qkv: float32 [2304, 384], P('clip', ('tm', 'height'))
- grad_b_qkv: float32 [2304], replicated
- grad_conv_kv: float32 [2, 3, 3, 3, 768], replicated
- grad_compress: float32 [2, 2, 2, 768], replicated
- grad_rel_t: float32 [15, 96], replicated
- grad_rel_h: float32 [47, 96], replicated
- grad_rel_w: float32 [47, 96], replicated
- grad_w_proj: float32 [768, 768], P('clip', ('tm', 'height'))
- grad_b_proj: float32 [768], replicated
- grad_w_short: float32 [768, 384], P('clip', ('tm', 'height'))
- grad_b_short: float32 [768], replicated
- grad_norm2_gain: float32 [768], replicated
- grad_norm2_bias: float32 [768], replicated
- grad_w_fc1: float32 [3072, 768], P('clip', ('tm', 'height'))
- grad_b_fc1: float32 [3072], replicated
- grad_w_fc2: float32 [768, 3072], P('clip', ('tm', 'height'))
- grad_b_fc2: float32 [768], replicated
The draws below stay inside these ranges and needn't reach their ends.
Inputs may be any that keep to these rules, and one draw needn't show every extreme that they name: `mem_len`: how many of a clip's 2 memory steps hold valid keys and values; some clip has all 2.
All inputs are finite; a program needn't handle non-finite values. No bound on the sum of `res_id` on one device may be relied on, other than what follows from the above.
Results may differ from the reference program's by a relative error of at most 0.019.
Values may be sent and summed in bfloat16 or wider, within the bound.
No kernel may reach another device: no remote copies, remote signals or barrier semaphores. Data moves between devices by JAX's collectives and lax.ppermute only.
A program may use at most 320 MiB of HBM per device.

```python
import jax
import jax.numpy as jnp
from jax import lax

D = 768
C = 384
HEADS = 8
MLP = 3072
HEAD = 96
FR = 8
GRID = 24
SIDE_SMALL = 14
SIDE_BIG = 20
MEM = 2
CLIPS = 4


def draw_mem_len(key, part):
    first, second = jax.random.split(key, 2)
    offset = jax.random.randint(second, (), 0, MEM + 1)
    lengths = (jax.random.randint(first, (CLIPS,), 0, MEM + 1) + offset) % (MEM + 1)
    chosen = jax.random.randint(jax.random.fold_in(second, 1), (), 0, CLIPS)
    return jnp.where(jnp.arange(CLIPS) == chosen, MEM, lengths).astype(jnp.int32)


def with_ends(entries, rng, least, high):
    longest = entries.shape.index(max(entries.shape))
    spots = []
    for shift in (0, 1):
        where = [jax.random.randint(jax.random.fold_in(rng, axis), (), 0, length) for axis, length in enumerate(entries.shape)]
        where[longest] = (where[longest] + shift) % entries.shape[longest]
        spots.append(tuple(where))
    return entries.at[spots[0]].set(least).at[spots[1]].set(high)


def spiked(drawn, key, source, target, blocks, factor):
    def block_of(axis_at):
        return (jnp.arange(drawn.shape[axis_at]) // (drawn.shape[axis_at] // blocks)).reshape((-1,) + (1,) * (drawn.ndim - 1 - axis_at))

    one_side = jax.random.permutation(key, blocks)[block_of(target)]
    other_side = (block_of(target) + blocks // 2) % blocks
    return jnp.where((block_of(source) == one_side) | (block_of(source) == other_side), factor * drawn, drawn)


def level_of(key, shape, shards, low, top_value):
    factor_of = 1.0
    for position, parts in shards:
        steps = jax.random.uniform(jax.random.fold_in(jax.random.fold_in(key, 6), position), (parts,), jnp.float32, low / len(shards), top_value / len(shards))
        factor_of = factor_of * jnp.repeat(jnp.exp(steps), shape[position] // parts).reshape((-1,) + (1,) * (len(shape) - 1 - position))
    return factor_of


def normal_values(stream_key, extent, scale, bound, cuts=(), dtype=jnp.bfloat16):
    values = jax.random.normal(stream_key, extent, jnp.float32) * scale
    if len(cuts) > 0:
        values = level_of(stream_key, extent, cuts, -0.22, 0.18) * values
    return jnp.clip(values, min=-bound, max=bound).astype(dtype)


def gaussian_with(key, dims, scale, most, shards, heavy, held_as=jnp.bfloat16):
    entries = scale * jax.random.normal(key, dims, jnp.float32)
    if shards:
        entries = entries * level_of(key, dims, shards, -0.22, 0.18)
    return jnp.clip(spiked(entries, jax.random.fold_in(key, 3), *heavy), -most, most).astype(held_as)


def setup_inputs(seed: int = 0) -> dict:
    splits = jax.random.split(jax.random.key(seed), 25)
    return {
        "clip_input": normal_values(splits[0], (CLIPS, FR, GRID, GRID, C), 1.0, 6.0, ((0, 4), (1, 2), (2, 4))),
        "memory": normal_values(splits[1], (CLIPS, MEM, 2, FR, GRID, GRID, D), 1.6, 8.0, ((0, 4), (3, 2), (4, 4))),
        "mem_len": draw_mem_len(jax.random.fold_in(splits[24], 71), 0),
        "res_id": with_ends((jax.random.randint(splits[3], (CLIPS,), 0, 8) < 1).astype(jnp.int32), jax.random.fold_in(splits[3], 1), 0, 1),
        "norm1_gain": jnp.clip(1.0 + 0.1 * jax.random.normal(splits[4], (C,), jnp.float32), 0.5, 1.5),
        "norm1_bias": normal_values(splits[5], (C,), 0.3, 1.75, (), jnp.float32),
        "w_qkv": normal_values(splits[6], (3 * D, C), (2 * C // 5) ** -0.5, 0.5),
        "b_qkv": normal_values(splits[7], (3 * D,), 0.3, 1.75, (), jnp.float32),
        "conv_kv": normal_values(splits[8], (2, 3, 3, 3, D), 27 ** -0.5, 1.25, (), jnp.float32),
        "compress": normal_values(splits[9], (2, 2, 2, D), 4 ** -0.5, 3.0, (), jnp.float32),
        "rel_t": normal_values(splits[10], (2 * FR - 1, HEAD), 0.12, 0.75, (), jnp.float32),
        "rel_h": normal_values(splits[11], (2 * GRID - 1, HEAD), 0.12, 0.75, (), jnp.float32),
        "rel_w": normal_values(splits[12], (2 * GRID - 1, HEAD), 0.12, 0.75, (), jnp.float32),
        "w_proj": normal_values(splits[13], (D, D), D ** -0.5, 0.21875),
        "b_proj": normal_values(splits[14], (D,), 0.3, 1.75, (), jnp.float32),
        "w_short": normal_values(splits[15], (D, C), C ** -0.5, 0.3125),
        "b_short": normal_values(splits[16], (D,), 0.3, 1.75, (), jnp.float32),
        "norm2_gain": jnp.clip(1.0 + 0.1 * jax.random.normal(splits[17], (D,), jnp.float32), 0.5, 1.5),
        "norm2_bias": normal_values(splits[18], (D,), 0.3, 1.75, (), jnp.float32),
        "w_fc1": normal_values(splits[19], (MLP, D), D ** -0.5, 0.21875),
        "b_fc1": normal_values(splits[20], (MLP,), 0.3, 1.75, (), jnp.float32),
        "w_fc2": normal_values(splits[21], (D, MLP), MLP ** -0.5, 0.109375),
        "b_fc2": normal_values(splits[22], (D,), 0.3, 1.75, (), jnp.float32),
        "cotangent": gaussian_with(splits[23], (CLIPS, FR, GRID // 2, GRID // 2, D), 1.0, 6.0, ((0, 4), (1, 2), (2, 4)), (0, 4, 4, 2.0)),
    }


HIGHEST_PREC = lax.Precision.HIGHEST
MASKED = -1e+30
EPSILON = 1e-06

@jax.custom_vjp
def low(v):
    return lax.optimization_barrier(v.astype(jnp.bfloat16)).astype(jnp.float32)

@jax.custom_vjp
def low_back(v):
    return v

def low_keep(v):
    return (low(v), None)

def low_pass(kept, grad):
    return (grad,)

def back_keep(v):
    return (v, None)

def back_low(kept, grad):
    return (low(grad),)
low.defvjp(low_keep, low_pass)
low_back.defvjp(back_keep, back_low)

def layer_norm(values, gain, shift):
    means = lax.optimization_barrier(jnp.mean(values, axis=-1, keepdims=True))
    centred = values - means
    spread = lax.optimization_barrier(jnp.mean(centred * centred, axis=-1, keepdims=True))
    return centred * lax.rsqrt(spread + EPSILON) * gain + shift

def selector(count_q, count_k, stride):
    target = stride * jnp.arange(count_q)[:, None] - jnp.arange(count_k)[None, :] + count_k - 1
    return (target[:, :, None] == jnp.arange(2 * count_k - 1)[None, None, :]).astype(jnp.float32)

def head_attend(query_head, key_head, value_head, tables, key_valid, select_time, select_space):
    rel_t, rel_h, rel_w = tables
    half = GRID // 2
    query_count = FR * half * half
    along_t = jnp.einsum('tabj,tkj->tabk', jnp.einsum('tabe,je->tabj', query_head, rel_t, precision=HIGHEST_PREC), select_time, precision=HIGHEST_PREC)
    along_h = jnp.einsum('tabj,akj->tabk', jnp.einsum('tabe,je->tabj', query_head, rel_h, precision=HIGHEST_PREC), select_space, precision=HIGHEST_PREC)
    along_w = jnp.einsum('tabj,bkj->tabk', jnp.einsum('tabe,je->tabj', query_head, rel_w, precision=HIGHEST_PREC), select_space, precision=HIGHEST_PREC)
    bias = (along_t[:, :, :, :, None, None] + along_h[:, :, :, None, :, None] + along_w[:, :, :, None, None, :]).reshape(query_count, FR * GRID * GRID)
    flat = query_head.reshape(query_count, HEAD)
    raw = jnp.dot(flat, key_head.T, precision=HIGHEST_PREC) * HEAD ** (-0.5)
    raw = raw + jnp.pad(bias, ((0, 0), (0, key_head.shape[0] - bias.shape[1])))
    scores = jnp.where(key_valid[None, :], low_back(raw), MASKED)
    top = lax.optimization_barrier(jnp.max(scores, axis=-1, keepdims=True))
    raised = jnp.exp(scores - top)
    shares = raised / lax.optimization_barrier(jnp.sum(raised, axis=-1, keepdims=True))
    return jnp.dot(low(shares), value_head, precision=HIGHEST_PREC)

def clip_forward(params, clip, past, side, length):
    norm1_gain, norm1_bias, w_qkv, b_qkv, conv_kv, compress, rel_t, rel_h, rel_w, w_proj, b_proj, w_short, b_short, norm2_gain, norm2_bias, w_fc1, b_fc1, w_fc2, b_fc2 = params
    half = GRID // 2
    positions = jnp.arange(GRID)
    inside = ((positions[:, None] < side) & (positions[None, :] < side)).astype(jnp.float32)
    normed = low(layer_norm(clip, norm1_gain, norm1_bias))
    projected = low_back(jnp.einsum('thwc,oc->thwo', normed, w_qkv, precision=HIGHEST_PREC) + b_qkv)
    pooled = low(projected[..., :D].reshape(FR, half, 2, half, 2, D).mean(axis=(2, 4)))
    masked = low(jnp.stack([projected[..., D:2 * D], projected[..., 2 * D:]]) * inside[None, None, :, :, None])
    framed = jnp.pad(masked, ((0, 0), (1, 1), (1, 1), (1, 1), (0, 0)))
    mixed = jnp.zeros_like(masked)
    for tap_t in range(3):
        for tap_h in range(3):
            for tap_w in range(3):
                mixed = mixed + framed[:, tap_t:tap_t + FR, tap_h:tap_h + GRID, tap_w:tap_w + GRID, :] * conv_kv[:, tap_t, tap_h, tap_w][:, None, None, None, :]
    mixed = low(mixed)
    squeezed = low(jnp.einsum('smtaicjd,mijd->smtacd', past.reshape(MEM, 2, FR, half, 2, half, 2, D), compress, precision=HIGHEST_PREC))
    keys = jnp.concatenate([mixed[0].reshape(-1, D), squeezed[:, 0].reshape(-1, D)], 0)
    values = jnp.concatenate([mixed[1].reshape(-1, D), squeezed[:, 1].reshape(-1, D)], 0)
    memory_ok = (jnp.arange(MEM)[:, None, None, None] < length) & (inside[::2, ::2][None, None, :, :] > 0)
    memory_ok = jnp.broadcast_to(memory_ok, (MEM, FR, half, half)).reshape(-1)
    current_ok = jnp.broadcast_to(inside[None] > 0, (FR, GRID, GRID)).reshape(-1)
    key_valid = jnp.concatenate([current_ok, memory_ok])
    heads_q = pooled.reshape(FR, half, half, HEADS, HEAD).transpose(3, 0, 1, 2, 4)
    heads_k = keys.reshape(-1, HEADS, HEAD).transpose(1, 0, 2)
    heads_v = values.reshape(-1, HEADS, HEAD).transpose(1, 0, 2)
    select_time = selector(FR, FR, 1)
    select_space = selector(half, GRID, 2)
    tables = (rel_t, rel_h, rel_w)
    attend = jax.checkpoint(lambda item: head_attend(item[0], item[1], item[2], tables, key_valid, select_time, select_space))
    attention = lax.map(attend, (heads_q, heads_k, heads_v))
    attention = attention.transpose(1, 0, 2).reshape(-1, D)
    joined = low(low_back(attention + pooled.reshape(-1, D)))
    branch = low_back(jnp.dot(joined, w_proj.T, precision=HIGHEST_PREC) + b_proj)
    maxima = clip.reshape(FR, half, 2, half, 2, C).max(axis=(2, 4)).reshape(-1, C)
    shortcut = low_back(jnp.dot(maxima, w_short.T, precision=HIGHEST_PREC) + b_short)
    resid = branch + shortcut
    normed2 = low(layer_norm(resid, norm2_gain, norm2_bias))
    hidden = low_back(jnp.dot(normed2, w_fc1.T, precision=HIGHEST_PREC) + b_fc1)
    activated = low(jax.nn.gelu(hidden, approximate=False))
    mlp_out = low_back(jnp.dot(activated, w_fc2.T, precision=HIGHEST_PREC) + b_fc2)
    return (resid + mlp_out).reshape(FR, half, half, D)

def reference(clip_input, memory, mem_len, res_id, norm1_gain, norm1_bias, w_qkv, b_qkv, conv_kv, compress, rel_t, rel_h, rel_w, w_proj, b_proj, w_short, b_short, norm2_gain, norm2_bias, w_fc1, b_fc1, w_fc2, b_fc2, cotangent):
    params = tuple((value.astype(jnp.float32) for value in (norm1_gain, norm1_bias, w_qkv, b_qkv, conv_kv, compress, rel_t, rel_h, rel_w, w_proj, b_proj, w_short, b_short, norm2_gain, norm2_bias, w_fc1, b_fc1, w_fc2, b_fc2)))

    def per_clip(totals, item):
        clip, past, length, resolution, grad = item
        side = SIDE_SMALL + (SIDE_BIG - SIDE_SMALL) * resolution

        def forward(weights, values):
            return clip_forward(weights, values, past.astype(jnp.float32), side, length)
        result, pull = jax.vjp(forward, params, clip.astype(jnp.float32))
        weight_grads, clip_grad = pull(grad.astype(jnp.float32))
        totals = jax.tree.map(lambda left, right: left + right, totals, weight_grads)
        return (totals, (result.astype(jnp.bfloat16), clip_grad.astype(jnp.bfloat16)))
    zeros = tuple((jnp.zeros_like(value) for value in params))
    totals, (output, input_grad) = lax.scan(per_clip, zeros, (clip_input, memory, mem_len, res_id, cotangent))
    return (output, input_grad, totals[0], totals[1], totals[2], totals[3], totals[4], totals[5], totals[6], totals[7], totals[8], totals[9], totals[10], totals[11], totals[12], totals[13], totals[14], totals[15], totals[16], totals[17], totals[18])
```

```python
import functools

import jax
import jax.numpy as jnp
import numpy as np
from jax import lax
from jax.experimental import pallas as pl
from jax.experimental.pallas import tpu as pltpu
from jax.sharding import PartitionSpec as P

HEADS = 8
SIDE_SMALL = 14
SIDE_BIG = 20
MEM = 2
EPSILON = 1e-06
SQRT_HALF = 0.7071067811865476
ROOT_TWO_PI = 2.5066282746310002
LOG2E = 1.4426950408889634
FAR = -1e30

GRID = 24
FR = 8
HALF = GRID // 2
VW = SIDE_BIG
VH = VW // 2
LANE = 128
PLANE = (VW + 1) * GRID
FLAT = GRID + (FR + 2) * PLANE
CUR = FR * VW * VW
KEYS_USED = CUR + MEM * FR * VH * VH
KEYS = -(-KEYS_USED // 256) * 256
TAB = 8 * FR + 2 * GRID * HALF

bf = jnp.bfloat16
f32 = jnp.float32
HI = lax.Precision.HIGHEST
G = ("tm", "height")


def nn(a, b, **kw):
    return lax.dot_general(a, b, (((1,), (0,)), ((), ())), preferred_element_type=f32, **kw)


def nt(a, b, **kw):
    return lax.dot_general(a, b, (((1,), (1,)), ((), ())), preferred_element_type=f32, **kw)


def tn(a, b, **kw):
    return lax.dot_general(a, b, (((0,), (0,)), ((), ())), preferred_element_type=f32, **kw)


def shape(dims, dtype):
    return jax.ShapeDtypeStruct(dims, dtype)


def call(kernel, outs, args, scratch=(), smem=1, cost=None, **kw):
    specs = [pl.BlockSpec(memory_space=pltpu.SMEM)] * smem
    specs += [pl.BlockSpec(memory_space=pltpu.VMEM)] * (len(args) - smem)
    return pl.pallas_call(
        kernel,
        out_shape=outs,
        in_specs=specs,
        out_specs=jax.tree.map(lambda _: pl.BlockSpec(memory_space=pltpu.VMEM), outs),
        scratch_shapes=list(scratch),
        compiler_params=pltpu.CompilerParams(vmem_limit_bytes=56 << 20),
        cost_estimate=cost,
        **kw,
    )(*args)


def pad_lanes(x, lanes):
    return jnp.concatenate([x, jnp.zeros((x.shape[0], lanes - x.shape[1]), x.dtype)], axis=1)


def layer_unit(x):
    centred = x - jnp.mean(x, axis=-1, keepdims=True)
    inverse = lax.rsqrt(jnp.mean(centred * centred, axis=-1, keepdims=True) + EPSILON)
    return centred * inverse, inverse


def pair_reduce(value, scratch, op):
    rows, lanes = value.shape
    outs = []
    for j in range(lanes // LANE):
        scratch[j, 0:rows, :] = value[:, j * LANE : (j + 1) * LANE]
    for j in range(lanes // LANE):
        outs.append(op(scratch[j, pl.ds(0, rows // 2, 2), :], scratch[j, pl.ds(1, rows // 2, 2), :]))
    return jnp.concatenate(outs, axis=1)


def pair_spread(value, scratch):
    rows, lanes = value.shape
    for j in range(lanes // LANE):
        part = value[:, j * LANE : (j + 1) * LANE]
        scratch[j, pl.ds(0, rows, 2), :] = part
        scratch[j, pl.ds(1, rows, 2), :] = part
    return jnp.concatenate([scratch[j, 0 : 2 * rows, :] for j in range(lanes // LANE)], axis=1)


def qkv_kernel(dims, meta, x_ref, g_ref, b_ref, w_ref, bq_ref, bkv_ref, kv_ref, n1_ref, mx_ref, q_ref, x20, tiles):
    frames, rows, width, hd = dims
    half = rows // 2
    side, height = meta[0], meta[3]
    per = rows * GRID
    valid_rows = frames * rows * VW
    quarter = frames * half * HALF
    g = g_ref[...]
    b = b_ref[...]
    for t in range(frames):
        x = x_ref[t * per : (t + 1) * per, :].astype(f32)
        unit, _ = layer_unit(x)
        low = (unit * g + b).astype(bf)
        full = low.astype(f32)
        for h in range(rows):
            x20[(t * rows + h) * VW : (t * rows + h + 1) * VW, :] = full[h * GRID : h * GRID + VW]
        tall = jnp.concatenate(
            [
                jnp.maximum(x[2 * a * GRID : (2 * a + 1) * GRID], x[(2 * a + 1) * GRID : (2 * a + 2) * GRID])
                for a in range(half)
            ],
            axis=0,
        )
        mx_ref[t * half * HALF : (t + 1) * half * HALF, :] = pair_reduce(tall, tiles, jnp.maximum)
        sums = jnp.concatenate(
            [full[2 * a * GRID : (2 * a + 1) * GRID] + full[(2 * a + 1) * GRID : (2 * a + 2) * GRID] for a in range(half)],
            axis=0,
        )
        n1_ref[valid_rows + t * half * HALF : valid_rows + (t + 1) * half * HALF, :] = pair_reduce(sums, tiles, jnp.add).astype(f32)
        query = nt(low, w_ref[0:width, :])
        tall = jnp.concatenate(
            [query[2 * a * GRID : (2 * a + 1) * GRID] + query[(2 * a + 1) * GRID : (2 * a + 2) * GRID] for a in range(half)],
            axis=0,
        )
        pooled = pair_reduce(tall, tiles, jnp.add) * 0.25 + bq_ref[...]
        for n in range(HEADS):
            q_ref[n, t * half * HALF : (t + 1) * half * HALF, :] = pad_lanes(pooled[:, n * hd : (n + 1) * hd], LANE)
    n1_ref[0:valid_rows, :] = x20[...]
    low20 = x20[...].astype(bf)
    cells = valid_rows // 2
    index = lax.broadcasted_iota(jnp.int32, (cells, 1), 0)
    line = (index * 3277) >> 16
    row = height * rows + lax.rem(line, rows)
    inside = ((row < side) & (index - line * VW < side)).astype(f32)
    for n in range(HEADS):
        weight = jnp.concatenate(
            [w_ref[width + n * hd : width + (n + 1) * hd, :], w_ref[2 * width + n * hd : 2 * width + (n + 1) * hd, :]], axis=0
        )
        y = nt(low20, weight)
        packed = jnp.concatenate([y[0:cells], y[cells : 2 * cells]], axis=1)
        kv_ref[n] = ((packed + bkv_ref[n : n + 1, :]) * inside).astype(bf)


def squeeze_kernel(dims, mem_ref, c_ref, q_ref, out_ref, tiles, squeezed):
    frames, rows, width, hd = dims
    half = rows // 2
    count = half * frames * VH
    odd = lax.broadcasted_iota(jnp.int32, (GRID, 1), 0) % 2 == 1
    for m in range(2):
        taps = [jnp.where(odd, c_ref[m, i, 1:2, :], c_ref[m, i, 0:1, :]) for i in range(2)]
        for s in range(MEM):
            for t in range(frames):
                parts = [
                    mem_ref[s, m, t, 2 * a].astype(f32) * taps[0] + mem_ref[s, m, t, 2 * a + 1].astype(f32) * taps[1]
                    for a in range(half)
                ]
                for a in range(half):
                    done = pair_reduce(parts[a], tiles.at[(t * half + a) % 4], jnp.add)
                    squeezed[m, s, a * frames * VH + t * VH : a * frames * VH + (t + 1) * VH, :] = done[0:VH]
            squeezed[m, s, count:LANE, :] = jnp.zeros((LANE - count, width), f32)
    quarter = frames * half * HALF
    for n in range(HEADS):
        cut = slice(n * hd, (n + 1) * hd)
        out_ref[n, 0:LANE, :] = jnp.concatenate(
            [squeezed[0, 0, :, cut], squeezed[1, 0, :, cut], squeezed[0, 1, :, cut], squeezed[1, 1, :, cut]], axis=1
        ).astype(bf)
        third = quarter // 3
        out_ref[n, LANE : LANE + third, :] = jnp.concatenate(
            [q_ref[n, i * third : (i + 1) * third, :] for i in range(3)], axis=1
        ).astype(bf)


def flat_row(t, h):
    return GRID + (1 + t) * PLANE + h * GRID


def fill_grid(grid):
    zero = jnp.zeros((GRID, LANE), f32)
    grid[0 : GRID + PLANE, :] = jnp.zeros((GRID + PLANE, LANE), f32)
    grid[flat_row(FR, 0) :, :] = jnp.zeros((FLAT - flat_row(FR, 0), LANE), f32)
    for t in range(FR):
        grid[flat_row(t, VW) : flat_row(t, VW) + GRID, :] = zero


def taps9(w_ref, part):
    return [[[w_ref[(a * 3 + b) * 3 + c : (a * 3 + b) * 3 + c + 1, part * LANE : (part + 1) * LANE] for c in range(3)] for b in range(3)] for a in range(3)]


def four_rows(grid, weights, base, flip):
    acc = [[None] * 3 for _ in range(4)]
    for line in range(-1, 5):
        for a in range(3):
            shift = (1 - a if flip else a - 1) * PLANE + line * GRID
            cells = grid[pl.ds(pl.multiple_of(base + shift, 8), GRID), :]
            for h in range(4):
                b = (h - line + 1) if flip else (line - h + 1)
                if b < 0 or b > 2:
                    continue
                for c in range(3):
                    term = cells * weights[a][b][c]
                    acc[h][c] = term if acc[h][c] is None else acc[h][c] + term
    outs = []
    for h in range(4):
        left, mid, right = (acc[h][2], acc[h][1], acc[h][0]) if flip else (acc[h][0], acc[h][1], acc[h][2])
        outs.append((pltpu.roll(left, 1, 0) + mid + pltpu.roll(right, GRID - 1, 0))[0:VW])
    return jnp.concatenate(outs, axis=0)


def conv_kernel(dims, meta, y_ref, w_ref, k_ref, v_ref, gk, gv):
    frames, rows, n_height, hd = dims
    side = meta[0]
    for grid in (gk, gv):
        fill_grid(grid)
    for src in range(HEADS):
        part = y_ref[src].astype(f32)
        for g in range(2):
            for m, grid in ((0, gk), (1, gv)):
                lane = (2 * g + m) * hd
                cut = pad_lanes(part[:, lane : lane + hd], LANE)
                for t2 in range(frames // 2):
                    for h in range(rows):
                        row = src % n_height * rows + h
                        if row >= VW:
                            continue
                        t = src // n_height * frames + g * (frames // 2) + t2
                        at = (t2 * rows + h) * VW
                        grid[flat_row(t, row) : flat_row(t, row) + GRID, :] = jnp.concatenate(
                            [cut[at : at + VW], jnp.zeros((GRID - VW, LANE), f32)], axis=0
                        )
    local = lax.broadcasted_iota(jnp.int32, (4 * VW, LANE), 0)
    lane = lax.broadcasted_iota(jnp.int32, (4 * VW, LANE), 1)
    line = (local * 3277) >> 16
    column = local - line * VW
    fixed = [(lane + o == 143 - column) | (lane + o == 191 - column) for o in (0, LANE)]
    ones = (lane == hd).astype(f32)

    def step(it, carry):
        t = it // (VW // 4)
        quad = it % (VW // 4)
        base = GRID + (1 + t) * PLANE + quad * 4 * GRID
        out = pl.ds(pl.multiple_of(it * (4 * VW), 16), 4 * VW)
        mixed_k = four_rows(gk, taps9(w_ref, 0), base, False)
        mixed_v = four_rows(gv, taps9(w_ref, 1), base, False)
        h = quad * 4 + line
        bad = (h >= side) | (column >= side)
        for o in range(2):
            at = lane + o * LANE
            hit = fixed[o] | (at == 103 - t) | (at == 151 - t) | (at == 123 - h) | (at == 171 - h) | ((at == 192) & bad)
            marks = hit.astype(f32)
            k_ref[out, o * LANE : (o + 1) * LANE] = ((mixed_k + marks) if o == 0 else marks).astype(bf)
        v_ref[out, :] = (mixed_v + ones).astype(bf)
        return carry

    lax.fori_loop(0, FR * VW // 4, step, 0)


def build_table(tab, t_ref, h_ref, w_ref):
    tab[...] = jnp.zeros(tab.shape, f32)
    for v in range(FR):
        tab[8 * v : 8 * v + FR, :] = t_ref[v : v + FR, :]
    for n, ref in ((0, h_ref), (1, w_ref)):
        for a in range(HALF):
            at = 8 * FR + (n * HALF + a) * GRID
            first = 2 * a + GRID - VW
            tab[at : at + VW, :] = ref[first : first + VW, :]


def attend_kernel(dims, meta, kc_ref, vc_ref, y_ref, t_ref, h_ref, w_ref, place_ref, k_ref, kt_ref, v_ref, qt_ref, q_ref, o_ref, l_ref, j_ref, vt, qrow, tab, s_ref):
    frames, rows, n_height, hd = dims
    half = rows // 2
    side, length = meta[0], meta[1]
    queries = qrow.shape[0]
    scale = hd**-0.5
    k_ref[0:CUR, :] = kc_ref[...]
    v_ref[0:CUR, :] = vc_ref[...]
    count = half * frames * VH
    each = frames * VH
    per_q = queries // HEADS
    third = per_q // 3
    lane1 = lax.broadcasted_iota(jnp.int32, (1, LANE), 1)
    at = CUR
    for src in range(HEADS):
        packed = y_ref[src].astype(f32)
        first = src % n_height * half
        used = min(max(VH - first, 0), half) * each
        if used > 0:
            halves = []
            for m in range(2):
                halves.append(jnp.concatenate([packed[0:used, m * hd : (m + 1) * hd], packed[0:used, (2 + m) * hd : (3 + m) * hd]], axis=0))
            index = lax.broadcasted_iota(jnp.int32, (2 * used, LANE), 0)
            step = (index >= used).astype(jnp.int32)
            inner = index - step * used
            a = (inner >= each).astype(jnp.int32) + (inner >= 2 * each).astype(jnp.int32)
            inner = inner - a * each
            c = inner - ((inner * 6554) >> 16) * VH
            bad = (step >= length) | (2 * (first + a) >= side) | (2 * c >= side)
            mark = (bad & (lax.broadcasted_iota(jnp.int32, (2 * used, LANE), 1) == 64)).astype(f32)
            k_ref[at : at + 2 * used, 0:LANE] = pad_lanes(halves[0], LANE).astype(bf)
            k_ref[at : at + 2 * used, LANE:] = mark.astype(bf)
            v_ref[at : at + 2 * used, :] = (pad_lanes(halves[1], LANE) + (lane1 == hd).astype(f32)).astype(bf)
            at += 2 * used
        for i in range(3):
            qrow[src * per_q + i * third : src * per_q + (i + 1) * third, :] = packed[LANE : LANE + third, i * LANE : (i + 1) * LANE]
    rest = KEYS - at
    k_ref[at:, 0:LANE] = jnp.zeros((rest, LANE), bf)
    k_ref[at:, LANE:] = jnp.broadcast_to((lane1 == 64).astype(f32), (rest, LANE)).astype(bf)
    v_ref[at:, :] = jnp.zeros((rest, LANE), bf)
    for i in range(KEYS // 256):
        cut = slice(i * 256, (i + 1) * 256)
        kt_ref[:, cut] = k_ref[cut, :].T
        vt[:, cut] = v_ref[cut, :].T
    q_ref[...] = qrow[...].astype(bf)
    pt = qrow[...].T[0:hd]
    build_table(tab, t_ref, h_ref, w_ref)
    along = nn(tab[...], pt, precision=HI)
    tq, aq, cq = place_ref[0:1, :], place_ref[1:2, :], place_ref[2:3, :]
    part_t = jnp.zeros((FR, queries), f32)
    for v in range(FR):
        part_t = jnp.where(tq == v, along[8 * v : 8 * v + FR], part_t)
    parts = []
    for n, place in ((0, aq), (1, cq)):
        part = jnp.zeros((GRID, queries), f32)
        for a in range(HALF):
            row = 8 * FR + (n * HALF + a) * GRID
            part = jnp.where(place == a, along[row : row + GRID], part)
        parts.append(part[0:VW])
    bias = jnp.concatenate([part_t] + parts, axis=0) * hd**0.5
    high = bias.astype(bf)
    low = (bias - high.astype(f32)).astype(bf)
    qt_ref[0:hd, :] = pt.astype(bf)
    qt_ref[hd : hd + 48, :] = high
    qt_ref[hd + 48 : hd + 96, :] = low
    tail = lax.broadcasted_iota(jnp.int32, (64, queries), 0)
    qt_ref[192:256, :] = jnp.where(tail == 0, FAR, 0.0).astype(bf)
    factor = scale * LOG2E
    wide = s_ref.shape[1]
    blocks = [(i, min(i + 512, KEYS)) for i in range(0, KEYS, 512)]

    def one(block, carry):
        cols = pl.ds(pl.multiple_of(block * wide, LANE), wide)
        query = qt_ref[:, cols]
        top = jnp.full((8, wide), FAR, f32)
        for lo, hi in blocks:
            scores = nn(k_ref[lo:hi, :], query)
            s_ref[lo:hi, :] = scores
            top = jnp.maximum(top, jnp.max(scores.reshape((hi - lo) // 8, 8, wide), axis=0))
        top = jnp.max(top, axis=0, keepdims=True) * factor
        total = jnp.zeros((LANE, wide), f32)
        for lo, hi in blocks:
            weights = jnp.exp2(s_ref[lo:hi, :] * factor - top).astype(bf)
            total = total + nn(vt[:, lo:hi], weights)
        norm = total[hd : hd + 1]
        o_ref[:, cols] = total[0:hd] / norm
        l_ref[:, cols] = top + jnp.log2(norm)
        return carry

    lax.fori_loop(0, queries // wide, one, 0)
    j_ref[...] = pad_lanes((o_ref[...] + pt).T, LANE).astype(bf)


def mlp_kernel(dims, j_ref, mx_ref, cot_ref, wp_ref, ws_ref, bps_ref, g_ref, b_ref, w1_ref, b1_ref, w2_ref, b2_ref,
               out_ref, keep_ref, act_ref, hg_ref, dj_ref, mg_ref, gb1_ref, small_ref,
               resid, n2, acc, ngrad, joined):
    width, hd = dims
    i = pl.program_id(0)

    @pl.when(i == 0)
    def _():
        joined[...] = jnp.concatenate([j_ref[n][:, 0:hd] for n in range(HEADS)], axis=1)
        value = nt(joined[...], wp_ref[...]) + nt(mx_ref[...].astype(bf), ws_ref[...]) + bps_ref[...]
        resid[...] = value
        unit, _ = layer_unit(value)
        n2[...] = (unit * g_ref[...] + b_ref[...]).astype(bf)
        acc[...] = jnp.zeros(acc.shape, f32)
        ngrad[...] = jnp.zeros(ngrad.shape, f32)

    hidden = nt(n2[...], w1_ref[...]) + b1_ref[...]
    gate = 0.5 * (1.0 + lax.erf(hidden * SQRT_HALF))
    act = (hidden * gate).astype(bf)
    act_ref[0] = act
    acc[...] += nt(act, w2_ref[...])
    grad = nn(cot_ref[...], w2_ref[...])
    hgrad = (grad * (gate + hidden * jnp.exp(-0.5 * hidden * hidden) / ROOT_TWO_PI)).astype(bf)
    hg_ref[0] = hgrad
    gb1_ref[...] = jnp.sum(hgrad.astype(f32), axis=0, keepdims=True)
    ngrad[...] += nn(hgrad, w1_ref[...])

    @pl.when(i == pl.num_programs(0) - 1)
    def _():
        value = resid[...]
        out_ref[...] = (value + acc[...] + b2_ref[...]).astype(bf)
        unit, inverse = layer_unit(value)
        cot = cot_ref[...].astype(f32)
        grad = ngrad[...]
        scaled = grad * g_ref[...]
        back = inverse * (
            scaled - jnp.mean(scaled, axis=-1, keepdims=True) - unit * jnp.mean(scaled * unit, axis=-1, keepdims=True)
        )
        low = (cot + back).astype(bf)
        keep_ref[:, 0:width] = n2[...]
        keep_ref[:, width : 2 * width] = low
        keep_ref[:, 2 * width :] = mx_ref[...].astype(bf)
        joined_grad = nn(low, wp_ref[...])
        for n in range(HEADS):
            dj_ref[n] = pad_lanes(joined_grad[:, n * hd : (n + 1) * hd], LANE).astype(bf)
        mg_ref[...] = nn(low, ws_ref[...])
        small_ref[0:1, :] = jnp.sum(low.astype(f32), axis=0, keepdims=True)
        small_ref[1:2, :] = jnp.sum(grad * unit, axis=0, keepdims=True)
        small_ref[2:3, :] = jnp.sum(grad, axis=0, keepdims=True)
        small_ref[3:4, :] = jnp.sum(cot, axis=0, keepdims=True)
        small_ref[4:8, :] = jnp.zeros((4, width), f32)


def attend_back_kernel(dims, k_ref, kt_ref, v_ref, qt_ref, q_ref, o_ref, l_ref, dj_ref, t_ref, h_ref, w_ref, place_ref,
                       dk_ref, dv_ref, mem_ref, pq_ref, gt_ref, gh_ref, gw_ref,
                       dot_ref, dq, tab, dtab, dks, dvs, delta):
    frames, rows, n_height, hd = dims
    half = rows // 2
    queries = q_ref.shape[0]
    scale = hd**-0.5
    factor = scale * LOG2E
    turned = dj_ref[...].astype(f32).T
    dot_ref[...] = turned.astype(bf)
    delta[...] = jnp.sum(turned[0:hd] * o_ref[...], axis=0, keepdims=True)
    dq[...] = jnp.zeros(dq.shape, f32)
    wide = 384

    def chunk(i, carry):
        cut = pl.ds(pl.multiple_of(i * 256, 256), 256)
        dk = jnp.zeros((256, LANE), f32)
        dv = jnp.zeros((256, LANE), f32)
        for lo in range(0, queries, wide):
            cols = slice(lo, lo + wide)
            shares = jnp.exp2(nn(k_ref[cut, :], qt_ref[:, cols]) * factor - l_ref[:, cols])
            slope = nn(v_ref[cut, :], dot_ref[:, cols])
            score = (shares * (slope - delta[:, cols])).astype(bf)
            dv = dv + nn(shares.astype(bf), dj_ref[cols, :])
            dk = dk + nn(score, q_ref[cols, :])
            dq[:, cols] += nn(kt_ref[0 : dq.shape[0], cut], score)
        dks[cut, :] = dk * scale
        dvs[cut, :] = dv
        return carry

    lax.fori_loop(0, KEYS // 256, chunk, 0)
    dk_ref[...] = dks[0:CUR, :]
    dv_ref[...] = dvs[0:CUR, :]
    each = frames * VH
    at = CUR
    for dst in range(HEADS):
        first = dst % n_height * half
        used = min(max(VH - first, 0), half) * each
        if used > 0:
            parts = [ref[at + s * used : at + (s + 1) * used, 0:hd] for s in range(MEM) for ref in (dks, dvs)]
            packed = jnp.concatenate(parts, axis=1)
            at += 2 * used
        if used < LANE:
            zero = jnp.zeros((LANE - used, 4 * hd), f32)
            packed = jnp.concatenate([packed, zero], axis=0) if used > 0 else zero
        mem_ref[dst] = packed.astype(bf)
    build_table(tab, t_ref, h_ref, w_ref)
    tq, aq, cq = place_ref[0:1, :], place_ref[1:2, :], place_ref[2:3, :]
    grad_t = dq[hd : hd + FR, :]
    for v in range(FR):
        dtab[8 * v : 8 * v + FR, :] = jnp.where(tq == v, grad_t, 0.0)
    for n, place in ((0, aq), (1, cq)):
        part = jnp.concatenate(
            [dq[hd + FR + n * VW : hd + FR + (n + 1) * VW, :], jnp.zeros((GRID - VW, queries), f32)], axis=0
        )
        for a in range(HALF):
            row = 8 * FR + (n * HALF + a) * GRID
            dtab[row : row + GRID, :] = jnp.where(place == a, part, 0.0)
    pooled_grad = dq[0:hd, :] * scale + tn(tab[...], dtab[...], precision=HI) + dot_ref[0:hd, :].astype(f32)
    pq_ref[...] = pad_lanes(pooled_grad.T * 0.25, LANE)
    grads = nn(dtab[...], q_ref[...].astype(f32), precision=HI)
    gt_ref[...] = jnp.zeros(gt_ref.shape, f32)
    gh_ref[...] = jnp.zeros(gh_ref.shape, f32)
    gw_ref[...] = jnp.zeros(gw_ref.shape, f32)
    for v in range(FR):
        gt_ref[v : v + FR, :] += grads[8 * v : 8 * v + FR]
    for n, ref in ((0, gh_ref), (1, gw_ref)):
        for a in range(HALF):
            row = 8 * FR + (n * HALF + a) * GRID
            first = 2 * a + GRID - VW
            ref[first : first + VW, :] += grads[row : row + VW]


def conv_back_kernel(dims, meta, y_ref, dk_ref, dv_ref, pq_ref, w_ref, out_ref, gw_ref, pg_ref, mk, mv, gk, gv, acc):
    frames, rows, n_height, hd = dims
    side = meta[0]
    for grid in (gk, gv, mk, mv):
        fill_grid(grid)
    for src in range(HEADS):
        part = y_ref[src].astype(f32)
        for g in range(2):
            for m, grid in ((0, mk), (1, mv)):
                lane = (2 * g + m) * hd
                cut = pad_lanes(part[:, lane : lane + hd], LANE)
                for t2 in range(frames // 2):
                    for h in range(rows):
                        row = src % n_height * rows + h
                        if row >= VW:
                            continue
                        t = src // n_height * frames + g * (frames // 2) + t2
                        at = (t2 * rows + h) * VW
                        grid[flat_row(t, row) : flat_row(t, row) + GRID, :] = jnp.concatenate(
                            [cut[at : at + VW], jnp.zeros((GRID - VW, LANE), f32)], axis=0
                        )
    for ref, grid in ((dk_ref, gk), (dv_ref, gv)):
        for t in range(FR):
            for h in range(VW):
                at = (t * VW + h) * VW
                grid[flat_row(t, h) : flat_row(t, h) + GRID, :] = jnp.concatenate(
                    [ref[at : at + VW, :], jnp.zeros((GRID - VW, LANE), f32)], axis=0
                )
    acc[...] = jnp.zeros(acc.shape, f32)
    local = lax.broadcasted_iota(jnp.int32, (4 * VW, 1), 0)
    line = (local * 3277) >> 16
    column = local - line * VW

    def step(it, carry):
        t = it // (VW // 4)
        quad = it % (VW // 4)
        base = GRID + (1 + t) * PLANE + quad * 4 * GRID
        out = pl.ds(pl.multiple_of(it * (4 * VW), 16), 4 * VW)
        inside = ((quad * 4 + line < side) & (column < side)).astype(f32)
        for m, grid in ((0, gk), (1, gv)):
            back = four_rows(grid, taps9(w_ref, m), base, True)
            pg_ref[out, m * LANE : (m + 1) * LANE] = back * inside
        for m, grid, masked in ((0, gk, mk), (1, gv, mv)):
            for h in range(4):
                here = grid[pl.ds(pl.multiple_of(base + h * GRID, 8), GRID), :]
                turned = [pltpu.roll(here, GRID - 1, 0), here, pltpu.roll(here, 1, 0)]
                for a in range(3):
                    for b in range(3):
                        cells = masked[pl.ds(pl.multiple_of(base + (a - 1) * PLANE + (h + b - 1) * GRID, 8), GRID), :]
                        for c in range(3):
                            prod = cells * turned[c]
                            tap = m * 27 + (a * 3 + b) * 3 + c
                            acc[tap] += prod[0:8] + prod[8:16] + prod[16:24]
        return carry

    lax.fori_loop(0, FR * VW // 4, step, 0)
    for tap in range(54):
        gw_ref[tap : tap + 1, :] = jnp.sum(acc[tap], axis=0, keepdims=True)
    gw_ref[54:, :] = jnp.zeros((gw_ref.shape[0] - 54, LANE), f32)
    span = rows * VW
    for dst in range(HEADS):
        first = dst % n_height * rows
        used = min(max(VW - first, 0), rows) * VW
        lines = []
        for t2 in range(frames // 2):
            parts = []
            for g in range(2):
                t = dst // n_height * frames + g * (frames // 2) + t2
                at = (t * VW + first) * VW
                for m in range(2):
                    parts.append(pg_ref[at : at + used, m * LANE : m * LANE + hd])
            packed = jnp.concatenate(parts, axis=1)
            if used < span:
                packed = jnp.concatenate([packed, jnp.zeros((span - used, 4 * hd), f32)], axis=0)
            lines.append(packed)
        cells = span * (frames // 2)
        out_ref[dst, 0:cells, :] = jnp.concatenate(lines, axis=0).astype(bf)
        per_q = pq_ref.shape[0] // HEADS
        third = per_q // 3
        out_ref[dst, cells : cells + third, :] = jnp.concatenate(
            [pq_ref[dst * per_q + i * third : dst * per_q + (i + 1) * third, :] for i in range(3)], axis=1
        ).astype(bf)


def qkv_grad_kernel(dims, pg_ref, n1_ref, grad_ref, bias_ref):
    frames, rows, n_height, hd, channels = dims
    cells = rows * VW * (frames // 2)
    third = pg_ref.shape[1] - cells
    total_kv = jnp.zeros((2 * hd, channels), f32)
    total_q = jnp.zeros((LANE, channels), f32)
    sum_kv = jnp.zeros((1, 2 * hd), f32)
    sum_q = jnp.zeros((1, LANE), f32)
    for src in range(HEADS):
        packed = pg_ref[src]
        for g in range(2):
            part = packed[0:cells, g * 2 * hd : (g + 1) * 2 * hd]
            total_kv = total_kv + tn(part, n1_ref[src, g * cells : (g + 1) * cells, :])
            sum_kv = sum_kv + jnp.sum(part.astype(f32), axis=0, keepdims=True)
        for i in range(3):
            part = packed[cells:, i * LANE : (i + 1) * LANE]
            at = 2 * cells + i * third
            total_q = total_q + tn(part, n1_ref[src, at : at + third, :])
            sum_q = sum_q + jnp.sum(part.astype(f32), axis=0, keepdims=True)
    total = jnp.concatenate([total_q[0:hd], total_kv], axis=0)
    cols = channels // HEADS
    for n in range(HEADS):
        grad_ref[n] = pad_lanes(total[:, n * cols : (n + 1) * cols], LANE).astype(bf)
    bias_ref[0:1, :] = jnp.concatenate([sum_q[:, 0:hd] * 4.0, sum_kv, jnp.zeros((1, hd), f32)], axis=1)
    bias_ref[1:8, :] = jnp.zeros((7, 4 * hd), f32)


def weight_grad_kernel(dims, meta, keep_ref, cot_ref, act_ref, hg_ref, j_ref, fc2_ref, fc1_ref, rest_ref):
    width, hd, channels = dims
    member = meta[4]
    normed = keep_ref[:, 0:width]
    resid = keep_ref[:, width : 2 * width]
    fc2_ref[...] = tn(cot_ref[...], act_ref[...]).astype(bf)
    fc1 = tn(hg_ref[...], normed)
    for n in range(HEADS):
        fc1_ref[n] = pad_lanes(fc1[:, n * hd : (n + 1) * hd], LANE).astype(bf)
    cols = channels // HEADS
    pick = (
        lax.broadcasted_iota(jnp.int32, (channels, LANE), 0)
        == lax.broadcasted_iota(jnp.int32, (channels, LANE), 1) + member * cols
    ) & (lax.broadcasted_iota(jnp.int32, (channels, LANE), 1) < cols)
    maxima = nn(keep_ref[:, 2 * width :], pick.astype(f32).astype(bf)).astype(bf)
    both = tn(resid, jnp.concatenate([j_ref[...], maxima], axis=1))
    rest_ref[...] = both.astype(bf)


def last_kernel(dims, x_ref, g_ref, w_ref, pg_ref, mx_ref, mg_ref, out_ref, small_ref, full, tiles):
    frames, rows, width, hd = dims
    half = rows // 2
    cells = rows * VW * (frames // 2)
    third = pg_ref.shape[1] - cells
    channels = x_ref.shape[1]
    tops = jnp.zeros((cells, channels), f32)
    lows = jnp.zeros((cells, channels), f32)
    queries = []
    for n in range(HEADS):
        weight = jnp.concatenate(
            [w_ref[width + n * hd : width + (n + 1) * hd, :], w_ref[2 * width + n * hd : 2 * width + (n + 1) * hd, :]], axis=0
        )
        packed = pg_ref[n]
        tops = tops + nn(packed[0:cells, 0 : 2 * hd], weight)
        lows = lows + nn(packed[0:cells, 2 * hd :], weight)
        queries.append(
            jnp.concatenate([packed[cells:, i * LANE : i * LANE + hd] for i in range(3)], axis=0)
        )
    for part, value in ((0, tops), (1, lows)):
        for line in range(frames // 2 * rows):
            at = (part * (frames // 2) * rows + line) * GRID
            full[at : at + GRID, :] = jnp.concatenate(
                [value[line * VW : (line + 1) * VW], jnp.zeros((GRID - VW, channels), f32)], axis=0
            )
    query = nn(jnp.concatenate(queries, axis=1), w_ref[0:width, :])
    per = rows * GRID
    per_q = half * HALF
    g = g_ref[...]
    gain = jnp.zeros((1, channels), f32)
    shift = jnp.zeros((1, channels), f32)
    for t in range(frames):
        cut = slice(t * per_q, (t + 1) * per_q)
        x = x_ref[t * per : (t + 1) * per, :].astype(f32)

        def spread(value):
            wide = pair_spread(value, tiles)
            lines = []
            for a in range(half):
                lines += [wide[a * GRID : (a + 1) * GRID]] * 2
            return jnp.concatenate(lines, axis=0)

        grad = full[t * per : (t + 1) * per, :] + spread(query[cut])
        hits = (x == spread(mx_ref[cut, :])).astype(f32)
        sums = jnp.concatenate(
            [hits[2 * a * GRID : (2 * a + 1) * GRID] + hits[(2 * a + 1) * GRID : (2 * a + 2) * GRID] for a in range(half)], axis=0
        )
        number = pair_reduce(sums, tiles, jnp.add)
        pool = hits * spread(mg_ref[cut, :] / number)
        unit, inverse = layer_unit(x)
        scaled = grad * g
        back = inverse * (
            scaled - jnp.mean(scaled, axis=-1, keepdims=True) - unit * jnp.mean(scaled * unit, axis=-1, keepdims=True)
        )
        out_ref[t * per : (t + 1) * per, :] = (back + pool).astype(bf)
        gain = gain + jnp.sum(grad * unit, axis=0, keepdims=True)
        shift = shift + jnp.sum(grad, axis=0, keepdims=True)
    small_ref[0:1, :] = gain
    small_ref[1:2, :] = shift
    small_ref[2:8, :] = jnp.zeros((6, channels), f32)


def compress_kernel(dims, mem_ref, p_ref, out_ref, tiles):
    frames, rows, width, hd = dims
    half = rows // 2
    for m in range(2):
        sums = [jnp.zeros((GRID, width), f32) for _ in range(2)]
        for s in range(MEM):
            grads = jnp.concatenate([p_ref[n][:, (2 * s + m) * hd : (2 * s + m + 1) * hd] for n in range(HEADS)], axis=1).astype(f32)
            for t in range(frames):
                for a in range(half):
                    at = (a * frames + t) * VH
                    some = jnp.concatenate([grads[at : at + VH], jnp.zeros((HALF - VH, width), f32)], axis=0)
                    wide = pair_spread(some, tiles.at[(t * half + a) % 4])
                    for i in range(2):
                        sums[i] = sums[i] + mem_ref[s, m, t, 2 * a + i].astype(f32) * wide
        odd = (lax.broadcasted_iota(jnp.int32, (GRID, 1), 0) % 2 == 1).astype(f32)
        for i in range(2):
            out_ref[4 * m + 2 * i : 4 * m + 2 * i + 1, :] = jnp.sum(sums[i] * (1.0 - odd), axis=0, keepdims=True)
            out_ref[4 * m + 2 * i + 1 : 4 * m + 2 * i + 2, :] = jnp.sum(sums[i] * odd, axis=0, keepdims=True)


def everywhere(block):
    group = lax.axis_size("tm") * lax.axis_size("height")
    rows = block.shape[0]
    padded = -(-rows // (8 * group)) * 8 * group
    block = jnp.pad(block, ((0, padded - rows), (0, 0))).reshape(group, padded // group, LANE)
    part = jnp.sum(lax.all_to_all(block, G, 0, 0, tiled=True), axis=0)
    part = jnp.sum(lax.all_gather(part, "clip", axis=0), axis=0)
    return lax.all_gather(part, G, axis=0, tiled=True)[0:rows]


def body(clip_input, memory, mem_len, res_id, norm1_gain, norm1_bias, w_qkv, b_qkv, conv_kv, compress, rel_t, rel_h, rel_w,
         w_proj, b_proj, w_short, b_short, norm2_gain, norm2_bias, w_fc1, b_fc1, w_fc2, b_fc2, cotangent):
    _, frames, rows, grid, channels = clip_input.shape
    width = w_proj.shape[0]
    mlp = w_fc1.shape[0]
    hd = width // HEADS
    half = rows // 2
    n_clip = lax.axis_size("clip")
    n_height = lax.axis_size("height")
    tm, height = lax.axis_index("tm"), lax.axis_index("height")
    member = tm * n_height + height
    side = SIDE_SMALL + (SIDE_BIG - SIDE_SMALL) * res_id[0]
    meta = jnp.stack([side, mem_len[0], tm, height, member]).astype(jnp.int32)
    cells_all = frames * rows * GRID
    valid = frames * rows * VW
    per_q = frames * half * HALF
    third = per_q // 3
    queries = HEADS * per_q
    x = clip_input.reshape(cells_all, channels)
    mem = memory[0]
    cot = cotangent.reshape(per_q, width)

    split = b_qkv.reshape(3, HEADS, hd)
    bkv = jnp.concatenate([split[1], split[2], split[1], split[2]], axis=1)
    dims = (frames, rows, width, hd)
    kvp, n1, mx, qh = call(
        functools.partial(qkv_kernel, dims),
        (shape((HEADS, valid // 2, 4 * hd), bf), shape((valid + per_q, channels), f32), shape((per_q, channels), f32), shape((HEADS, per_q, LANE), f32)),
        (meta, x, norm1_gain[None], norm1_bias[None], w_qkv, b_qkv[None, :width], bkv),
        scratch=[pltpu.VMEM((valid, channels), f32), pltpu.VMEM((width // LANE, rows * GRID, LANE), f32)],
    )
    y1 = lax.all_to_all(kvp, G, 0, 0, tiled=True)
    pay2 = call(
        functools.partial(squeeze_kernel, dims),
        shape((HEADS, LANE + third, 4 * hd), bf),
        (mem, compress, qh),
        scratch=[pltpu.VMEM((4, width // LANE, GRID, LANE), f32), pltpu.VMEM((2, MEM, LANE, width), f32)],
        smem=0,
    )
    y2 = lax.all_to_all(pay2, G, 0, 0, tiled=True)
    taps = lax.dynamic_slice_in_dim(conv_kv.reshape(2, 27, width), member * hd, hd, 2)
    taps = jnp.pad(taps, ((0, 0), (0, 5), (0, LANE - hd)))
    taps = jnp.concatenate([taps[0], taps[1]], axis=1)
    hdims = (frames, rows, n_height, hd)
    kc, vc = call(
        functools.partial(conv_kernel, hdims),
        (shape((CUR, 2 * LANE), bf), shape((CUR, LANE), bf)),
        (meta, y1, taps),
        scratch=[pltpu.VMEM((FLAT, LANE), f32)] * 2,
    )
    index = np.arange(queries)
    src, local = index // per_q, index % per_q
    place = np.zeros((8, queries), np.int32)
    place[0] = src // n_height * frames + local // (half * HALF)
    place[1] = src % n_height * half + local // HALF % half
    place[2] = local % HALF
    place = jnp.asarray(place)
    wide = 384
    k_all, kt_all, v_all, qt_all, q_all, o_all, l_all, joined = call(
        functools.partial(attend_kernel, hdims),
        (
            shape((KEYS, 2 * LANE), bf),
            shape((2 * LANE, KEYS), bf),
            shape((KEYS, LANE), bf),
            shape((2 * LANE, queries), bf),
            shape((queries, LANE), bf),
            shape((hd, queries), f32),
            shape((1, queries), f32),
            shape((queries, LANE), bf),
        ),
        (meta, kc, vc, y2, rel_t, rel_h, rel_w, place),
        scratch=[
            pltpu.VMEM((LANE, KEYS), bf),
            pltpu.VMEM((queries, LANE), f32),
            pltpu.VMEM((TAB, hd), f32),
            pltpu.VMEM((KEYS, wide), f32),
        ],
    )
    joined_rows = lax.all_to_all(joined.reshape(HEADS, per_q, LANE), G, 0, 0, tiled=True)
    block = mlp // HEADS
    whole = lambda *dims: pl.BlockSpec(dims, lambda i: (0,) * len(dims))
    keep_width = 2 * width + channels
    output, keep, act, hgrad, dj, max_grad, gb1, small2 = pl.pallas_call(
        functools.partial(mlp_kernel, (width, hd)),
        grid=(HEADS,),
        out_shape=(
            shape((per_q, width), bf),
            shape((per_q, keep_width), bf),
            shape((HEADS, per_q, block), bf),
            shape((HEADS, per_q, block), bf),
            shape((HEADS, per_q, LANE), bf),
            shape((per_q, channels), f32),
            shape((1, mlp), f32),
            shape((8, width), f32),
        ),
        in_specs=[
            whole(HEADS, per_q, LANE),
            whole(per_q, channels),
            whole(per_q, width),
            whole(width, width),
            whole(width, channels),
            whole(1, width),
            whole(1, width),
            whole(1, width),
            pl.BlockSpec((block, width), lambda i: (i, 0)),
            pl.BlockSpec((1, block), lambda i: (0, i)),
            pl.BlockSpec((width, block), lambda i: (0, i)),
            whole(1, width),
        ],
        out_specs=(
            whole(per_q, width),
            whole(per_q, keep_width),
            pl.BlockSpec((1, per_q, block), lambda i: (i, 0, 0)),
            pl.BlockSpec((1, per_q, block), lambda i: (i, 0, 0)),
            whole(HEADS, per_q, LANE),
            whole(per_q, channels),
            pl.BlockSpec((1, block), lambda i: (0, i)),
            whole(8, width),
        ),
        scratch_shapes=[
            pltpu.VMEM((per_q, width), f32),
            pltpu.VMEM((per_q, width), bf),
            pltpu.VMEM((per_q, width), f32),
            pltpu.VMEM((per_q, width), f32),
            pltpu.VMEM((per_q, width), bf),
        ],
        compiler_params=pltpu.CompilerParams(vmem_limit_bytes=56 << 20),
    )(
        joined_rows, mx, cot, w_proj, w_short, (b_proj + b_short)[None], norm2_gain[None], norm2_bias[None],
        w_fc1, b_fc1[None], w_fc2, b_fc2[None],
    )
    dj_head = lax.all_to_all(dj, G, 0, 0, tiled=True).reshape(queries, LANE)
    n1_full = lax.all_gather(n1.astype(bf), G, axis=0)
    cot_full = lax.all_gather(cot, G, axis=0, tiled=True)
    keep_full = lax.all_gather(keep, G, axis=0, tiled=True)
    act_head = lax.all_to_all(act, G, 0, 0, tiled=True).reshape(queries, block)
    hg_head = lax.all_to_all(hgrad, G, 0, 0, tiled=True).reshape(queries, block)

    dk, dv, dmem, pq, gt, gh, gw = call(
        functools.partial(attend_back_kernel, hdims),
        (
            shape((CUR, LANE), f32),
            shape((CUR, LANE), f32),
            shape((HEADS, LANE, 4 * hd), bf),
            shape((queries, LANE), f32),
            shape((16, LANE), f32),
            shape((48, LANE), f32),
            shape((48, LANE), f32),
        ),
        (k_all, kt_all, v_all, qt_all, q_all, o_all, l_all, dj_head, rel_t, rel_h, rel_w, place),
        scratch=[
            pltpu.VMEM((LANE, queries), bf),
            pltpu.VMEM((hd + 48, queries), f32),
            pltpu.VMEM((TAB, hd), f32),
            pltpu.VMEM((TAB, queries), f32),
            pltpu.VMEM((KEYS, LANE), f32),
            pltpu.VMEM((KEYS, LANE), f32),
            pltpu.VMEM((1, queries), f32),
        ],
        smem=0,
    )
    mem_back = lax.all_to_all(dmem, G, 0, 0, tiled=True)
    pgp, gconv = pl.pallas_call(
        functools.partial(conv_back_kernel, hdims),
        out_shape=(shape((HEADS, valid // 2 + third, 4 * hd), bf), shape((64, LANE), f32)),
        in_specs=[pl.BlockSpec(memory_space=pltpu.SMEM)] + [pl.BlockSpec(memory_space=pltpu.VMEM)] * 5,
        out_specs=(pl.BlockSpec(memory_space=pltpu.VMEM),) * 2,
        scratch_shapes=[pltpu.VMEM((CUR, 2 * LANE), f32)] + [pltpu.VMEM((FLAT, LANE), f32)] * 4 + [pltpu.VMEM((54, 8, LANE), f32)],
        compiler_params=pltpu.CompilerParams(vmem_limit_bytes=56 << 20),
    )(meta, y1, dk, dv, pq, taps)
    pg_rows = lax.all_to_all(pgp, G, 0, 0, tiled=True)
    fc2p, fc1p, restp = call(
        functools.partial(weight_grad_kernel, (width, hd, channels)),
        (shape((width, block), bf), shape((HEADS, block, LANE), bf), shape((width, 2 * LANE), bf)),
        (meta, keep_full, cot_full, act_head, hg_head, joined),
    )
    qkvp, bqkv = call(
        functools.partial(qkv_grad_kernel, (frames, rows, n_height, hd, channels)),
        (shape((HEADS, 3 * hd, LANE), bf), shape((8, 4 * hd), f32)),
        (pgp, n1_full),
        smem=0,
    )
    fc1m = lax.all_to_all(fc1p, G, 0, 0, tiled=True)
    qkvm = lax.all_to_all(qkvp, G, 0, 0, tiled=True)

    def over_clips(value):
        value = value.reshape((n_clip, value.shape[0] // n_clip) + value.shape[1:])
        return jnp.sum(lax.all_to_all(value, "clip", 0, 0, tiled=True).astype(f32), axis=0)

    part_fc2 = over_clips(fc2p)
    rest = over_clips(restp)
    part_fc1 = over_clips(fc1m.reshape(mlp, LANE))[:, :hd]
    cols = channels // HEADS
    qkv_rows = qkvm.reshape(HEADS, 3, hd, LANE).transpose(1, 0, 2, 3).reshape(3 * width, LANE)
    part_qkv = over_clips(qkv_rows)[:, :cols]
    part_proj = rest[:, :hd]
    part_short = rest[:, LANE : LANE + cols]

    input_grad, small1 = call(
        functools.partial(last_kernel, dims),
        (shape((cells_all, channels), bf), shape((8, channels), f32)),
        (x, norm1_gain[None], w_qkv, pg_rows, mx, max_grad),
        scratch=[pltpu.VMEM((cells_all, channels), f32), pltpu.VMEM((width // LANE, rows * GRID, LANE), f32)],
        smem=0,
    )
    gcomp = call(
        functools.partial(compress_kernel, dims),
        shape((8, width), f32),
        (mem, mem_back),
        scratch=[pltpu.VMEM((4, width // LANE, GRID, LANE), f32)],
        smem=0,
    )
    head_part = jnp.concatenate([gconv[:54, :hd], bqkv[0, : 3 * hd].reshape(3, hd)], axis=0)
    head_part = lax.all_gather(head_part, G, axis=0)
    head_part = jnp.moveaxis(head_part, 0, 1).reshape(57, width)
    pieces = [head_part / (lax.axis_size("tm") * n_height), gcomp, small2[:4], gb1.reshape(-1, width)]
    flat = jnp.concatenate(pieces, axis=0).reshape(-1, LANE)
    tables = jnp.concatenate([gt, gh, gw], axis=0)
    norm1 = small1[:2].reshape(-1, LANE)
    flat_rows, table_rows = flat.shape[0], tables.shape[0]
    total = everywhere(jnp.concatenate([flat, tables, norm1], axis=0))
    wide_rows = total[:flat_rows].reshape(-1, width)
    tables = total[flat_rows : flat_rows + table_rows]
    norm1 = total[flat_rows + table_rows :].reshape(2, channels)
    bqkv = wide_rows[54:57].reshape(-1)
    base = 57
    gcomp = wide_rows[base : base + 8].reshape(2, 2, 2, width)
    small2 = wide_rows[base + 8 : base + 12]
    gb1 = wide_rows[base + 12 :].reshape(-1)
    return (
        output.reshape(1, frames, half, HALF, width),
        input_grad.reshape(clip_input.shape),
        norm1[0],
        norm1[1],
        part_qkv,
        bqkv,
        wide_rows[:54].reshape(2, 3, 3, 3, width),
        gcomp,
        tables[:15, :hd],
        tables[16 : 16 + 47, :hd],
        tables[64 : 64 + 47, :hd],
        part_proj,
        small2[0],
        part_short,
        small2[0],
        small2[1],
        small2[2],
        part_fc1,
        gb1,
        part_fc2,
        small2[3],
    )


def solution(mesh):
    split = P("clip", "tm", "height", None, None)
    shared = P()
    weight = P("clip", ("tm", "height"))
    placed = (split, P("clip", None, None, "tm", "height", None, None), P("clip"), P("clip")) + (shared,) * 19 + (split,)
    outs = (split, split, shared, shared, weight) + (shared,) * 6 + (weight, shared, weight, shared, shared, shared, weight, shared, weight, shared)
    return jax.shard_map(body, mesh=mesh, in_specs=placed, out_specs=outs, check_vma=False)
```

```python
import functools

import jax
import jax.numpy as jnp
import numpy as np
from jax import lax
from jax.experimental import pallas as pl
from jax.experimental.pallas import tpu as pltpu
from jax.sharding import PartitionSpec as P

HEADS = 8
SIDE_SMALL = 14
SIDE_BIG = 20
MEM = 2
EPSILON = 1e-06
SQRT_HALF = 0.7071067811865476
ROOT_TWO_PI = 2.5066282746310002
LOG2E = 1.4426950408889634
FAR = -1e30

GRID = 24
FR = 8
HALF = GRID // 2
VW = SIDE_BIG
VH = VW // 2
LANE = 128
PLANE = (VW + 1) * GRID
FLAT = GRID + (FR + 2) * PLANE
CUR = FR * VW * VW
KEYS_USED = CUR + MEM * FR * VH * VH
KEYS = -(-KEYS_USED // 256) * 256
LATE_COMP, LATE_SMALL, LATE_TABLE, LATE = 17, 33, 35, 40
TABLE_ROWS = 2 * FR + 4 * GRID
TAB = 8 * FR + 2 * GRID * HALF

bf = jnp.bfloat16
f32 = jnp.float32
HI = lax.Precision.HIGHEST
G = ("tm", "height")


def nn(a, b, **kw):
    return lax.dot_general(a, b, (((1,), (0,)), ((), ())), preferred_element_type=f32, **kw)


def nt(a, b, **kw):
    return lax.dot_general(a, b, (((1,), (1,)), ((), ())), preferred_element_type=f32, **kw)


def tn(a, b, **kw):
    return lax.dot_general(a, b, (((0,), (0,)), ((), ())), preferred_element_type=f32, **kw)


def shape(dims, dtype):
    return jax.ShapeDtypeStruct(dims, dtype)


def cost(us):
    return pl.CostEstimate(flops=int(us * 1e9), bytes_accessed=0, transcendentals=0)


def call(kernel, outs, args, scratch=(), smem=1, us=5, far=0):
    specs = [pl.BlockSpec(memory_space=pltpu.SMEM)] * smem
    specs += [pl.BlockSpec(memory_space=pltpu.VMEM)] * (len(args) - smem - far)
    specs += [pl.BlockSpec(memory_space=pl.ANY)] * far
    return pl.pallas_call(
        kernel,
        out_shape=outs,
        in_specs=specs,
        out_specs=jax.tree.map(lambda _: pl.BlockSpec(memory_space=pltpu.VMEM), outs),
        scratch_shapes=list(scratch),
        compiler_params=pltpu.CompilerParams(vmem_limit_bytes=56 << 20),
        cost_estimate=cost(us),
    )(*args)


def row_of(ref, lo, hi):
    return ref[lo:hi].reshape(1, hi - lo)


def pack_rows(value, scratch, groups):
    rows, lanes = value.shape
    scratch[0:rows, :] = pad_lanes(value, LANE)
    parts = [scratch[pl.ds(g, rows // groups, groups), :][:, 0:lanes] for g in range(groups)]
    return jnp.concatenate(parts, axis=1)


def pad_lanes(x, lanes):
    return jnp.concatenate([x, jnp.zeros((x.shape[0], lanes - x.shape[1]), x.dtype)], axis=1)


def layer_unit(x):
    centred = x - jnp.mean(x, axis=-1, keepdims=True)
    inverse = lax.rsqrt(jnp.mean(centred * centred, axis=-1, keepdims=True) + EPSILON)
    return centred * inverse, inverse


def pair_reduce(value, scratch, op):
    rows, lanes = value.shape
    outs = []
    for j in range(lanes // LANE):
        scratch[j, 0:rows, :] = value[:, j * LANE : (j + 1) * LANE]
    for j in range(lanes // LANE):
        outs.append(op(scratch[j, pl.ds(0, rows // 2, 2), :], scratch[j, pl.ds(1, rows // 2, 2), :]))
    return jnp.concatenate(outs, axis=1)


def join_lines(value, op):
    return jnp.concatenate(
        [op(value[a : a + GRID], value[a + GRID : a + 2 * GRID]) for a in range(0, value.shape[0], 2 * GRID)], axis=0
    )


def pair_spread(value, scratch):
    rows, lanes = value.shape
    for j in range(lanes // LANE):
        part = value[:, j * LANE : (j + 1) * LANE]
        scratch[j, pl.ds(0, rows, 2), :] = part
        scratch[j, pl.ds(1, rows, 2), :] = part
    return jnp.concatenate([scratch[j, 0 : 2 * rows, :] for j in range(lanes // LANE)], axis=1)


def norm_kernel(dims, x_ref, g_ref, b_ref, n1_ref, mx_ref, tiles):
    frames, rows = dims
    half = rows // 2
    channels = x_ref.shape[1]
    per = rows * GRID
    g = row_of(g_ref, 0, channels)
    b = row_of(b_ref, 0, channels)
    for t in range(frames):
        x = x_ref[t * per : (t + 1) * per, :].astype(f32)
        unit, _ = layer_unit(x)
        n1_ref[t * per : (t + 1) * per, :] = (unit * g + b).astype(bf)
        tall = join_lines(x, jnp.maximum)
        mx_ref[t * half * HALF : (t + 1) * half * HALF, :] = pair_reduce(tall, tiles, jnp.maximum)


def squeeze_kernel(dims, mem_ref, c_ref, out_ref, tiles, squeezed):
    frames, rows, width, hd = dims
    half = rows // 2
    count = half * frames * VH
    odd = lax.broadcasted_iota(jnp.int32, (GRID, 1), 0) % 2 == 1
    for m in range(2):
        taps = [jnp.where(odd, c_ref[m, i, 1:2, :], c_ref[m, i, 0:1, :]) for i in range(2)]
        for s in range(MEM):
            for t in range(frames):
                parts = [
                    mem_ref[s, m, t, 2 * a].astype(f32) * taps[0] + mem_ref[s, m, t, 2 * a + 1].astype(f32) * taps[1]
                    for a in range(half)
                ]
                for a in range(half):
                    done = pair_reduce(parts[a], tiles.at[(t * half + a) % 4], jnp.add)
                    squeezed[m, s, a * frames * VH + t * VH : a * frames * VH + (t + 1) * VH, :] = done[0:VH]
            squeezed[m, s, count:LANE, :] = jnp.zeros((LANE - count, width), f32)
    for n in range(HEADS):
        cut = slice(n * hd, (n + 1) * hd)
        out_ref[n] = jnp.concatenate(
            [squeezed[0, 0, :, cut], squeezed[1, 0, :, cut], squeezed[0, 1, :, cut], squeezed[1, 1, :, cut]], axis=1
        ).astype(bf)


def flat_row(t, h):
    return GRID + (1 + t) * PLANE + h * GRID


def fill_grid(grid):
    zero = jnp.zeros((GRID, LANE), f32)
    grid[0 : GRID + PLANE, :] = jnp.zeros((GRID + PLANE, LANE), f32)
    grid[flat_row(FR, 0) :, :] = jnp.zeros((FLAT - flat_row(FR, 0), LANE), f32)
    for t in range(FR):
        grid[flat_row(t, VW) : flat_row(t, VW) + GRID, :] = zero


def taps9(w_ref, part):
    return [[[w_ref[(a * 3 + b) * 3 + c : (a * 3 + b) * 3 + c + 1, part * LANE : (part + 1) * LANE] for c in range(3)] for b in range(3)] for a in range(3)]


def four_rows(grid, weights, base, flip, keep=VW):
    acc = [[None] * 3 for _ in range(4)]
    for line in range(-1, 5):
        for a in range(3):
            shift = (1 - a if flip else a - 1) * PLANE + line * GRID
            cells = grid[pl.ds(pl.multiple_of(base + shift, 8), GRID), :]
            for h in range(4):
                b = (h - line + 1) if flip else (line - h + 1)
                if b < 0 or b > 2:
                    continue
                for c in range(3):
                    term = cells * weights[a][b][c]
                    acc[h][c] = term if acc[h][c] is None else acc[h][c] + term
    outs = []
    for h in range(4):
        left, mid, right = (acc[h][2], acc[h][1], acc[h][0]) if flip else (acc[h][0], acc[h][1], acc[h][2])
        outs.append((pltpu.roll(left, 1, 0) + mid + pltpu.roll(right, GRID - 1, 0))[0:keep])
    return jnp.concatenate(outs, axis=0)


def gather_blocks(dims, meta, refs, out, sems):
    frames, rows, n_height = dims
    member = meta[4]
    per = rows * GRID
    x0, x2, x4, x6a, x6b, x1, x3, x5, x7a, x7b = refs
    copies = []
    for d, parts in enumerate([[x0], [x1], [x2], [x3], [x4], [x5], [x6a, x6b], [x7a, x7b]]):
        src = member ^ d
        t = lax.div(src, n_height) * frames
        at = pl.ds(pl.multiple_of(lax.rem(src, n_height) * per, 16), per)
        for ref in parts:
            for i in range(ref.shape[0] // per):
                copies.append(pltpu.make_async_copy(ref.at[i * per : (i + 1) * per, :], out.at[t, at, :], sems.at[len(copies)]))
                t = t + 1
    return copies


def conv_kernel(dims, meta, w_ref, qkv_ref, bias_ref, *refs):
    frames, rows, n_height, hd = dims
    half = rows // 2
    blocks, (k_ref, v_ref, q_ref, gk, gv, gather, tiles, qrow, sems) = refs[:10], refs[10:]
    copies = gather_blocks(dims[:3], meta, blocks, gather, sems)
    for copy in copies:
        copy.start()
    side, member = meta[0], meta[4]
    width = qkv_ref.shape[0] // 3
    channels = qkv_ref.shape[1]
    for grid in (gk, gv):
        fill_grid(grid)
    blank = jnp.zeros((LANE - hd, channels), bf)
    own = [qkv_ref[pl.ds(pl.multiple_of(p * width + member * hd, 32), hd), :] for p in range(3)]
    weight_q = jnp.concatenate([own[0], blank], axis=0)
    weight_kv = jnp.concatenate([own[1], blank, own[2], blank], axis=0)
    index = lax.broadcasted_iota(jnp.int32, (VW * GRID, 1), 0)
    line = (index * 2731) >> 16
    inside = ((line < side) & (index - line * GRID < side)).astype(f32)
    for copy in copies:
        copy.wait()
    piece = half * HALF
    for t in range(FR):
        query = pair_reduce(join_lines(nt(gather[t], weight_q), jnp.add), tiles.at[t % 2], jnp.add) * 0.25 + bias_ref[0:1, 0:LANE]
        for h in range(n_height):
            at = (t // frames * n_height + h) * frames * piece + t % frames * piece
            qrow[at : at + piece, :] = query[h * piece : (h + 1) * piece]
        pair = ((nt(gather[t, 0 : VW * GRID, :], weight_kv) + bias_ref[0:1, LANE:]) * inside).astype(bf).astype(f32)
        gk[flat_row(t, 0) : flat_row(t, VW), :] = pair[:, 0:LANE]
        gv[flat_row(t, 0) : flat_row(t, VW), :] = pair[:, LANE:]
    q_ref[...] = qrow[...].astype(bf)
    local = lax.broadcasted_iota(jnp.int32, (4 * VW, LANE), 0)
    lane = lax.broadcasted_iota(jnp.int32, (4 * VW, LANE), 1)
    line = (local * 3277) >> 16
    column = local - line * VW
    fixed = [(lane + o == 143 - column) | (lane + o == 191 - column) for o in (0, LANE)]
    ones = (lane == hd).astype(f32)

    def step(it, carry):
        t = it // (VW // 4)
        quad = it % (VW // 4)
        base = GRID + (1 + t) * PLANE + quad * 4 * GRID
        out = pl.ds(pl.multiple_of(it * (4 * VW), 16), 4 * VW)
        mixed_k = four_rows(gk, taps9(w_ref, 0), base, False)
        mixed_v = four_rows(gv, taps9(w_ref, 1), base, False)
        h = quad * 4 + line
        bad = (h >= side) | (column >= side)
        for o in range(2):
            at = lane + o * LANE
            hit = fixed[o] | (at == 103 - t) | (at == 151 - t) | (at == 123 - h) | (at == 171 - h) | ((at == 192) & bad)
            marks = hit.astype(f32)
            k_ref[out, o * LANE : (o + 1) * LANE] = ((mixed_k + marks) if o == 0 else marks).astype(bf)
        v_ref[out, :] = (mixed_v + ones).astype(bf)
        return carry

    lax.fori_loop(0, FR * VW // 4, step, 0)


def build_table(tab, t_ref, h_ref, w_ref):
    tab[...] = jnp.zeros(tab.shape, f32)
    for v in range(FR):
        tab[8 * v : 8 * v + FR, :] = t_ref[v : v + FR, :]
    for n, ref in ((0, h_ref), (1, w_ref)):
        for a in range(HALF):
            at = 8 * FR + (n * HALF + a) * GRID
            first = 2 * a + GRID - VW
            tab[at : at + VW, :] = ref[first : first + VW, :]


def attend_kernel(dims, meta, kc_ref, vc_ref, q_ref, y_ref, t_ref, h_ref, w_ref, place_ref, k_ref, kt_ref, v_ref, qt_ref, o_ref, l_ref, j_ref, vt, tab, s_ref):
    frames, rows, n_height, hd = dims
    half = rows // 2
    side, length = meta[0], meta[1]
    queries = q_ref.shape[0]
    scale = hd**-0.5
    k_ref[0:CUR, :] = kc_ref[...]
    v_ref[0:CUR, :] = vc_ref[...]
    count = half * frames * VH
    each = frames * VH
    lane1 = lax.broadcasted_iota(jnp.int32, (1, LANE), 1)
    at = CUR
    for src in range(HEADS):
        packed = y_ref[src].astype(f32)
        first = src % n_height * half
        used = min(max(VH - first, 0), half) * each
        if used > 0:
            halves = []
            for m in range(2):
                halves.append(jnp.concatenate([packed[0:used, m * hd : (m + 1) * hd], packed[0:used, (2 + m) * hd : (3 + m) * hd]], axis=0))
            index = lax.broadcasted_iota(jnp.int32, (2 * used, LANE), 0)
            step = (index >= used).astype(jnp.int32)
            inner = index - step * used
            a = (inner >= each).astype(jnp.int32) + (inner >= 2 * each).astype(jnp.int32)
            inner = inner - a * each
            c = inner - ((inner * 6554) >> 16) * VH
            bad = (step >= length) | (2 * (first + a) >= side) | (2 * c >= side)
            mark = (bad & (lax.broadcasted_iota(jnp.int32, (2 * used, LANE), 1) == 64)).astype(f32)
            k_ref[at : at + 2 * used, 0:LANE] = pad_lanes(halves[0], LANE).astype(bf)
            k_ref[at : at + 2 * used, LANE:] = mark.astype(bf)
            v_ref[at : at + 2 * used, :] = (pad_lanes(halves[1], LANE) + (lane1 == hd).astype(f32)).astype(bf)
            at += 2 * used
    rest = KEYS - at
    k_ref[at:, 0:LANE] = jnp.zeros((rest, LANE), bf)
    k_ref[at:, LANE:] = jnp.broadcast_to((lane1 == 64).astype(f32), (rest, LANE)).astype(bf)
    v_ref[at:, :] = jnp.zeros((rest, LANE), bf)
    for i in range(KEYS // 256):
        cut = slice(i * 256, (i + 1) * 256)
        kt_ref[:, cut] = k_ref[cut, :].T
        vt[:, cut] = v_ref[cut, :].T
    pt = q_ref[...].astype(f32).T[0:hd]
    build_table(tab, t_ref, h_ref, w_ref)
    along = nn(tab[...], pt, precision=HI)
    tq, aq, cq = place_ref[0:1, :], place_ref[1:2, :], place_ref[2:3, :]
    part_t = jnp.zeros((FR, queries), f32)
    for v in range(FR):
        part_t = jnp.where(tq == v, along[8 * v : 8 * v + FR], part_t)
    parts = []
    for n, place in ((0, aq), (1, cq)):
        part = jnp.zeros((GRID, queries), f32)
        for a in range(HALF):
            row = 8 * FR + (n * HALF + a) * GRID
            part = jnp.where(place == a, along[row : row + GRID], part)
        parts.append(part[0:VW])
    bias = jnp.concatenate([part_t] + parts, axis=0) * hd**0.5
    high = bias.astype(bf)
    low = (bias - high.astype(f32)).astype(bf)
    qt_ref[0:hd, :] = pt.astype(bf)
    qt_ref[hd : hd + 48, :] = high
    qt_ref[hd + 48 : hd + 96, :] = low
    tail = lax.broadcasted_iota(jnp.int32, (64, queries), 0)
    qt_ref[192:256, :] = jnp.where(tail == 0, FAR, 0.0).astype(bf)
    factor = scale * LOG2E
    wide = s_ref.shape[1]
    blocks = [(i, min(i + 512, KEYS)) for i in range(0, KEYS, 512)]

    def one(block, carry):
        cols = pl.ds(pl.multiple_of(block * wide, LANE), wide)
        query = qt_ref[:, cols]
        top = jnp.full((8, wide), FAR, f32)
        for lo, hi in blocks:
            scores = nn(k_ref[lo:hi, :], query)
            s_ref[lo:hi, :] = scores
            top = jnp.maximum(top, jnp.max(scores.reshape((hi - lo) // 8, 8, wide), axis=0))
        top = jnp.max(top, axis=0, keepdims=True) * factor
        total = jnp.zeros((LANE, wide), f32)
        for lo, hi in blocks:
            weights = jnp.exp2(s_ref[lo:hi, :] * factor - top).astype(bf)
            total = total + nn(vt[:, lo:hi], weights)
        norm = total[hd : hd + 1]
        o_ref[:, cols] = total[0:hd] / norm
        l_ref[:, cols] = top + jnp.log2(norm)
        return carry

    lax.fori_loop(0, queries // wide, one, 0)
    j_ref[...] = pad_lanes((o_ref[...] + pt).T, LANE).astype(bf)


def mlp_kernel(dims, j_ref, mx_ref, cot_ref, wp_ref, ws_ref, bp_ref, bs_ref, g_ref, b_ref, w1_ref, b1_ref, w2_ref, b2_ref,
               out_ref, keep_ref, act_ref, dj_ref, mg_ref,
               resid, n2, acc, ngrad, joined, gb1):
    width, hd = dims
    i = pl.program_id(0)
    per_q = cot_ref.shape[0]
    block = w1_ref.shape[0]

    @pl.when(i == 0)
    def _():
        joined[...] = jnp.concatenate([j_ref[n][:, 0:hd] for n in range(HEADS)], axis=1)
        shift = row_of(bp_ref, 0, width) + row_of(bs_ref, 0, width)
        value = nt(joined[...], wp_ref[...]) + nt(mx_ref[...].astype(bf), ws_ref[...]) + shift
        resid[...] = value
        unit, _ = layer_unit(value)
        n2[...] = (unit * row_of(g_ref, 0, width) + row_of(b_ref, 0, width)).astype(bf)
        acc[...] = jnp.zeros(acc.shape, f32)
        ngrad[...] = jnp.zeros(ngrad.shape, f32)

    here = pl.ds(pl.multiple_of(i * block, LANE), block)
    hidden = nt(n2[...], w1_ref[...]) + b1_ref[here].reshape(1, block)
    gate = 0.5 * (1.0 + lax.erf(hidden * SQRT_HALF))
    act = (hidden * gate).astype(bf)
    act_ref[0, 0:per_q, :] = act
    acc[...] += nt(act, w2_ref[...])
    grad = nn(cot_ref[...], w2_ref[...])
    hgrad = (grad * (gate + hidden * jnp.exp(-0.5 * hidden * hidden) / ROOT_TWO_PI)).astype(bf)
    act_ref[0, per_q:, :] = hgrad
    gb1[:, here] = jnp.sum(hgrad.astype(f32), axis=0, keepdims=True)
    ngrad[...] += nn(hgrad, w1_ref[...])

    @pl.when(i == pl.num_programs(0) - 1)
    def _():
        value = resid[...]
        out_ref[...] = (value + acc[...] + row_of(b2_ref, 0, width)).astype(bf)
        unit, inverse = layer_unit(value)
        cot = cot_ref[...].astype(f32)
        grad = ngrad[...]
        scaled = grad * row_of(g_ref, 0, width)
        back = inverse * (
            scaled - jnp.mean(scaled, axis=-1, keepdims=True) - unit * jnp.mean(scaled * unit, axis=-1, keepdims=True)
        )
        low = (cot + back).astype(bf)
        channels = mx_ref.shape[1]
        keep_ref[:, 0:width] = n2[...]
        keep_ref[:, width : 2 * width] = low
        keep_ref[:, 2 * width : 2 * width + channels] = mx_ref[...].astype(bf)
        joined_grad = nn(low, wp_ref[...])
        for n in range(HEADS):
            dj_ref[n] = pad_lanes(joined_grad[:, n * hd : (n + 1) * hd], LANE).astype(bf)
        mg_ref[...] = nn(low, ws_ref[...])
        sums = [jnp.sum(v, axis=0, keepdims=True) for v in (low.astype(f32), grad * unit, grad, cot)] + [gb1[...]]
        lines = [v[:, k : k + LANE] for v in sums for k in range(0, v.shape[1], LANE)]
        exact = jnp.concatenate(lines, axis=0)
        high = exact.astype(bf).astype(f32)
        lines = jnp.concatenate([high, exact - high, jnp.zeros((per_q - 2 * exact.shape[0], LANE), f32)], axis=0)
        keep_ref[:, 2 * width + channels :] = lines.astype(bf)


def attend_back_kernel(dims, k_ref, kt_ref, v_ref, qt_ref, q_ref, o_ref, l_ref, dj_ref, t_ref, h_ref, w_ref, place_ref,
                       dk_ref, dv_ref, mem_ref, pq_ref,
                       dot_ref, dq, tab, dtab, dks, dvs, delta, tables):
    frames, rows, n_height, hd = dims
    half = rows // 2
    queries = q_ref.shape[0]
    scale = hd**-0.5
    factor = scale * LOG2E
    turned = dj_ref[...].astype(f32).T
    dot_ref[...] = turned.astype(bf)
    delta[...] = jnp.sum(turned[0:hd] * o_ref[...], axis=0, keepdims=True)
    dq[...] = jnp.zeros(dq.shape, f32)
    wide = 384

    def chunk(i, carry):
        cut = pl.ds(pl.multiple_of(i * 256, 256), 256)
        dk = jnp.zeros((256, LANE), f32)
        dv = jnp.zeros((256, LANE), f32)
        for lo in range(0, queries, wide):
            cols = slice(lo, lo + wide)
            shares = jnp.exp2(nn(k_ref[cut, :], qt_ref[:, cols]) * factor - l_ref[:, cols])
            slope = nn(v_ref[cut, :], dot_ref[:, cols])
            score = (shares * (slope - delta[:, cols])).astype(bf)
            dv = dv + nn(shares.astype(bf), dj_ref[cols, :])
            dk = dk + nn(score, q_ref[cols, :])
            dq[:, cols] += nn(kt_ref[0 : dq.shape[0], cut], score)
        dks[cut, :] = dk * scale
        dvs[cut, :] = dv
        return carry

    lax.fori_loop(0, KEYS // 256, chunk, 0)
    dk_ref[...] = dks[0:CUR, :]
    dv_ref[...] = dvs[0:CUR, :]
    each = frames * VH
    at = CUR
    for dst in range(HEADS):
        first = dst % n_height * half
        used = min(max(VH - first, 0), half) * each
        if used > 0:
            parts = [ref[at + s * used : at + (s + 1) * used, 0:hd] for s in range(MEM) for ref in (dks, dvs)]
            packed = jnp.concatenate(parts, axis=1)
            at += 2 * used
        if used < LANE:
            zero = jnp.zeros((LANE - used, 4 * hd), f32)
            packed = jnp.concatenate([packed, zero], axis=0) if used > 0 else zero
        mem_ref[dst, 0:LANE, :] = packed.astype(bf)
    build_table(tab, t_ref, h_ref, w_ref)
    tq, aq, cq = place_ref[0:1, :], place_ref[1:2, :], place_ref[2:3, :]
    grad_t = dq[hd : hd + FR, :]
    for v in range(FR):
        dtab[8 * v : 8 * v + FR, :] = jnp.where(tq == v, grad_t, 0.0)
    for n, place in ((0, aq), (1, cq)):
        part = jnp.concatenate(
            [dq[hd + FR + n * VW : hd + FR + (n + 1) * VW, :], jnp.zeros((GRID - VW, queries), f32)], axis=0
        )
        for a in range(HALF):
            row = 8 * FR + (n * HALF + a) * GRID
            dtab[row : row + GRID, :] = jnp.where(place == a, part, 0.0)
    pooled_grad = dq[0:hd, :] * scale + tn(tab[...], dtab[...], precision=HI) + dot_ref[0:hd, :].astype(f32)
    pq_ref[...] = pad_lanes(pooled_grad.T * 0.25, LANE)
    grads = nn(dtab[...], q_ref[...].astype(f32), precision=HI)
    tables[...] = jnp.zeros(tables.shape, f32)
    for v in range(FR):
        tables[v : v + FR, :] += grads[8 * v : 8 * v + FR]
    for n in range(2):
        for a in range(HALF):
            row = 8 * FR + (n * HALF + a) * GRID
            first = 2 * FR + n * 2 * GRID + 2 * a + GRID - VW
            tables[first : first + VW, :] += grads[row : row + VW]
    share = TABLE_ROWS // HEADS
    for dst in range(HEADS):
        part = jnp.concatenate([tables[dst * share : (dst + 1) * share, :], jnp.zeros((16 - share, LANE), f32)], axis=0)
        high = part.astype(bf).astype(f32)
        mem_ref[dst, LANE:, :] = jnp.concatenate([high, part - high, jnp.zeros((16, LANE), f32)], axis=1).astype(bf)


def conv_back_kernel(dims, meta, mk, mv, dk_ref, dv_ref, pq_ref, w_ref, g_ref, b_ref, qkv_ref, *refs):
    frames, rows, n_height, hd = dims
    half = rows // 2
    blocks, (out_ref, gw_ref, stat_ref, pg, gk, gv, acc, wide, gather, tall, sems) = refs[:10], refs[10:]
    copies = gather_blocks(dims[:3], meta, blocks, gather, sems)
    for copy in copies:
        copy.start()
    side, member = meta[0], meta[4]
    width = qkv_ref.shape[0] // 3
    channels = qkv_ref.shape[1]
    for grid in (gk, gv):
        fill_grid(grid)
    for ref, grid in ((dk_ref, gk), (dv_ref, gv)):
        for t in range(FR):
            for h in range(VW):
                at = (t * VW + h) * VW
                grid[flat_row(t, h) : flat_row(t, h) + GRID, :] = jnp.concatenate(
                    [ref[at : at + VW, :], jnp.zeros((GRID - VW, LANE), f32)], axis=0
                )
    acc[...] = jnp.zeros(acc.shape, f32)
    local = lax.broadcasted_iota(jnp.int32, (4 * GRID, 1), 0)
    line = (local * 2731) >> 16
    column = local - line * GRID
    empty = jnp.zeros(((GRID - VW) * GRID, 2 * LANE), bf)
    for t in range(FR):
        pg[t * GRID * GRID + VW * GRID : (t + 1) * GRID * GRID, LANE:] = empty

    def step(it, carry):
        t = it // (VW // 4)
        quad = it % (VW // 4)
        base = GRID + (1 + t) * PLANE + quad * 4 * GRID
        out = pl.ds(pl.multiple_of((t * GRID + quad * 4) * GRID, 32), 4 * GRID)
        inside = ((quad * 4 + line < side) & (column < side)).astype(f32)
        for m, grid in ((0, gk), (1, gv)):
            back = four_rows(grid, taps9(w_ref, m), base, True, GRID)
            pg[out, (1 + m) * LANE : (2 + m) * LANE] = (back * inside).astype(bf)
        for m, grid, masked in ((0, gk, mk), (1, gv, mv)):
            for h in range(4):
                here = grid[pl.ds(pl.multiple_of(base + h * GRID, 8), GRID), :]
                turned = [pltpu.roll(here, GRID - 1, 0), here, pltpu.roll(here, 1, 0)]
                for a in range(3):
                    for b in range(3):
                        cells = masked[pl.ds(pl.multiple_of(base + (a - 1) * PLANE + (h + b - 1) * GRID, 8), GRID), :]
                        for c in range(3):
                            prod = cells * turned[c]
                            tap = m * 27 + (a * 3 + b) * 3 + c
                            acc[tap] += prod[0:8] + prod[8:16] + prod[16:24]
        return carry

    lax.fori_loop(0, FR * VW // 4, step, 0)
    for tap in range(54):
        gw_ref[tap : tap + 1, :] = jnp.sum(acc[tap], axis=0, keepdims=True)
    gw_ref[54:, :] = jnp.zeros((gw_ref.shape[0] - 54, LANE), f32)
    queries = pq_ref.shape[0]
    wide[pl.ds(0, queries, 2), :] = pq_ref[...]
    wide[pl.ds(1, queries, 2), :] = pq_ref[...]
    per_q = queries // HEADS
    for src in range(HEADS):
        for t in range(frames):
            for a in range(half):
                at = ((src * frames + t) * half + a) * GRID
                lines = wide[at : at + GRID, :]
                row = ((src // n_height * frames + t) * GRID + src % n_height * rows + 2 * a) * GRID
                pg[row : row + 2 * GRID, 0:LANE] = jnp.concatenate([lines, lines], axis=0).astype(bf)
    span = rows * VW
    cells = span * (frames // 2)
    third = per_q // 3
    for dst in range(HEADS):
        first = dst % n_height * rows
        lines = []
        for t2 in range(frames // 2):
            parts = []
            for g in range(2):
                t = dst // n_height * frames + g * (frames // 2) + t2
                at = (t * GRID + first) * GRID
                block = pg[at : at + rows * GRID, LANE:].astype(f32)
                block = jnp.concatenate([block[h * GRID : h * GRID + VW] for h in range(rows)], axis=0)
                parts += [block[:, 0:hd], block[:, LANE : LANE + hd]]
            lines.append(jnp.concatenate(parts, axis=1))
        out_ref[dst, 0:cells, :] = jnp.concatenate(lines, axis=0).astype(bf)
        out_ref[dst, cells : cells + third, :] = jnp.concatenate(
            [pq_ref[dst * per_q + i * third : dst * per_q + (i + 1) * third, :] for i in range(3)], axis=1
        ).astype(bf)
    for copy in copies:
        copy.wait()
    total = jnp.zeros((3 * LANE, channels), f32)
    sums = jnp.zeros((1, 3 * LANE), f32)
    for t in range(FR):
        part = pg[t * GRID * GRID : (t + 1) * GRID * GRID, :]
        total = total + tn(part, gather[t])
        sums = sums + jnp.sum(part.astype(f32), axis=0, keepdims=True)
    total = jnp.concatenate([total[p * LANE : p * LANE + hd] for p in range(3)], axis=0)
    sums = jnp.concatenate([sums[:, p * LANE : p * LANE + hd] for p in range(3)], axis=1)
    cols = channels // HEADS
    packed = 3 * hd // HEADS
    rest = out_ref.shape[1] - cells - third
    for n in range(HEADS):
        value = pack_rows(total[:, n * cols : (n + 1) * cols], tall.at[n % 2], HEADS)
        out_ref[n, cells + third :, :] = jnp.concatenate([value, jnp.zeros((rest - packed, channels), f32)], axis=0).astype(bf)
    weight = jnp.concatenate(
        [qkv_ref[pl.ds(pl.multiple_of(p * width + member * hd, 32), hd), :].astype(f32) for p in range(3)], axis=0
    )
    shift = nn(jnp.broadcast_to(sums, (8, 3 * hd)), weight, precision=HI)[0:1]
    gain = jnp.sum(total * weight, axis=0, keepdims=True)
    gain = (gain - shift * row_of(b_ref, 0, channels)) / row_of(g_ref, 0, channels)
    stat_ref[0:1, :] = pad_lanes(sums, channels)
    stat_ref[1:2, :] = gain
    stat_ref[2:3, :] = shift
    stat_ref[3:8, :] = jnp.zeros((5, channels), f32)


def weight_grad_kernel(dims, meta, keep_ref, ah_ref, j_ref, cot_ref, dmem_ref, fc2_ref, fc1_ref, proj_ref, short_ref, small_ref,
                       act, hgrad, tall, parts):
    width, hd, channels, per_q = dims
    member = meta[4]
    for src in range(HEADS):
        cut = slice(src * per_q, (src + 1) * per_q)
        act[cut, :] = ah_ref[src, 0:per_q, :]
        hgrad[cut, :] = ah_ref[src, per_q:, :]
    normed = keep_ref[:, 0:width]
    resid = keep_ref[:, width : 2 * width]
    fc1 = tn(hgrad[...], normed)
    for n in range(HEADS):
        fc1_ref[n, 0 : dmem_ref.shape[1], :] = dmem_ref[n]
        fc1_ref[n, dmem_ref.shape[1] :, :] = pack_rows(fc1[:, n * hd : (n + 1) * hd], parts.at[n % 2], channels // hd).astype(bf)
    cols = channels // HEADS
    lane = lax.broadcasted_iota(jnp.int32, (channels, LANE), 1)
    pick = (lax.broadcasted_iota(jnp.int32, (channels, LANE), 0) == lane + member * cols) & (lane < cols)
    maxima = nn(keep_ref[:, 2 * width : 2 * width + channels], pick.astype(f32).astype(bf)).astype(bf)
    both = tn(resid, jnp.concatenate([j_ref[...], maxima], axis=1))
    proj_ref[...] = pack_rows(both[:, 0:hd], tall.at[0], channels // hd).astype(bf)
    short_ref[...] = pack_rows(both[:, LANE : LANE + cols], tall.at[1], channels // cols).astype(bf)
    sums = jnp.zeros((per_q, LANE), f32)
    for src in range(HEADS):
        sums = sums + keep_ref[src * per_q : (src + 1) * per_q, 2 * width + channels :].astype(f32)
    lines = HEADS * width // LANE
    sums = sums[0:lines] + sums[lines : 2 * lines]
    each = lines // HEADS
    own = jnp.zeros((each, LANE), f32)
    for n in range(HEADS):
        own = jnp.where(member == n, sums[n * each : (n + 1) * each], own)
    small_ref[...] = jnp.concatenate([own, jnp.zeros((8 - each, LANE), f32)], axis=0)
    fc2_ref[...] = tn(cot_ref[...], act[...]).astype(bf)


def last_kernel(dims, x_ref, g_ref, w_ref, pg_ref, mx_ref, mg_ref, out_ref, full, tiles):
    frames, rows, width, hd = dims
    half = rows // 2
    cells = rows * VW * (frames // 2)
    third = frames * half * HALF // 3
    channels = x_ref.shape[1]
    tops = jnp.zeros((cells, channels), f32)
    lows = jnp.zeros((cells, channels), f32)
    queries = []
    for n in range(HEADS):
        weight = jnp.concatenate(
            [w_ref[width + n * hd : width + (n + 1) * hd, :], w_ref[2 * width + n * hd : 2 * width + (n + 1) * hd, :]], axis=0
        )
        packed = pg_ref[n]
        tops = tops + nn(packed[0:cells, 0 : 2 * hd], weight)
        lows = lows + nn(packed[0:cells, 2 * hd :], weight)
        queries.append(
            jnp.concatenate([packed[cells : cells + third, i * LANE : i * LANE + hd] for i in range(3)], axis=0)
        )
    for part, value in ((0, tops), (1, lows)):
        for line in range(frames // 2 * rows):
            at = (part * (frames // 2) * rows + line) * GRID
            full[at : at + GRID, :] = jnp.concatenate(
                [value[line * VW : (line + 1) * VW], jnp.zeros((GRID - VW, channels), f32)], axis=0
            )
    query = nn(jnp.concatenate(queries, axis=1), w_ref[0:width, :])
    per = rows * GRID
    per_q = half * HALF
    g = row_of(g_ref, 0, channels)
    for t in range(frames):
        cut = slice(t * per_q, (t + 1) * per_q)
        x = x_ref[t * per : (t + 1) * per, :].astype(f32)

        def spread(value):
            wide = pair_spread(value, tiles)
            lines = []
            for a in range(half):
                lines += [wide[a * GRID : (a + 1) * GRID]] * 2
            return jnp.concatenate(lines, axis=0)

        grad = full[t * per : (t + 1) * per, :] + spread(query[cut])
        hits = (x == spread(mx_ref[cut, :])).astype(f32)
        sums = jnp.concatenate(
            [hits[2 * a * GRID : (2 * a + 1) * GRID] + hits[(2 * a + 1) * GRID : (2 * a + 2) * GRID] for a in range(half)], axis=0
        )
        number = pair_reduce(sums, tiles, jnp.add)
        pool = hits * spread(mg_ref[cut, :] / number)
        unit, inverse = layer_unit(x)
        scaled = grad * g
        back = inverse * (
            scaled - jnp.mean(scaled, axis=-1, keepdims=True) - unit * jnp.mean(scaled * unit, axis=-1, keepdims=True)
        )
        out_ref[t * per : (t + 1) * per, :] = (back + pool).astype(bf)


def compress_kernel(dims, mem_ref, p_ref, conv_ref, stat_ref, small_ref, late_ref, tiles, lines):
    frames, rows, width, hd = dims
    half = rows // 2
    channels = late_ref.shape[1]
    for m in range(2):
        sums = [jnp.zeros((GRID, width), f32) for _ in range(2)]
        for s in range(MEM):
            grads = jnp.concatenate(
                [p_ref[n][0:LANE, (2 * s + m) * hd : (2 * s + m + 1) * hd] for n in range(HEADS)], axis=1
            ).astype(f32)
            for t in range(frames):
                for a in range(half):
                    at = (a * frames + t) * VH
                    some = jnp.concatenate([grads[at : at + VH], jnp.zeros((HALF - VH, width), f32)], axis=0)
                    wide = pair_spread(some, tiles.at[(t * half + a) % 4])
                    for i in range(2):
                        sums[i] = sums[i] + mem_ref[s, m, t, 2 * a + i].astype(f32) * wide
        odd = (lax.broadcasted_iota(jnp.int32, (GRID, 1), 0) % 2 == 1).astype(f32)
        for i in range(2):
            for j, keep in ((0, 1.0 - odd), (1, odd)):
                done = jnp.sum(sums[i] * keep, axis=0, keepdims=True)
                for k in range(width // channels):
                    at = LATE_COMP + 8 * k + 4 * m + 2 * i + j
                    lines[at : at + 1, :] = done[:, k * channels : (k + 1) * channels]
    conv = jnp.concatenate([conv_ref[14 * g : 14 * (g + 1), 0:hd] for g in range(4)], axis=1)
    lines[0:14, :] = conv
    lines[14:17, :] = stat_ref[0:3, :]
    for k in range(2):
        lines[LATE_SMALL + k : LATE_SMALL + k + 1, :] = jnp.concatenate([small_ref[3 * k + i : 3 * k + i + 1, :] for i in range(3)], axis=1)
    tables = jnp.zeros((16, LANE), f32)
    for n in range(HEADS):
        part = p_ref[n][LANE:, :].astype(f32)
        tables = tables + part[:, 0:LANE] + part[:, LANE : 2 * LANE]
    lines[LATE_TABLE : LATE_TABLE + 5, :] = jnp.concatenate([tables[5 * g : 5 * (g + 1), :] for g in range(3)], axis=1)
    late_ref[...] = lines[...].astype(bf)


def sums_kernel(dims, late_ref, g1_ref, b1_ref, bqkv_ref, conv_ref, comp_ref, t_ref, h_ref, w_ref, bp_ref, bs_ref, g2_ref, b2_ref, bf1_ref, bf2_ref, lines):
    width, hd, channels = dims
    parts = []
    for n in range(HEADS):
        parts.append(late_ref[n])
    total = parts[0]
    for n in range(1, HEADS):
        total = total + parts[n]
    for g in range(4):
        conv = jnp.concatenate([parts[n][0:14, g * hd : (g + 1) * hd] for n in range(HEADS)], axis=1)
        for r in range(14):
            i = 14 * g + r
            if i < 54:
                conv_ref[i // 27, i % 27 // 9, i % 9 // 3, i % 3 : i % 3 + 1, :] = conv[r : r + 1]
    for p in range(3):
        value = jnp.concatenate([parts[n][14:15, p * hd : (p + 1) * hd] for n in range(HEADS)], axis=1)
        bqkv_ref[p * width : (p + 1) * width] = value.reshape(width)
    g1_ref[...] = total[15:16].reshape(channels)
    b1_ref[...] = total[16:17].reshape(channels)
    for i in range(8):
        value = jnp.concatenate([total[LATE_COMP + 8 * k + i : LATE_COMP + 8 * k + i + 1] for k in range(2)], axis=1)
        comp_ref[i // 4, i % 4 // 2, i % 2 : i % 2 + 1, :] = value
    for n in range(HEADS):
        value = jnp.concatenate([parts[n][LATE_SMALL + k : LATE_SMALL + k + 1] for k in range(2)], axis=1).reshape(width)
        if n == 0:
            bp_ref[...] = value
            bs_ref[...] = value
        elif n < 4:
            (g2_ref, b2_ref, bf2_ref)[n - 1][...] = value
        else:
            bf1_ref[(n - 4) * width : (n - 3) * width] = value
    share = TABLE_ROWS // HEADS
    for n in range(HEADS):
        part = parts[n][LATE_TABLE : LATE_TABLE + 5]
        value = jnp.concatenate([part[:, g * LANE : (g + 1) * LANE] for g in range(3)], axis=0)
        lines[n * share : (n + 1) * share, :] = value[0:share]
    at = 0
    for ref, step in ((t_ref, 2 * FR), (h_ref, 2 * GRID), (w_ref, 2 * GRID)):
        ref[...] = lines[at : at + ref.shape[0], 0:hd]
        at += step


def body(clip_input, memory, mem_len, res_id, norm1_gain, norm1_bias, w_qkv, b_qkv, conv_kv, compress, rel_t, rel_h, rel_w,
         w_proj, b_proj, w_short, b_short, norm2_gain, norm2_bias, w_fc1, b_fc1, w_fc2, b_fc2, cotangent):
    _, frames, rows, grid, channels = clip_input.shape
    width = w_proj.shape[0]
    mlp = w_fc1.shape[0]
    hd = width // HEADS
    half = rows // 2
    n_clip = lax.axis_size("clip")
    n_height = lax.axis_size("height")
    tm, height = lax.axis_index("tm"), lax.axis_index("height")
    member = tm * n_height + height
    side = SIDE_SMALL + (SIDE_BIG - SIDE_SMALL) * res_id[0]
    meta = jnp.stack([side, mem_len[0], tm, height, member]).astype(jnp.int32)
    cells_all = frames * rows * GRID
    valid = frames * rows * VW
    per_q = frames * half * HALF
    third = per_q // 3
    queries = HEADS * per_q
    x = clip_input.reshape(cells_all, channels)
    mem = memory[0]
    cot = cotangent.reshape(per_q, width)

    dims = (frames, rows, width, hd)
    n1, mx = call(
        functools.partial(norm_kernel, (frames, rows)),
        (shape((cells_all, channels), bf), shape((per_q, channels), f32)),
        (x, norm1_gain, norm1_bias),
        scratch=[pltpu.VMEM((channels // LANE, rows * GRID, LANE), f32)],
        smem=0,
        us=3,
    )

    def swap(value, bit):
        if bit == 4:
            return lax.ppermute(value, "tm", [(i, i ^ 1) for i in range(lax.axis_size("tm"))])
        return lax.ppermute(value, "height", [(i, i ^ bit) for i in range(n_height)])

    x2, x4, x1 = swap(n1, 2), swap(n1, 4), swap(n1, 1)
    pay2 = call(
        functools.partial(squeeze_kernel, dims),
        shape((HEADS, LANE, 4 * hd), bf),
        (mem, compress),
        scratch=[pltpu.VMEM((4, width // LANE, GRID, LANE), f32), pltpu.VMEM((2, MEM, LANE, width), f32)],
        smem=0,
        us=5,
    )
    x2, x4, pay2 = lax.optimization_barrier((x2, x4, pay2))
    cut = cells_all // 2
    x6a, x6b = swap(x2[:cut], 4), swap(x4[cut:], 2)
    x3, x5 = swap(x2, 1), swap(x4, 1)
    x7a, x7b = swap(x6a, 1), swap(x6b, 1)
    y2 = lax.all_to_all(pay2, G, 0, 0, tiled=True)
    cot_late, x7a = lax.optimization_barrier((cot, x7a))
    cot_full = lax.all_gather(cot_late, G, axis=0, tiled=True)
    taps = lax.dynamic_slice_in_dim(conv_kv.reshape(2, 27, width), member * hd, hd, 2)
    taps = jnp.pad(taps, ((0, 0), (0, 5), (0, LANE - hd)))
    taps = jnp.concatenate([taps[0], taps[1]], axis=1)
    hdims = (frames, rows, n_height, hd)
    bias = lax.dynamic_slice_in_dim(b_qkv.reshape(3, width), member * hd, hd, 1)
    bias = jnp.pad(bias, ((0, 0), (0, LANE - hd))).reshape(1, 3 * LANE)
    vmem = pl.BlockSpec(memory_space=pltpu.VMEM)
    blocks = (n1, x2, x4, x6a, x6b, x1, x3, x5, x7a, x7b)
    kc, vc, q_all, mk, mv = pl.pallas_call(
        functools.partial(conv_kernel, hdims),
        out_shape=(
            shape((CUR, 2 * LANE), bf),
            shape((CUR, LANE), bf),
            shape((queries, LANE), bf),
            shape((FLAT, LANE), f32),
            shape((FLAT, LANE), f32),
        ),
        in_specs=[pl.BlockSpec(memory_space=pltpu.SMEM)] + [vmem] * 3 + [pl.BlockSpec(memory_space=pl.ANY)] * 10,
        out_specs=(vmem,) * 5,
        scratch_shapes=[
            pltpu.VMEM((FR, GRID * GRID, channels), bf),
            pltpu.VMEM((2, 1, GRID * HALF, LANE), f32),
            pltpu.VMEM((queries, LANE), f32),
            pltpu.SemaphoreType.DMA((HEADS * frames,)),
        ],
        compiler_params=pltpu.CompilerParams(vmem_limit_bytes=56 << 20),
        cost_estimate=cost(18),
    )(meta, taps, w_qkv, bias, *blocks)
    index = np.arange(queries)
    src, local = index // per_q, index % per_q
    place = np.zeros((8, queries), np.int32)
    place[0] = src // n_height * frames + local // (half * HALF)
    place[1] = src % n_height * half + local // HALF % half
    place[2] = local % HALF
    place = jnp.asarray(place)
    wide = 384
    k_all, kt_all, v_all, qt_all, o_all, l_all, joined = call(
        functools.partial(attend_kernel, hdims),
        (
            shape((KEYS, 2 * LANE), bf),
            shape((2 * LANE, KEYS), bf),
            shape((KEYS, LANE), bf),
            shape((2 * LANE, queries), bf),
            shape((hd, queries), f32),
            shape((1, queries), f32),
            shape((queries, LANE), bf),
        ),
        (meta, kc, vc, q_all, y2, rel_t, rel_h, rel_w, place),
        scratch=[
            pltpu.VMEM((LANE, KEYS), bf),
            pltpu.VMEM((TAB, hd), f32),
            pltpu.VMEM((KEYS, wide), f32),
        ],
        us=16,
    )
    joined_rows = lax.all_to_all(joined.reshape(HEADS, per_q, LANE), G, 0, 0, tiled=True)
    block = mlp // HEADS
    whole = lambda *dims: pl.BlockSpec(dims, lambda i: (0,) * len(dims))
    keep_width = 2 * width + channels
    keep_width = keep_width + LANE
    output, keep, acthg, dj, max_grad = pl.pallas_call(
        functools.partial(mlp_kernel, (width, hd)),
        grid=(HEADS,),
        out_shape=(
            shape((per_q, width), bf),
            shape((per_q, keep_width), bf),
            shape((HEADS, 2 * per_q, block), bf),
            shape((HEADS, per_q, LANE), bf),
            shape((per_q, channels), f32),
        ),
        in_specs=[
            whole(HEADS, per_q, LANE),
            whole(per_q, channels),
            whole(per_q, width),
            whole(width, width),
            whole(width, channels),
            whole(width),
            whole(width),
            whole(width),
            whole(width),
            pl.BlockSpec((block, width), lambda i: (i, 0)),
            whole(mlp),
            pl.BlockSpec((width, block), lambda i: (0, i)),
            whole(width),
        ],
        out_specs=(
            whole(per_q, width),
            whole(per_q, keep_width),
            pl.BlockSpec((1, 2 * per_q, block), lambda i: (i, 0, 0)),
            whole(HEADS, per_q, LANE),
            whole(per_q, channels),
        ),
        scratch_shapes=[
            pltpu.VMEM((per_q, width), f32),
            pltpu.VMEM((per_q, width), bf),
            pltpu.VMEM((per_q, width), f32),
            pltpu.VMEM((per_q, width), f32),
            pltpu.VMEM((per_q, width), bf),
            pltpu.VMEM((1, mlp), f32),
        ],
        compiler_params=pltpu.CompilerParams(vmem_limit_bytes=56 << 20),
        cost_estimate=cost(14),
    )(joined_rows, mx, cot, w_proj, w_short, b_proj, b_short, norm2_gain, norm2_bias, w_fc1, b_fc1, w_fc2, b_fc2)
    dj_head = lax.all_to_all(dj, G, 0, 0, tiled=True).reshape(queries, LANE)
    keep_full = lax.all_gather(keep, G, axis=0, tiled=True)
    acthg, dj_head = lax.optimization_barrier((acthg, dj_head))
    ah_head = lax.all_to_all(acthg, G, 0, 0, tiled=True)

    dk, dv, dmem, pq = call(
        functools.partial(attend_back_kernel, hdims),
        (
            shape((CUR, LANE), f32),
            shape((CUR, LANE), f32),
            shape((HEADS, LANE + 16, 4 * hd), bf),
            shape((queries, LANE), f32),
        ),
        (k_all, kt_all, v_all, qt_all, q_all, o_all, l_all, dj_head, rel_t, rel_h, rel_w, place),
        scratch=[
            pltpu.VMEM((LANE, queries), bf),
            pltpu.VMEM((hd + 48, queries), f32),
            pltpu.VMEM((TAB, hd), f32),
            pltpu.VMEM((TAB, queries), f32),
            pltpu.VMEM((KEYS, LANE), f32),
            pltpu.VMEM((KEYS, LANE), f32),
            pltpu.VMEM((1, queries), f32),
            pltpu.VMEM((TABLE_ROWS, LANE), f32),
        ],
        smem=0,
        us=32,
    )
    cols = channels // HEADS
    taken = dmem.shape[1]
    fc2p, fc1p, projp, shortp, small2 = call(
        functools.partial(weight_grad_kernel, (width, hd, channels, per_q)),
        (
            shape((width, block), bf),
            shape((HEADS, taken + block * hd // channels, channels), bf),
            shape((width * hd // channels, channels), bf),
            shape((width // HEADS, channels), bf),
            shape((8, LANE), f32),
        ),
        (meta, keep_full, ah_head, joined, cot_full, dmem),
        scratch=[
            pltpu.VMEM((queries, block), bf),
            pltpu.VMEM((queries, block), bf),
            pltpu.VMEM((2, width, LANE), f32),
            pltpu.VMEM((2, block, LANE), f32),
        ],
        us=9,
    )

    def over_clips(parts, permute):
        parts = [v.reshape(n_clip, v.shape[0] // n_clip, v.shape[1]) for v in parts]
        ends = np.cumsum([0] + [v.shape[1] for v in parts])
        value = jnp.concatenate(parts, axis=1) if len(parts) > 1 else parts[0]
        if permute and n_clip <= 4:
            clip = lax.axis_index("clip")
            total = lax.dynamic_index_in_dim(value, clip, 0, keepdims=False).astype(f32)
            for k in range(1, n_clip):
                sent = lax.dynamic_index_in_dim(value, lax.rem(clip + k, n_clip), 0, keepdims=False)
                total = total + lax.ppermute(sent, "clip", [(i, (i + k) % n_clip) for i in range(n_clip)]).astype(f32)
        else:
            total = jnp.sum(lax.all_to_all(value, "clip", 0, 0, tiled=True).astype(f32), axis=0)
        return [total[lo:hi] for lo, hi in zip(ends, ends[1:])]

    dk, fc1p = lax.optimization_barrier((dk, fc1p))
    first_back = lax.all_to_all(fc1p, G, 0, 0, tiled=True)
    part_fc2, part_proj, part_short = over_clips([fc2p, projp, shortp], True)
    sent = valid // 2 + third
    pgp, gconv, stats = pl.pallas_call(
        functools.partial(conv_back_kernel, hdims),
        out_shape=(shape((HEADS, sent + 48, 4 * hd), bf), shape((64, LANE), f32), shape((8, channels), f32)),
        in_specs=[pl.BlockSpec(memory_space=pltpu.SMEM)] + [vmem] * 9 + [pl.BlockSpec(memory_space=pl.ANY)] * 10,
        out_specs=(vmem,) * 3,
        scratch_shapes=[
            pltpu.VMEM((FR * GRID * GRID, 3 * LANE), bf),
            pltpu.VMEM((FLAT, LANE), f32),
            pltpu.VMEM((FLAT, LANE), f32),
            pltpu.VMEM((54, 8, LANE), f32),
            pltpu.VMEM((2 * queries, LANE), f32),
            pltpu.VMEM((FR, GRID * GRID, channels), bf),
            pltpu.VMEM((2, 3 * hd, LANE), f32),
            pltpu.SemaphoreType.DMA((HEADS * frames,)),
        ],
        compiler_params=pltpu.CompilerParams(vmem_limit_bytes=56 << 20),
        cost_estimate=cost(28),
    )(meta, mk, mv, dk, dv, pq, taps, norm1_gain, norm1_bias, w_qkv, *blocks)
    pgp, first_back = lax.optimization_barrier((pgp, first_back))
    pg_rows = lax.all_to_all(pgp, G, 0, 0, tiled=True)
    mem_back = first_back[:, :taken]
    [part_fc1] = over_clips([first_back[:, taken:].reshape(-1, channels)], True)
    late = call(
        functools.partial(compress_kernel, dims),
        shape((LATE, channels), bf),
        (mem, mem_back, gconv, stats, small2),
        scratch=[pltpu.VMEM((4, width // LANE, GRID, LANE), f32), pltpu.VMEM((LATE, channels), f32)],
        smem=0,
        us=6,
    )
    late = jnp.sum(lax.all_gather(late, "clip", axis=0).astype(f32), axis=0)
    late_full = lax.all_gather(late, G, axis=0)
    vector = lambda n: shape((n,), f32)
    g1, b1, gbq, gconv, gcomp, gt, gh, gw, gbp, gbs, g2, b2, gb1, gb2 = call(
        functools.partial(sums_kernel, (width, hd, channels)),
        (
            vector(channels), vector(channels), vector(3 * width), shape(conv_kv.shape, f32), shape(compress.shape, f32),
            shape(rel_t.shape, f32), shape(rel_h.shape, f32), shape(rel_w.shape, f32),
            vector(width), vector(width), vector(width), vector(width), vector(mlp), vector(width),
        ),
        (late_full,),
        scratch=[pltpu.VMEM((TABLE_ROWS, LANE), f32)],
        smem=0,
        us=3,
    )
    pg_rows, gb1 = lax.optimization_barrier((pg_rows, gb1))
    qkv_rows = pg_rows[:, sent : sent + 3 * hd // HEADS]
    qkv_rows = qkv_rows.reshape(HEADS, 3, hd // HEADS, channels).transpose(1, 0, 2, 3).reshape(-1, channels)
    [part_qkv] = over_clips([qkv_rows], False)
    input_grad = call(
        functools.partial(last_kernel, dims),
        shape((cells_all, channels), bf),
        (x, norm1_gain, w_qkv, pg_rows, mx, max_grad),
        scratch=[pltpu.VMEM((cells_all, channels), f32), pltpu.VMEM((width // LANE, rows * GRID, LANE), f32)],
        smem=0,
        us=8,
    )
    return (
        output.reshape(1, frames, half, HALF, width),
        input_grad.reshape(clip_input.shape),
        g1,
        b1,
        part_qkv.reshape(-1, cols),
        gbq,
        gconv,
        gcomp,
        gt,
        gh,
        gw,
        part_proj.reshape(-1, hd),
        gbp,
        part_short.reshape(-1, cols),
        gbs,
        g2,
        b2,
        part_fc1.reshape(-1, hd),
        gb1,
        part_fc2,
        gb2,
    )


def solution(mesh):
    split = P("clip", "tm", "height", None, None)
    shared = P()
    weight = P("clip", ("tm", "height"))
    placed = (split, P("clip", None, None, "tm", "height", None, None), P("clip"), P("clip")) + (shared,) * 19 + (split,)
    outs = (split, split, shared, shared, weight) + (shared,) * 6 + (weight, shared, weight, shared, shared, shared, weight, shared, weight, shared)
    return jax.shard_map(body, mesh=mesh, in_specs=placed, out_specs=outs, check_vma=False)
```

```python
import functools

import jax
import jax.numpy as jnp
import numpy as np
from jax import lax
from jax.experimental import pallas as pl
from jax.experimental.pallas import tpu as pltpu
from jax.sharding import PartitionSpec as P

HEADS = 8
SIDE_SMALL = 14
SIDE_BIG = 20
MEM = 2
EPSILON = 1e-06
SQRT_HALF = 0.7071067811865476
ROOT_TWO_PI = 2.5066282746310002
LOG2E = 1.4426950408889634
FAR = -1e30

GRID = 24
FR = 8
HALF = GRID // 2
VW = SIDE_BIG
VH = VW // 2
LANE = 128
PLANE = (VW + 1) * GRID
FLAT = GRID + (FR + 2) * PLANE
CUR = FR * VW * VW
KEYS_USED = CUR + MEM * FR * VH * VH
KEYS = -(-KEYS_USED // 256) * 256
LATE_COMP, LATE_SMALL, LATE_TABLE, LATE = 17, 33, 35, 40
TABLE_ROWS = 2 * FR + 4 * GRID
TAB = 8 * FR + 2 * GRID * HALF

bf = jnp.bfloat16
f32 = jnp.float32
HI = lax.Precision.HIGHEST
G = ("tm", "height")


def nn(a, b, **kw):
    return lax.dot_general(a, b, (((1,), (0,)), ((), ())), preferred_element_type=f32, **kw)


def nt(a, b, **kw):
    return lax.dot_general(a, b, (((1,), (1,)), ((), ())), preferred_element_type=f32, **kw)


def tn(a, b, **kw):
    return lax.dot_general(a, b, (((0,), (0,)), ((), ())), preferred_element_type=f32, **kw)


def shape(dims, dtype):
    return jax.ShapeDtypeStruct(dims, dtype)


def cost(us):
    return pl.CostEstimate(flops=int(us * 1e9), bytes_accessed=0, transcendentals=0)


def call(kernel, outs, args, scratch=(), smem=1, us=5, far=0):
    specs = [pl.BlockSpec(memory_space=pltpu.SMEM)] * smem
    specs += [pl.BlockSpec(memory_space=pltpu.VMEM)] * (len(args) - smem - far)
    specs += [pl.BlockSpec(memory_space=pl.ANY)] * far
    return pl.pallas_call(
        kernel,
        out_shape=outs,
        in_specs=specs,
        out_specs=jax.tree.map(lambda _: pl.BlockSpec(memory_space=pltpu.VMEM), outs),
        scratch_shapes=list(scratch),
        compiler_params=pltpu.CompilerParams(vmem_limit_bytes=56 << 20),
        cost_estimate=cost(us),
    )(*args)


def row_of(ref, lo, hi):
    return ref[lo:hi].reshape(1, hi - lo)


def pack_rows(value, scratch, groups):
    rows, lanes = value.shape
    scratch[0:rows, :] = pad_lanes(value, LANE)
    parts = [scratch[pl.ds(g, rows // groups, groups), :][:, 0:lanes] for g in range(groups)]
    return jnp.concatenate(parts, axis=1)


def pad_lanes(x, lanes):
    return jnp.concatenate([x, jnp.zeros((x.shape[0], lanes - x.shape[1]), x.dtype)], axis=1)


def layer_unit(x):
    centred = x - jnp.mean(x, axis=-1, keepdims=True)
    inverse = lax.rsqrt(jnp.mean(centred * centred, axis=-1, keepdims=True) + EPSILON)
    return centred * inverse, inverse


def pair_reduce(value, scratch, op):
    rows, lanes = value.shape
    outs = []
    for j in range(lanes // LANE):
        scratch[j, 0:rows, :] = value[:, j * LANE : (j + 1) * LANE]
    for j in range(lanes // LANE):
        outs.append(op(scratch[j, pl.ds(0, rows // 2, 2), :], scratch[j, pl.ds(1, rows // 2, 2), :]))
    return jnp.concatenate(outs, axis=1)


def join_lines(value, op):
    return jnp.concatenate(
        [op(value[a : a + GRID], value[a + GRID : a + 2 * GRID]) for a in range(0, value.shape[0], 2 * GRID)], axis=0
    )


def pair_spread(value, scratch):
    rows, lanes = value.shape
    for j in range(lanes // LANE):
        part = value[:, j * LANE : (j + 1) * LANE]
        scratch[j, pl.ds(0, rows, 2), :] = part
        scratch[j, pl.ds(1, rows, 2), :] = part
    return jnp.concatenate([scratch[j, 0 : 2 * rows, :] for j in range(lanes // LANE)], axis=1)


def norm_kernel(dims, x_ref, g_ref, b_ref, n1_ref, mx_ref, tiles):
    frames, rows = dims
    half = rows // 2
    channels = x_ref.shape[1]
    per = rows * GRID
    g = row_of(g_ref, 0, channels)
    b = row_of(b_ref, 0, channels)
    for t in range(frames):
        x = x_ref[t * per : (t + 1) * per, :].astype(f32)
        unit, _ = layer_unit(x)
        n1_ref[t * per : (t + 1) * per, :] = (unit * g + b).astype(bf)
        tall = join_lines(x, jnp.maximum)
        mx_ref[t * half * HALF : (t + 1) * half * HALF, :] = pair_reduce(tall, tiles, jnp.maximum)


def squeeze_kernel(dims, mem_ref, c_ref, cot_ref, mx_ref, out_ref, early_ref, tiles, squeezed):
    frames, rows, width, hd = dims
    half = rows // 2
    count = half * frames * VH
    odd = lax.broadcasted_iota(jnp.int32, (GRID, 1), 0) % 2 == 1
    for m in range(2):
        taps = [jnp.where(odd, c_ref[m, i, 1:2, :], c_ref[m, i, 0:1, :]) for i in range(2)]
        for s in range(MEM):
            for t in range(frames):
                parts = [
                    mem_ref[s, m, t, 2 * a].astype(f32) * taps[0] + mem_ref[s, m, t, 2 * a + 1].astype(f32) * taps[1]
                    for a in range(half)
                ]
                for a in range(half):
                    done = pair_reduce(parts[a], tiles.at[(t * half + a) % 4], jnp.add)
                    squeezed[m, s, a * frames * VH + t * VH : a * frames * VH + (t + 1) * VH, :] = done[0:VH]
            squeezed[m, s, count:LANE, :] = jnp.zeros((LANE - count, width), f32)
    for n in range(HEADS):
        cut = slice(n * hd, (n + 1) * hd)
        out_ref[n] = jnp.concatenate(
            [squeezed[0, 0, :, cut], squeezed[1, 0, :, cut], squeezed[0, 1, :, cut], squeezed[1, 1, :, cut]], axis=1
        ).astype(bf)
    cot = jnp.concatenate([cot_ref[t, a].astype(f32) for t in range(frames) for a in range(half)], axis=0)
    early_ref[:, 0:width] = cot.astype(bf)
    early_ref[:, width:] = mx_ref[...].astype(bf)


def flat_row(t, h):
    return GRID + (1 + t) * PLANE + h * GRID


def fill_grid(grid):
    zero = jnp.zeros((GRID, LANE), f32)
    grid[0 : GRID + PLANE, :] = jnp.zeros((GRID + PLANE, LANE), f32)
    grid[flat_row(FR, 0) :, :] = jnp.zeros((FLAT - flat_row(FR, 0), LANE), f32)
    for t in range(FR):
        grid[flat_row(t, VW) : flat_row(t, VW) + GRID, :] = zero


def taps9(w_ref, part):
    return [[[w_ref[(a * 3 + b) * 3 + c : (a * 3 + b) * 3 + c + 1, part * LANE : (part + 1) * LANE] for c in range(3)] for b in range(3)] for a in range(3)]


def four_rows(grid, weights, base, flip, keep=VW):
    acc = [[None] * 3 for _ in range(4)]
    for line in range(-1, 5):
        for a in range(3):
            shift = (1 - a if flip else a - 1) * PLANE + line * GRID
            cells = grid[pl.ds(pl.multiple_of(base + shift, 8), GRID), :]
            for h in range(4):
                b = (h - line + 1) if flip else (line - h + 1)
                if b < 0 or b > 2:
                    continue
                for c in range(3):
                    term = cells * weights[a][b][c]
                    acc[h][c] = term if acc[h][c] is None else acc[h][c] + term
    outs = []
    for h in range(4):
        left, mid, right = (acc[h][2], acc[h][1], acc[h][0]) if flip else (acc[h][0], acc[h][1], acc[h][2])
        outs.append((pltpu.roll(left, 1, 0) + mid + pltpu.roll(right, GRID - 1, 0))[0:keep])
    return jnp.concatenate(outs, axis=0)


def gather_blocks(dims, meta, refs, out, sems):
    frames, rows, n_height = dims
    member = meta[4]
    per = rows * GRID
    x0, x2, x4, x6a, x6b, x1, x3, x5, x7a, x7b = refs
    copies = []
    for d, parts in enumerate([[x0], [x1], [x2], [x3], [x4], [x5], [x6a, x6b], [x7a, x7b]]):
        src = member ^ d
        t = lax.div(src, n_height) * frames
        at = pl.ds(pl.multiple_of(lax.rem(src, n_height) * per, 16), per)
        for ref in parts:
            for i in range(ref.shape[0] // per):
                copies.append(pltpu.make_async_copy(ref.at[i * per : (i + 1) * per, :], out.at[t, at, :], sems.at[len(copies)]))
                t = t + 1
    return copies


def conv_kernel(dims, meta, w_ref, qkv_ref, bias_ref, *refs):
    frames, rows, n_height, hd = dims
    half = rows // 2
    blocks, (k_ref, v_ref, q_ref, gk, gv, gather, tiles, qrow, sems) = refs[:10], refs[10:]
    copies = gather_blocks(dims[:3], meta, blocks, gather, sems)
    for copy in copies:
        copy.start()
    side, member = meta[0], meta[4]
    width = qkv_ref.shape[0] // 3
    channels = qkv_ref.shape[1]
    for grid in (gk, gv):
        fill_grid(grid)
    blank = jnp.zeros((LANE - hd, channels), bf)
    own = [qkv_ref[pl.ds(pl.multiple_of(p * width + member * hd, 32), hd), :] for p in range(3)]
    weight_q = jnp.concatenate([own[0], blank], axis=0)
    weight_kv = jnp.concatenate([own[1], blank, own[2], blank], axis=0)
    index = lax.broadcasted_iota(jnp.int32, (VW * GRID, 1), 0)
    line = (index * 2731) >> 16
    inside = ((line < side) & (index - line * GRID < side)).astype(f32)
    for copy in copies:
        copy.wait()
    piece = half * HALF
    for t in range(FR):
        query = pair_reduce(join_lines(nt(gather[t], weight_q), jnp.add), tiles.at[t % 2], jnp.add) * 0.25 + bias_ref[0:1, 0:LANE]
        for h in range(n_height):
            at = (t // frames * n_height + h) * frames * piece + t % frames * piece
            qrow[at : at + piece, :] = query[h * piece : (h + 1) * piece]
        pair = ((nt(gather[t, 0 : VW * GRID, :], weight_kv) + bias_ref[0:1, LANE:]) * inside).astype(bf).astype(f32)
        gk[flat_row(t, 0) : flat_row(t, VW), :] = pair[:, 0:LANE]
        gv[flat_row(t, 0) : flat_row(t, VW), :] = pair[:, LANE:]
    q_ref[...] = qrow[...].astype(bf)
    local = lax.broadcasted_iota(jnp.int32, (4 * VW, LANE), 0)
    lane = lax.broadcasted_iota(jnp.int32, (4 * VW, LANE), 1)
    line = (local * 3277) >> 16
    column = local - line * VW
    fixed = [(lane + o == 143 - column) | (lane + o == 191 - column) for o in (0, LANE)]
    ones = (lane == hd).astype(f32)

    def step(it, carry):
        t = it // (VW // 4)
        quad = it % (VW // 4)
        base = GRID + (1 + t) * PLANE + quad * 4 * GRID
        out = pl.ds(pl.multiple_of(it * (4 * VW), 16), 4 * VW)
        mixed_k = four_rows(gk, taps9(w_ref, 0), base, False)
        mixed_v = four_rows(gv, taps9(w_ref, 1), base, False)
        h = quad * 4 + line
        bad = (h >= side) | (column >= side)
        for o in range(2):
            at = lane + o * LANE
            hit = fixed[o] | (at == 103 - t) | (at == 151 - t) | (at == 123 - h) | (at == 171 - h) | ((at == 192) & bad)
            marks = hit.astype(f32)
            k_ref[out, o * LANE : (o + 1) * LANE] = ((mixed_k + marks) if o == 0 else marks).astype(bf)
        v_ref[out, :] = (mixed_v + ones).astype(bf)
        return carry

    lax.fori_loop(0, FR * VW // 4, step, 0)


def build_table(tab, t_ref, h_ref, w_ref):
    tab[...] = jnp.zeros(tab.shape, f32)
    for v in range(FR):
        tab[8 * v : 8 * v + FR, :] = t_ref[v : v + FR, :]
    for n, ref in ((0, h_ref), (1, w_ref)):
        for a in range(HALF):
            at = 8 * FR + (n * HALF + a) * GRID
            first = 2 * a + GRID - VW
            tab[at : at + VW, :] = ref[first : first + VW, :]


def attend_kernel(dims, meta, kc_ref, vc_ref, q_ref, y_ref, t_ref, h_ref, w_ref, place_ref, k_ref, v_ref, qt_ref, o_ref, l_ref, j_ref, vt, tab):
    frames, rows, n_height, hd = dims
    half = rows // 2
    side, length = meta[0], meta[1]
    queries = q_ref.shape[0]
    scale = hd**-0.5
    k_ref[0:CUR, :] = kc_ref[...]
    v_ref[0:CUR, :] = vc_ref[...]
    count = half * frames * VH
    each = frames * VH
    lane1 = lax.broadcasted_iota(jnp.int32, (1, LANE), 1)
    at = CUR
    for src in range(HEADS):
        packed = y_ref[src].astype(f32)
        first = src % n_height * half
        used = min(max(VH - first, 0), half) * each
        if used > 0:
            halves = []
            for m in range(2):
                halves.append(jnp.concatenate([packed[0:used, m * hd : (m + 1) * hd], packed[0:used, (2 + m) * hd : (3 + m) * hd]], axis=0))
            index = lax.broadcasted_iota(jnp.int32, (2 * used, LANE), 0)
            step = (index >= used).astype(jnp.int32)
            inner = index - step * used
            a = (inner >= each).astype(jnp.int32) + (inner >= 2 * each).astype(jnp.int32)
            inner = inner - a * each
            c = inner - ((inner * 6554) >> 16) * VH
            bad = (step >= length) | (2 * (first + a) >= side) | (2 * c >= side)
            mark = (bad & (lax.broadcasted_iota(jnp.int32, (2 * used, LANE), 1) == 64)).astype(f32)
            k_ref[at : at + 2 * used, 0:LANE] = pad_lanes(halves[0], LANE).astype(bf)
            k_ref[at : at + 2 * used, LANE:] = mark.astype(bf)
            v_ref[at : at + 2 * used, :] = (pad_lanes(halves[1], LANE) + (lane1 == hd).astype(f32)).astype(bf)
            at += 2 * used
    rest = KEYS - at
    k_ref[at:, 0:LANE] = jnp.zeros((rest, LANE), bf)
    k_ref[at:, LANE:] = jnp.broadcast_to((lane1 == 64).astype(f32), (rest, LANE)).astype(bf)
    v_ref[at:, :] = jnp.zeros((rest, LANE), bf)
    for i in range(KEYS // 256):
        cut = slice(i * 256, (i + 1) * 256)
        vt[:, cut] = v_ref[cut, :].T
    pt = q_ref[...].astype(f32).T[0:hd]
    build_table(tab, t_ref, h_ref, w_ref)
    table = tab[...]
    coarse = table.astype(bf)
    turned = pt.astype(bf)
    along = nn(coarse, turned) + nn((table - coarse.astype(f32)).astype(bf), turned)
    tq, aq, cq = place_ref[0:1, :], place_ref[1:2, :], place_ref[2:3, :]
    part_t = jnp.zeros((FR, queries), f32)
    for v in range(FR):
        part_t = jnp.where(tq == v, along[8 * v : 8 * v + FR], part_t)
    parts = []
    for n, place in ((0, aq), (1, cq)):
        part = jnp.zeros((GRID, queries), f32)
        for a in range(HALF):
            row = 8 * FR + (n * HALF + a) * GRID
            part = jnp.where(place == a, along[row : row + GRID], part)
        parts.append(part[0:VW])
    bias = jnp.concatenate([part_t] + parts, axis=0) * hd**0.5
    high = bias.astype(bf)
    low = (bias - high.astype(f32)).astype(bf)
    qt_ref[0:hd, :] = pt.astype(bf)
    qt_ref[hd : hd + 48, :] = high
    qt_ref[hd + 48 : hd + 96, :] = low
    tail = lax.broadcasted_iota(jnp.int32, (64, queries), 0)
    qt_ref[192:256, :] = jnp.where(tail == 0, FAR, 0.0).astype(bf)
    factor = scale * LOG2E
    query = qt_ref[...]
    top = None
    for lo in range(0, KEYS, 1024):
        cut = slice(lo, min(lo + 1024, KEYS))
        scores = nn(k_ref[cut, :], query)
        here = jnp.max(scores.reshape(scores.shape[0] // 8, 8, queries), axis=0)
        here = jnp.max(here, axis=0, keepdims=True) * factor
        new = here if top is None else jnp.maximum(top, here)
        part = nn(vt[:, cut], jnp.exp2(scores * factor - new).astype(bf))
        total = part if top is None else total * jnp.exp2(top - new) + part
        top = new
    norm = total[hd : hd + 1]
    o_ref[...] = total[0:hd] / norm
    l_ref[...] = top + jnp.log2(norm)
    j_ref[...] = pad_lanes((o_ref[...] + pt).T, LANE).astype(bf)


def turn_kernel(k_ref, kt_ref):
    for i in range(KEYS // 256):
        cut = slice(i * 256, (i + 1) * 256)
        kt_ref[:, cut] = k_ref[cut, :].T


def mlp_kernel(dims, j_ref, early_ref, wp_ref, ws_ref, bp_ref, bs_ref, g_ref, b_ref, w1_ref, b1_ref, w2_ref, b2_ref,
               out_ref, keep_ref, act_ref, dj_ref, mg_ref,
               resid, n2, acc, ngrad, joined, gb1):
    width, hd = dims
    i = pl.program_id(0)
    per_q = early_ref.shape[0]
    block = w1_ref.shape[0]

    @pl.when(i == 0)
    def _():
        joined[...] = jnp.concatenate([j_ref[n][:, 0:hd] for n in range(HEADS)], axis=1)
        shift = row_of(bp_ref, 0, width) + row_of(bs_ref, 0, width)
        value = nt(joined[...], wp_ref[...]) + nt(early_ref[:, width:], ws_ref[...]) + shift
        resid[...] = value
        unit, _ = layer_unit(value)
        n2[...] = (unit * row_of(g_ref, 0, width) + row_of(b_ref, 0, width)).astype(bf)
        acc[...] = jnp.zeros(acc.shape, f32)
        ngrad[...] = jnp.zeros(ngrad.shape, f32)

    here = pl.ds(pl.multiple_of(i * block, LANE), block)
    hidden = nt(n2[...], w1_ref[...]) + b1_ref[here].reshape(1, block)
    gate = 0.5 * (1.0 + lax.erf(hidden * SQRT_HALF))
    act = (hidden * gate).astype(bf)
    act_ref[0, 0:per_q, :] = act
    acc[...] += nt(act, w2_ref[...])
    grad = nn(early_ref[:, 0:width], w2_ref[...])
    hgrad = (grad * (gate + hidden * jnp.exp(-0.5 * hidden * hidden) / ROOT_TWO_PI)).astype(bf)
    act_ref[0, per_q:, :] = hgrad
    gb1[:, here] = jnp.sum(hgrad.astype(f32), axis=0, keepdims=True)
    ngrad[...] += nn(hgrad, w1_ref[...])

    @pl.when(i == pl.num_programs(0) - 1)
    def _():
        value = resid[...]
        result = value + acc[...] + row_of(b2_ref, 0, width)
        for t in range(out_ref.shape[0]):
            for a in range(out_ref.shape[1]):
                at = (t * out_ref.shape[1] + a) * HALF
                out_ref[t, a] = result[at : at + HALF].astype(bf)
        unit, inverse = layer_unit(value)
        cot = early_ref[:, 0:width].astype(f32)
        grad = ngrad[...]
        scaled = grad * row_of(g_ref, 0, width)
        back = inverse * (
            scaled - jnp.mean(scaled, axis=-1, keepdims=True) - unit * jnp.mean(scaled * unit, axis=-1, keepdims=True)
        )
        low = (cot + back).astype(bf)
        keep_ref[:, 0:width] = n2[...]
        keep_ref[:, width:] = low
        joined_grad = nn(low, wp_ref[...])
        mg_ref[...] = nn(low, ws_ref[...])
        sums = [jnp.sum(v, axis=0, keepdims=True) for v in (low.astype(f32), grad * unit, grad, cot)] + [gb1[...]]
        flat = [v[:, k : k + width] for v in sums for k in range(0, v.shape[1], width)]
        spare = LANE - hd
        for n in range(HEADS):
            exact = jnp.concatenate([flat[n][:, k : k + spare] for k in range(0, width, spare)], axis=0)
            high = exact.astype(bf).astype(f32)
            side = jnp.concatenate([high, exact - high, jnp.zeros((per_q - 2 * exact.shape[0], spare), f32)], axis=0)
            dj_ref[n] = jnp.concatenate([joined_grad[:, n * hd : (n + 1) * hd], side], axis=1).astype(bf)


def attend_back_kernel(dims, k_ref, kt_ref, v_ref, qt_ref, q_ref, o_ref, l_ref, dj_ref, t_ref, h_ref, w_ref, place_ref,
                       dk_ref, dv_ref, mem_ref, pq_ref, small_ref,
                       dot_ref, dq, tab, dtab, dks, dvs, delta, tables):
    frames, rows, n_height, hd = dims
    half = rows // 2
    queries = q_ref.shape[0]
    scale = hd**-0.5
    factor = scale * LOG2E
    turned = dj_ref[...].astype(f32).T
    per_q = queries // HEADS
    spare = jnp.zeros((per_q, LANE - hd), f32)
    for src in range(HEADS):
        spare = spare + dj_ref[src * per_q : (src + 1) * per_q, hd:].astype(f32)
    lines = small_ref.shape[0]
    small_ref[...] = spare[0:lines] + spare[lines : 2 * lines]
    dot_ref[0:hd, :] = turned[0:hd].astype(bf)
    dot_ref[hd:, :] = jnp.zeros((LANE - hd, queries), bf)
    delta[...] = jnp.sum(turned[0:hd] * o_ref[...], axis=0, keepdims=True)
    dq[...] = jnp.zeros(dq.shape, f32)
    half_keys = KEYS // 2

    def chunk(i, carry):
        cut = pl.ds(pl.multiple_of(i * half_keys, LANE), half_keys)
        shares = jnp.exp2(nn(k_ref[cut, :], qt_ref[...]) * factor - l_ref[...])
        slope = nn(v_ref[cut, :], dot_ref[...])
        score = (shares * (slope - delta[...])).astype(bf)
        dvs[cut, :] = nn(shares.astype(bf), dj_ref[...])
        dks[cut, :] = nn(score, q_ref[...]) * scale
        dq[...] += nn(kt_ref[0 : dq.shape[0], cut], score)
        return carry

    lax.fori_loop(0, 2, chunk, 0)
    dk_ref[...] = dks[0:CUR, :]
    dv_ref[...] = dvs[0:CUR, :]
    each = frames * VH
    at = CUR
    for dst in range(HEADS):
        first = dst % n_height * half
        used = min(max(VH - first, 0), half) * each
        if used > 0:
            parts = [ref[at + s * used : at + (s + 1) * used, 0:hd] for s in range(MEM) for ref in (dks, dvs)]
            packed = jnp.concatenate(parts, axis=1)
            at += 2 * used
        if used < LANE:
            zero = jnp.zeros((LANE - used, 4 * hd), f32)
            packed = jnp.concatenate([packed, zero], axis=0) if used > 0 else zero
        mem_ref[dst, 0:LANE, :] = packed.astype(bf)
    build_table(tab, t_ref, h_ref, w_ref)
    tq, aq, cq = place_ref[0:1, :], place_ref[1:2, :], place_ref[2:3, :]
    grad_t = dq[hd : hd + FR, :]
    for v in range(FR):
        dtab[8 * v : 8 * v + FR, :] = jnp.where(tq == v, grad_t, 0.0)
    for n, place in ((0, aq), (1, cq)):
        part = jnp.concatenate(
            [dq[hd + FR + n * VW : hd + FR + (n + 1) * VW, :], jnp.zeros((GRID - VW, queries), f32)], axis=0
        )
        for a in range(HALF):
            row = 8 * FR + (n * HALF + a) * GRID
            dtab[row : row + GRID, :] = jnp.where(place == a, part, 0.0)
    spread = dtab[...].astype(bf)
    pooled_grad = dq[0:hd, :] * scale + tn(tab[...].astype(bf), spread) + dot_ref[0:hd, :].astype(f32)
    pq_ref[...] = pad_lanes(pooled_grad.T * 0.25, LANE)
    grads = nn(spread, q_ref[...])
    tables[...] = jnp.zeros(tables.shape, f32)
    for v in range(FR):
        tables[v : v + FR, :] += grads[8 * v : 8 * v + FR]
    for n in range(2):
        for a in range(HALF):
            row = 8 * FR + (n * HALF + a) * GRID
            first = 2 * FR + n * 2 * GRID + 2 * a + GRID - VW
            tables[first : first + VW, :] += grads[row : row + VW]
    share = TABLE_ROWS // HEADS
    for dst in range(HEADS):
        part = jnp.concatenate([tables[dst * share : (dst + 1) * share, :], jnp.zeros((16 - share, LANE), f32)], axis=0)
        high = part.astype(bf).astype(f32)
        mem_ref[dst, LANE:, :] = jnp.concatenate([high, part - high, jnp.zeros((16, LANE), f32)], axis=1).astype(bf)


def conv_back_kernel(dims, meta, dk_ref, dv_ref, pq_ref, w_ref, g_ref, b_ref, qkv_ref, *refs):
    frames, rows, n_height, hd = dims
    half = rows // 2
    blocks, (out_ref, stat_ref, pg, gk, gv, wide, gather, tall, sems) = refs[:10], refs[10:]
    copies = gather_blocks(dims[:3], meta, blocks, gather, sems)
    for copy in copies:
        copy.start()
    side, member = meta[0], meta[4]
    width = qkv_ref.shape[0] // 3
    channels = qkv_ref.shape[1]
    for grid in (gk, gv):
        fill_grid(grid)
    for ref, grid in ((dk_ref, gk), (dv_ref, gv)):
        for t in range(FR):
            for h in range(VW):
                at = (t * VW + h) * VW
                grid[flat_row(t, h) : flat_row(t, h) + GRID, :] = jnp.concatenate(
                    [ref[at : at + VW, :], jnp.zeros((GRID - VW, LANE), f32)], axis=0
                )
    local = lax.broadcasted_iota(jnp.int32, (4 * GRID, 1), 0)
    line = (local * 2731) >> 16
    column = local - line * GRID
    empty = jnp.zeros(((GRID - VW) * GRID, 2 * LANE), bf)
    for t in range(FR):
        pg[t * GRID * GRID + VW * GRID : (t + 1) * GRID * GRID, LANE:] = empty

    def step(it, carry):
        t = it // (VW // 4)
        quad = it % (VW // 4)
        base = GRID + (1 + t) * PLANE + quad * 4 * GRID
        out = pl.ds(pl.multiple_of((t * GRID + quad * 4) * GRID, 32), 4 * GRID)
        inside = ((quad * 4 + line < side) & (column < side)).astype(f32)
        for m, grid in ((0, gk), (1, gv)):
            back = four_rows(grid, taps9(w_ref, m), base, True, GRID)
            pg[out, (1 + m) * LANE : (2 + m) * LANE] = (back * inside).astype(bf)
        return carry

    lax.fori_loop(0, FR * VW // 4, step, 0)
    queries = pq_ref.shape[0]
    wide[pl.ds(0, queries, 2), :] = pq_ref[...]
    wide[pl.ds(1, queries, 2), :] = pq_ref[...]
    per_q = queries // HEADS
    for src in range(HEADS):
        for t in range(frames):
            for a in range(half):
                at = ((src * frames + t) * half + a) * GRID
                lines = wide[at : at + GRID, :]
                row = ((src // n_height * frames + t) * GRID + src % n_height * rows + 2 * a) * GRID
                pg[row : row + 2 * GRID, 0:LANE] = jnp.concatenate([lines, lines], axis=0).astype(bf)
    span = rows * VW
    cells = span * (frames // 2)
    third = per_q // 3
    for dst in range(HEADS):
        first = dst % n_height * rows
        lines = []
        for t2 in range(frames // 2):
            parts = []
            for g in range(2):
                t = dst // n_height * frames + g * (frames // 2) + t2
                at = (t * GRID + first) * GRID
                block = pg[at : at + rows * GRID, LANE:].astype(f32)
                block = jnp.concatenate([block[h * GRID : h * GRID + VW] for h in range(rows)], axis=0)
                parts += [block[:, 0:hd], block[:, LANE : LANE + hd]]
            lines.append(jnp.concatenate(parts, axis=1))
        out_ref[dst, 0:cells, :] = jnp.concatenate(lines, axis=0).astype(bf)
        out_ref[dst, cells : cells + third, :] = jnp.concatenate(
            [pq_ref[dst * per_q + i * third : dst * per_q + (i + 1) * third, :] for i in range(3)], axis=1
        ).astype(bf)
    for copy in copies:
        copy.wait()
    total = jnp.zeros((3 * LANE, channels), f32)
    sums = jnp.zeros((1, 3 * LANE), f32)
    for t in range(FR):
        part = pg[t * GRID * GRID : (t + 1) * GRID * GRID, :]
        total = total + tn(part, gather[t])
        sums = sums + jnp.sum(part.astype(f32), axis=0, keepdims=True)
    total = jnp.concatenate([total[p * LANE : p * LANE + hd] for p in range(3)], axis=0)
    sums = jnp.concatenate([sums[:, p * LANE : p * LANE + hd] for p in range(3)], axis=1)
    cols = channels // HEADS
    packed = 3 * hd // HEADS
    rest = out_ref.shape[1] - cells - third
    for n in range(HEADS):
        value = pack_rows(total[:, n * cols : (n + 1) * cols], tall.at[n % 2], HEADS)
        out_ref[n, cells + third :, :] = jnp.concatenate([value, jnp.zeros((rest - packed, channels), f32)], axis=0).astype(bf)
    weight = jnp.concatenate(
        [qkv_ref[pl.ds(pl.multiple_of(p * width + member * hd, 32), hd), :].astype(f32) for p in range(3)], axis=0
    )
    shift = nn(jnp.broadcast_to(sums, (8, 3 * hd)), weight, precision=HI)[0:1]
    gain = jnp.sum(total * weight, axis=0, keepdims=True)
    gain = (gain - shift * row_of(b_ref, 0, channels)) / row_of(g_ref, 0, channels)
    stat_ref[0:1, :] = pad_lanes(sums, channels)
    stat_ref[1:2, :] = gain
    stat_ref[2:3, :] = shift
    stat_ref[3:8, :] = jnp.zeros((5, channels), f32)


def gather_rows(meta, refs, out, sems):
    x0, x2, x4, x6a, x6b, x1, x3, x5, x7a, x7b = refs
    copies = []
    for d, parts in enumerate([[x0], [x1], [x2], [x3], [x4], [x5], [x6a, x6b], [x7a, x7b]]):
        at = (meta[4] ^ d) * (out.shape[0] // HEADS)
        for ref in parts:
            size = ref.shape[0]
            copies.append(pltpu.make_async_copy(ref, out.at[pl.ds(pl.multiple_of(at, 16), size), :], sems.at[len(copies)]))
            at = at + size
    return copies


def weight_grad_kernel(dims, meta, ah_ref, j_ref, dmem_ref, *refs):
    width, hd, channels, per_q = dims
    early, kept = refs[:10], refs[10:20]
    fc2_ref, fc1_ref, proj_ref, short_ref, act, hgrad, tall, parts, cot_ref, keep_ref, sems = refs[20:]
    member = meta[4]
    first = gather_rows(meta, early, cot_ref, sems.at[0])
    second = gather_rows(meta, kept, keep_ref, sems.at[1])
    for copy in first + second:
        copy.start()
    for src in range(HEADS):
        cut = slice(src * per_q, (src + 1) * per_q)
        act[cut, :] = ah_ref[src, 0:per_q, :]
        hgrad[cut, :] = ah_ref[src, per_q:, :]
    for copy in first:
        copy.wait()
    fc2_ref[...] = tn(cot_ref[:, 0:width], act[...]).astype(bf)
    for copy in second:
        copy.wait()
    normed = keep_ref[:, 0:width]
    resid = keep_ref[:, width : 2 * width]
    fc1 = tn(hgrad[...], normed)
    for n in range(HEADS):
        fc1_ref[n, 0 : dmem_ref.shape[1], :] = dmem_ref[n]
        fc1_ref[n, dmem_ref.shape[1] :, :] = pack_rows(fc1[:, n * hd : (n + 1) * hd], parts.at[n % 2], channels // hd).astype(bf)
    cols = channels // HEADS
    lane = lax.broadcasted_iota(jnp.int32, (channels, LANE), 1)
    pick = (lax.broadcasted_iota(jnp.int32, (channels, LANE), 0) == lane + member * cols) & (lane < cols)
    maxima = nn(cot_ref[:, width:], pick.astype(f32).astype(bf)).astype(bf)
    both = tn(resid, jnp.concatenate([j_ref[...], maxima], axis=1))
    proj_ref[...] = pack_rows(both[:, 0:hd], tall.at[0], channels // hd).astype(bf)
    short_ref[...] = pack_rows(both[:, LANE : LANE + cols], tall.at[1], channels // cols).astype(bf)


def last_kernel(dims, x_ref, g_ref, w_ref, pg_ref, mx_ref, mg_ref, out_ref, full, tiles):
    frames, rows, width, hd = dims
    half = rows // 2
    cells = rows * VW * (frames // 2)
    third = frames * half * HALF // 3
    channels = x_ref.shape[1]
    tops = jnp.zeros((cells, channels), f32)
    lows = jnp.zeros((cells, channels), f32)
    queries = []
    for n in range(HEADS):
        weight = jnp.concatenate(
            [w_ref[width + n * hd : width + (n + 1) * hd, :], w_ref[2 * width + n * hd : 2 * width + (n + 1) * hd, :]], axis=0
        )
        packed = pg_ref[n]
        tops = tops + nn(packed[0:cells, 0 : 2 * hd], weight)
        lows = lows + nn(packed[0:cells, 2 * hd :], weight)
        queries.append(
            jnp.concatenate([packed[cells : cells + third, i * LANE : i * LANE + hd] for i in range(3)], axis=0)
        )
    for part, value in ((0, tops), (1, lows)):
        for line in range(frames // 2 * rows):
            at = (part * (frames // 2) * rows + line) * GRID
            full[at : at + GRID, :] = jnp.concatenate(
                [value[line * VW : (line + 1) * VW], jnp.zeros((GRID - VW, channels), f32)], axis=0
            )
    query = nn(jnp.concatenate(queries, axis=1), w_ref[0:width, :])
    per = rows * GRID
    per_q = half * HALF
    g = row_of(g_ref, 0, channels)
    for t in range(frames):
        cut = slice(t * per_q, (t + 1) * per_q)
        x = x_ref[t * per : (t + 1) * per, :].astype(f32)

        def spread(value):
            wide = pair_spread(value, tiles)
            lines = []
            for a in range(half):
                lines += [wide[a * GRID : (a + 1) * GRID]] * 2
            return jnp.concatenate(lines, axis=0)

        grad = full[t * per : (t + 1) * per, :] + spread(query[cut])
        hits = (x == spread(mx_ref[cut, :])).astype(f32)
        sums = jnp.concatenate(
            [hits[2 * a * GRID : (2 * a + 1) * GRID] + hits[(2 * a + 1) * GRID : (2 * a + 2) * GRID] for a in range(half)], axis=0
        )
        number = pair_reduce(sums, tiles, jnp.add)
        pool = hits * spread(mg_ref[cut, :] / number)
        unit, inverse = layer_unit(x)
        scaled = grad * g
        back = inverse * (
            scaled - jnp.mean(scaled, axis=-1, keepdims=True) - unit * jnp.mean(scaled * unit, axis=-1, keepdims=True)
        )
        out_ref[t * per : (t + 1) * per, :] = (back + pool).astype(bf)


def conv_grad_kernel(hd, mk, mv, dk_ref, dv_ref, out_ref, acc):
    acc[...] = jnp.zeros(acc.shape, f32)
    blank = jnp.zeros((GRID - VW, LANE), f32)

    def step(it, carry):
        t = it // (VW // 4)
        base = GRID + (1 + t) * PLANE + it % (VW // 4) * 4 * GRID
        for m, ref, masked in ((0, dk_ref, mk), (1, dv_ref, mv)):
            quad = ref[pl.ds(pl.multiple_of(it * (4 * VW), 16), 4 * VW), :]
            for h in range(4):
                here = jnp.concatenate([quad[h * VW : (h + 1) * VW], blank], axis=0)
                turned = [pltpu.roll(here, GRID - 1, 0), here, pltpu.roll(here, 1, 0)]
                for a in range(3):
                    for b in range(3):
                        cells = masked[pl.ds(pl.multiple_of(base + (a - 1) * PLANE + (h + b - 1) * GRID, 8), GRID), :]
                        for c in range(3):
                            prod = cells * turned[c]
                            acc[m * 27 + (a * 3 + b) * 3 + c] += prod[0:8] + prod[8:16] + prod[16:24]
        return carry

    lax.fori_loop(0, FR * VW // 4, step, 0)
    sums = [jnp.sum(acc[tap], axis=0, keepdims=True) for tap in range(54)] + [jnp.zeros((1, LANE), f32)] * 2
    sums = jnp.concatenate(sums, axis=0)
    out_ref[0:14, :] = jnp.concatenate([sums[14 * g : 14 * (g + 1), 0:hd] for g in range(4)], axis=1)
    out_ref[14:16, :] = jnp.zeros((2, 4 * hd), f32)


def late_kernel(dims, mem_ref, p_ref, conv_ref, stat_ref, small_ref, late_ref, tiles, lines):
    frames, rows, width, hd = dims
    half = rows // 2
    channels = late_ref.shape[1]
    for m in range(2):
        sums = [jnp.zeros((GRID, width), f32) for _ in range(2)]
        for s in range(MEM):
            grads = jnp.concatenate(
                [p_ref[n][0:LANE, (2 * s + m) * hd : (2 * s + m + 1) * hd] for n in range(HEADS)], axis=1
            ).astype(f32)
            for t in range(frames):
                for a in range(half):
                    at = (a * frames + t) * VH
                    some = jnp.concatenate([grads[at : at + VH], jnp.zeros((HALF - VH, width), f32)], axis=0)
                    wide = pair_spread(some, tiles.at[(t * half + a) % 4])
                    for i in range(2):
                        sums[i] = sums[i] + mem_ref[s, m, t, 2 * a + i].astype(f32) * wide
        odd = (lax.broadcasted_iota(jnp.int32, (GRID, 1), 0) % 2 == 1).astype(f32)
        for i in range(2):
            for j, keep in ((0, 1.0 - odd), (1, odd)):
                done = jnp.sum(sums[i] * keep, axis=0, keepdims=True)
                for k in range(width // channels):
                    at = LATE_COMP + 8 * k + 4 * m + 2 * i + j
                    lines[at : at + 1, :] = done[:, k * channels : (k + 1) * channels]
    lines[0:14, :] = conv_ref[0:14, :]
    lines[14:17, :] = stat_ref[0:3, :]
    count = small_ref.shape[0] // 2
    for k in range(2):
        lines[LATE_SMALL + k : LATE_SMALL + k + 1, :] = jnp.concatenate(
            [small_ref[k * count + i : k * count + i + 1, :] for i in range(count)], axis=1
        )
    tables = jnp.zeros((16, LANE), f32)
    for n in range(HEADS):
        part = p_ref[n][LANE : LANE + 16, :].astype(f32)
        tables = tables + part[:, 0:LANE] + part[:, LANE : 2 * LANE]
    lines[LATE_TABLE : LATE_TABLE + 5, :] = jnp.concatenate([tables[5 * g : 5 * (g + 1), :] for g in range(3)], axis=1)
    late_ref[...] = lines[...].astype(bf)


def sums_kernel(dims, late_ref, g1_ref, b1_ref, bqkv_ref, conv_ref, comp_ref, t_ref, h_ref, w_ref, bp_ref, bs_ref, g2_ref, b2_ref, bf1_ref, bf2_ref, lines):
    width, hd, channels = dims
    parts = []
    for n in range(HEADS):
        parts.append(late_ref[n])
    total = parts[0]
    for n in range(1, HEADS):
        total = total + parts[n]
    for g in range(4):
        conv = jnp.concatenate([parts[n][0:14, g * hd : (g + 1) * hd] for n in range(HEADS)], axis=1)
        for r in range(14):
            i = 14 * g + r
            if i < 54:
                conv_ref[i % 27 // 9, i % 9 // 3, i % 3, i // 27 : i // 27 + 1, :] = conv[r : r + 1]
    for p in range(3):
        value = jnp.concatenate([parts[n][14:15, p * hd : (p + 1) * hd] for n in range(HEADS)], axis=1)
        bqkv_ref[p * width : (p + 1) * width] = value.reshape(width)
    g1_ref[...] = total[15:16].reshape(channels)
    b1_ref[...] = total[16:17].reshape(channels)
    for i in range(8):
        value = jnp.concatenate([total[LATE_COMP + 8 * k + i : LATE_COMP + 8 * k + i + 1] for k in range(2)], axis=1)
        comp_ref[i // 4, i % 4 // 2, i % 2 : i % 2 + 1, :] = value
    for n in range(HEADS):
        value = jnp.concatenate([parts[n][LATE_SMALL + k : LATE_SMALL + k + 1] for k in range(2)], axis=1).reshape(width)
        if n == 0:
            bp_ref[...] = value
            bs_ref[...] = value
        elif n < 4:
            (g2_ref, b2_ref, bf2_ref)[n - 1][...] = value
        else:
            bf1_ref[(n - 4) * width : (n - 3) * width] = value
    share = TABLE_ROWS // HEADS
    for n in range(HEADS):
        part = parts[n][LATE_TABLE : LATE_TABLE + 5]
        value = jnp.concatenate([part[:, g * LANE : (g + 1) * LANE] for g in range(3)], axis=0)
        lines[n * share : (n + 1) * share, :] = value[0:share]
    at = 0
    for ref, step in ((t_ref, 2 * FR), (h_ref, 2 * GRID), (w_ref, 2 * GRID)):
        ref[...] = lines[at : at + ref.shape[0], 0:hd]
        at += step


def body(clip_input, memory, mem_len, res_id, norm1_gain, norm1_bias, w_qkv, b_qkv, conv_kv, compress, rel_t, rel_h, rel_w,
         w_proj, b_proj, w_short, b_short, norm2_gain, norm2_bias, w_fc1, b_fc1, w_fc2, b_fc2, cotangent):
    _, frames, rows, grid, channels = clip_input.shape
    width = w_proj.shape[0]
    mlp = w_fc1.shape[0]
    hd = width // HEADS
    half = rows // 2
    n_clip = lax.axis_size("clip")
    n_height = lax.axis_size("height")
    tm, height = lax.axis_index("tm"), lax.axis_index("height")
    member = tm * n_height + height
    side = SIDE_SMALL + (SIDE_BIG - SIDE_SMALL) * res_id[0]
    meta = jnp.stack([side, mem_len[0], tm, height, member]).astype(jnp.int32)
    cells_all = frames * rows * GRID
    valid = frames * rows * VW
    per_q = frames * half * HALF
    third = per_q // 3
    queries = HEADS * per_q
    x = clip_input.reshape(cells_all, channels)
    mem = memory[0]

    dims = (frames, rows, width, hd)
    n1, mx = call(
        functools.partial(norm_kernel, (frames, rows)),
        (shape((cells_all, channels), bf), shape((per_q, channels), f32)),
        (x, norm1_gain, norm1_bias),
        scratch=[pltpu.VMEM((channels // LANE, rows * GRID, LANE), f32)],
        smem=0,
        us=3,
    )

    def swap(value, bit):
        if bit == 4:
            return lax.ppermute(value, "tm", [(i, i ^ 1) for i in range(lax.axis_size("tm"))])
        return lax.ppermute(value, "height", [(i, i ^ bit) for i in range(n_height)])

    def near(value):
        return swap(value, 2), swap(value, 4), swap(value, 1)

    def across(x2, x4, cut):
        return swap(x2[:cut], 4), swap(x4[cut:], 2), swap(x2, 1), swap(x4, 1)

    def last(x6a, x6b):
        return swap(x6a, 1), swap(x6b, 1)

    x2, x4, x1 = near(n1)
    pay2, early = call(
        functools.partial(squeeze_kernel, dims),
        (shape((HEADS, LANE, 4 * hd), bf), shape((per_q, width + channels), bf)),
        (mem, compress, cotangent[0], mx),
        scratch=[pltpu.VMEM((4, width // LANE, GRID, LANE), f32), pltpu.VMEM((2, MEM, LANE, width), f32)],
        smem=0,
        us=5,
    )
    x2, x4, pay2 = lax.optimization_barrier((x2, x4, pay2))
    x6a, x6b, x3, x5 = across(x2, x4, cells_all // 2)
    x7a, x7b = last(x6a, x6b)
    y2 = lax.all_to_all(pay2, G, 0, 0, tiled=True)
    early, x7a = lax.optimization_barrier((early, x7a))
    e2, e4, e1 = near(early)
    cut = -(-per_q // 32) * 16
    taps = lax.dynamic_slice_in_dim(conv_kv.reshape(2, 27, width), member * hd, hd, 2)
    taps = jnp.pad(taps, ((0, 0), (0, 5), (0, LANE - hd)))
    taps = jnp.concatenate([taps[0], taps[1]], axis=1)
    hdims = (frames, rows, n_height, hd)
    bias = lax.dynamic_slice_in_dim(b_qkv.reshape(3, width), member * hd, hd, 1)
    bias = jnp.pad(bias, ((0, 0), (0, LANE - hd))).reshape(1, 3 * LANE)
    vmem = pl.BlockSpec(memory_space=pltpu.VMEM)
    blocks = (n1, x2, x4, x6a, x6b, x1, x3, x5, x7a, x7b)
    kc, vc, q_all, mk, mv = pl.pallas_call(
        functools.partial(conv_kernel, hdims),
        out_shape=(
            shape((CUR, 2 * LANE), bf),
            shape((CUR, LANE), bf),
            shape((queries, LANE), bf),
            shape((FLAT, LANE), f32),
            shape((FLAT, LANE), f32),
        ),
        in_specs=[pl.BlockSpec(memory_space=pltpu.SMEM)] + [vmem] * 3 + [pl.BlockSpec(memory_space=pl.ANY)] * 10,
        out_specs=(vmem,) * 5,
        scratch_shapes=[
            pltpu.VMEM((FR, GRID * GRID, channels), bf),
            pltpu.VMEM((2, 1, GRID * HALF, LANE), f32),
            pltpu.VMEM((queries, LANE), f32),
            pltpu.SemaphoreType.DMA((HEADS * frames,)),
        ],
        compiler_params=pltpu.CompilerParams(vmem_limit_bytes=56 << 20),
        cost_estimate=cost(18),
    )(meta, taps, w_qkv, bias, *blocks)
    index = np.arange(queries)
    src, local = index // per_q, index % per_q
    place = np.zeros((8, queries), np.int32)
    place[0] = src // n_height * frames + local // (half * HALF)
    place[1] = src % n_height * half + local // HALF % half
    place[2] = local % HALF
    place = jnp.asarray(place)
    wide = 384
    kc, e2, e4, e1 = lax.optimization_barrier((kc, e2, e4, e1))
    e6a, e6b, e3, e5 = across(e2, e4, cut)
    k_all, v_all, qt_all, o_all, l_all, joined = call(
        functools.partial(attend_kernel, hdims),
        (
            shape((KEYS, 2 * LANE), bf),
            shape((KEYS, LANE), bf),
            shape((2 * LANE, queries), bf),
            shape((hd, queries), f32),
            shape((1, queries), f32),
            shape((queries, LANE), bf),
        ),
        (meta, kc, vc, q_all, y2, rel_t, rel_h, rel_w, place),
        scratch=[
            pltpu.VMEM((LANE, KEYS), bf),
            pltpu.VMEM((TAB, hd), f32),
        ],
        us=16,
    )
    joined_rows = lax.all_to_all(joined.reshape(HEADS, per_q, LANE), G, 0, 0, tiled=True)
    kt_all = call(turn_kernel, shape((2 * LANE, KEYS), bf), (k_all,), smem=0, us=4)
    joined_rows, kt_all, e6a, e6b, e3, e5 = lax.optimization_barrier((joined_rows, kt_all, e6a, e6b, e3, e5))
    e7a, e7b = last(e6a, e6b)
    block = mlp // HEADS
    whole = lambda *dims: pl.BlockSpec(dims, lambda i: (0,) * len(dims))
    keep_width = 2 * width
    output, keep, acthg, dj, max_grad = pl.pallas_call(
        functools.partial(mlp_kernel, (width, hd)),
        grid=(HEADS,),
        out_shape=(
            shape((frames, half, HALF, width), bf),
            shape((per_q, keep_width), bf),
            shape((HEADS, 2 * per_q, block), bf),
            shape((HEADS, per_q, LANE), bf),
            shape((per_q, channels), f32),
        ),
        in_specs=[
            whole(HEADS, per_q, LANE),
            whole(per_q, width + channels),
            whole(width, width),
            whole(width, channels),
            whole(width),
            whole(width),
            whole(width),
            whole(width),
            pl.BlockSpec((block, width), lambda i: (i, 0)),
            whole(mlp),
            pl.BlockSpec((width, block), lambda i: (0, i)),
            whole(width),
        ],
        out_specs=(
            whole(frames, half, HALF, width),
            whole(per_q, keep_width),
            pl.BlockSpec((1, 2 * per_q, block), lambda i: (i, 0, 0)),
            whole(HEADS, per_q, LANE),
            whole(per_q, channels),
        ),
        scratch_shapes=[
            pltpu.VMEM((per_q, width), f32),
            pltpu.VMEM((per_q, width), bf),
            pltpu.VMEM((per_q, width), f32),
            pltpu.VMEM((per_q, width), f32),
            pltpu.VMEM((per_q, width), bf),
            pltpu.VMEM((1, mlp), f32),
        ],
        compiler_params=pltpu.CompilerParams(vmem_limit_bytes=56 << 20),
        cost_estimate=cost(14),
    )(joined_rows, early, w_proj, w_short, b_proj, b_short, norm2_gain, norm2_bias, w_fc1, b_fc1, w_fc2, b_fc2)
    dj_head = lax.all_to_all(dj, G, 0, 0, tiled=True).reshape(queries, LANE)
    k2, k4, k1 = near(keep)
    acthg, dj_head, e7a, e7b = lax.optimization_barrier((acthg, dj_head, e7a, e7b))
    ah_head = lax.all_to_all(acthg, G, 0, 0, tiled=True)

    dk, dv, dmem, pq, small2 = call(
        functools.partial(attend_back_kernel, hdims),
        (
            shape((CUR, LANE), f32),
            shape((CUR, LANE), f32),
            shape((HEADS, LANE + 16, 4 * hd), bf),
            shape((queries, LANE), f32),
            shape((width // (LANE - hd), LANE - hd), f32),
        ),
        (k_all, kt_all, v_all, qt_all, q_all, o_all, l_all, dj_head, rel_t, rel_h, rel_w, place),
        scratch=[
            pltpu.VMEM((LANE, queries), bf),
            pltpu.VMEM((hd + 48, queries), f32),
            pltpu.VMEM((TAB, hd), f32),
            pltpu.VMEM((TAB, queries), f32),
            pltpu.VMEM((KEYS, LANE), f32),
            pltpu.VMEM((KEYS, LANE), f32),
            pltpu.VMEM((1, queries), f32),
            pltpu.VMEM((TABLE_ROWS, LANE), f32),
        ],
        smem=0,
        us=25,
    )
    cols = channels // HEADS
    taken = dmem.shape[1]
    mk, k2, k4, k1 = lax.optimization_barrier((mk, k2, k4, k1))
    k6a, k6b, k3, k5 = across(k2, k4, cut)
    k7a, k7b = last(k6a, k6b)
    gconv = call(
        functools.partial(conv_grad_kernel, hd),
        shape((16, 4 * hd), f32),
        (mk, mv, dk, dv),
        scratch=[pltpu.VMEM((54, 8, LANE), f32)],
        smem=0,
        us=12,
    )
    dmem, gconv = lax.optimization_barrier((dmem, gconv))
    outs = (
        shape((width, block), bf),
        shape((HEADS, taken + block * hd // channels, channels), bf),
        shape((width * hd // channels, channels), bf),
        shape((width // HEADS, channels), bf),
    )
    fc2p, fc1p, projp, shortp = call(
        functools.partial(weight_grad_kernel, (width, hd, channels, per_q)),
        outs,
        (meta, ah_head, joined, dmem, early, e2, e4, e6a, e6b, e1, e3, e5, e7a, e7b, keep, k2, k4, k6a, k6b, k1, k3, k5, k7a, k7b),
        scratch=[
            pltpu.VMEM((queries, block), bf),
            pltpu.VMEM((queries, block), bf),
            pltpu.VMEM((2, width, LANE), f32),
            pltpu.VMEM((2, block, LANE), f32),
            pltpu.VMEM((queries, width + channels), bf),
            pltpu.VMEM((queries, 2 * width), bf),
            pltpu.SemaphoreType.DMA((2, 10)),
        ],
        us=9,
        far=20,
    )

    def over_four(sent):
        got = [lax.ppermute(sent[k], "clip", [(i, i ^ k) for i in range(n_clip)]) for k in range(1, n_clip)]
        first, second, third_, fourth = [v.astype(f32) for v in [sent[0]] + got]
        return (first + second) + (third_ + fourth)

    def over_clips(parts, permute):
        parts = [v.reshape(n_clip, v.shape[0] // n_clip, v.shape[1]) for v in parts]
        ends = np.cumsum([0] + [v.shape[1] for v in parts])
        value = jnp.concatenate(parts, axis=1) if len(parts) > 1 else parts[0]
        if permute and n_clip == 4:
            clip = lax.axis_index("clip")
            total = over_four([lax.dynamic_index_in_dim(value, clip ^ k, 0, keepdims=False) for k in range(n_clip)])
        else:
            total = jnp.sum(lax.all_to_all(value, "clip", 0, 0, tiled=True).astype(f32), axis=0)
        return [total[lo:hi] for lo, hi in zip(ends, ends[1:])]

    dk, fc1p = lax.optimization_barrier((dk, fc1p))
    first_back = lax.all_to_all(fc1p, G, 0, 0, tiled=True)
    part_fc2, part_proj, part_short = over_clips([fc2p, projp, shortp], True)
    sent = valid // 2 + third
    pgp, stats = pl.pallas_call(
        functools.partial(conv_back_kernel, hdims),
        out_shape=(shape((HEADS, sent + 48, 4 * hd), bf), shape((8, channels), f32)),
        in_specs=[pl.BlockSpec(memory_space=pltpu.SMEM)] + [vmem] * 7 + [pl.BlockSpec(memory_space=pl.ANY)] * 10,
        out_specs=(vmem,) * 2,
        scratch_shapes=[
            pltpu.VMEM((FR * GRID * GRID, 3 * LANE), bf),
            pltpu.VMEM((FLAT, LANE), f32),
            pltpu.VMEM((FLAT, LANE), f32),
            pltpu.VMEM((2 * queries, LANE), f32),
            pltpu.VMEM((FR, GRID * GRID, channels), bf),
            pltpu.VMEM((2, 3 * hd, LANE), f32),
            pltpu.SemaphoreType.DMA((HEADS * frames,)),
        ],
        compiler_params=pltpu.CompilerParams(vmem_limit_bytes=56 << 20),
        cost_estimate=cost(18),
    )(meta, dk, dv, pq, taps, norm1_gain, norm1_bias, w_qkv, *blocks)
    pgp, first_back = lax.optimization_barrier((pgp, first_back))
    pg_rows = lax.all_to_all(pgp, G, 0, 0, tiled=True)
    [part_fc1] = over_clips([first_back[:, taken:].reshape(-1, channels)], True)
    late = call(
        functools.partial(late_kernel, dims),
        shape((LATE, channels), bf),
        (mem, first_back, gconv, stats, small2),
        scratch=[pltpu.VMEM((4, width // LANE, GRID, LANE), f32), pltpu.VMEM((LATE, channels), f32)],
        smem=0,
        us=5,
    )
    if n_clip == 4:
        late = over_four([late] * n_clip)
    else:
        late = jnp.sum(lax.all_gather(late, "clip", axis=0).astype(f32), axis=0)
    late_full = lax.all_gather(late, G, axis=0)
    vector = lambda n: shape((n,), f32)
    g1, b1, gbq, gconv, gcomp, gt, gh, gw, gbp, gbs, g2, b2, gb1, gb2 = call(
        functools.partial(sums_kernel, (width, hd, channels)),
        (
            vector(channels), vector(channels), vector(3 * width), shape((3, 3, 3, 2, width), f32), shape(compress.shape, f32),
            shape(rel_t.shape, f32), shape(rel_h.shape, f32), shape(rel_w.shape, f32),
            vector(width), vector(width), vector(width), vector(width), vector(mlp), vector(width),
        ),
        (late_full,),
        scratch=[pltpu.VMEM((TABLE_ROWS, LANE), f32)],
        smem=0,
        us=3,
    )
    pg_rows, gb1, part_fc1 = lax.optimization_barrier((pg_rows, gb1, part_fc1))
    qkv_rows = pg_rows[:, sent : sent + 3 * hd // HEADS]
    qkv_rows = qkv_rows.reshape(HEADS, 3, hd // HEADS, channels).transpose(1, 0, 2, 3).reshape(-1, channels)
    [part_qkv] = over_clips([qkv_rows], False)
    input_grad = call(
        functools.partial(last_kernel, dims),
        shape((cells_all, channels), bf),
        (x, norm1_gain, w_qkv, pg_rows, mx, max_grad),
        scratch=[pltpu.VMEM((cells_all, channels), f32), pltpu.VMEM((width // LANE, rows * GRID, LANE), f32)],
        smem=0,
        us=5,
    )
    return (
        output[None],
        input_grad.reshape(clip_input.shape),
        g1,
        b1,
        part_qkv.reshape(-1, cols),
        gbq,
        jnp.moveaxis(gconv, 3, 0),
        gcomp,
        gt,
        gh,
        gw,
        part_proj.reshape(-1, hd),
        gbp,
        part_short.reshape(-1, cols),
        gbs,
        g2,
        b2,
        part_fc1.reshape(-1, hd),
        gb1,
        part_fc2,
        gb2,
    )


def solution(mesh):
    split = P("clip", "tm", "height", None, None)
    shared = P()
    weight = P("clip", ("tm", "height"))
    placed = (split, P("clip", None, None, "tm", "height", None, None), P("clip"), P("clip")) + (shared,) * 19 + (split,)
    outs = (split, split, shared, shared, weight) + (shared,) * 6 + (weight, shared, weight, shared, shared, shared, weight, shared, weight, shared)
    return jax.shard_map(body, mesh=mesh, in_specs=placed, out_specs=outs, check_vma=False)
```

```python
import functools

import jax
import jax.numpy as jnp
import numpy as np
from jax import lax
from jax.experimental import pallas as pl
from jax.experimental.pallas import tpu as pltpu
from jax.sharding import PartitionSpec as P

HEADS = 8
SIDE_SMALL = 14
SIDE_BIG = 20
MEM = 2
EPSILON = 1e-06
SQRT_HALF = 0.7071067811865476
ROOT_TWO_PI = 2.5066282746310002
LOG2E = 1.4426950408889634
FAR = -1e30

GRID = 24
FR = 8
HALF = GRID // 2
VW = SIDE_BIG
VH = VW // 2
LANE = 128
PLANE = (VW + 1) * GRID
FLAT = GRID + (FR + 2) * PLANE
CUR = FR * VW * VW
KEYS_USED = CUR + MEM * FR * VH * VH
KEYS = -(-KEYS_USED // 256) * 256
BACK = 144
LATE_COMP, LATE_SMALL, LATE_TABLE, LATE = 17, 33, 35, 40
STEP = 4
TABLE_ROWS = 2 * FR + 4 * GRID
TAB = 8 * FR + 2 * GRID * HALF

bf = jnp.bfloat16
f32 = jnp.float32
HI = lax.Precision.HIGHEST
G = ("tm", "height")


def nn(a, b, **kw):
    return lax.dot_general(a, b, (((1,), (0,)), ((), ())), preferred_element_type=f32, **kw)


def nt(a, b, **kw):
    return lax.dot_general(a, b, (((1,), (1,)), ((), ())), preferred_element_type=f32, **kw)


def tn(a, b, **kw):
    return lax.dot_general(a, b, (((0,), (0,)), ((), ())), preferred_element_type=f32, **kw)


def shape(dims, dtype):
    return jax.ShapeDtypeStruct(dims, dtype)


def cost(us):
    return pl.CostEstimate(flops=int(us * 1e9), bytes_accessed=0, transcendentals=0)


def call(kernel, outs, args, scratch=(), smem=1, us=5, far=0, away=()):
    specs = [pl.BlockSpec(memory_space=pltpu.SMEM)] * smem
    specs += [pl.BlockSpec(memory_space=pltpu.VMEM)] * (len(args) - smem - far)
    specs += [pl.BlockSpec(memory_space=pl.ANY)] * far
    return pl.pallas_call(
        kernel,
        out_shape=outs,
        in_specs=specs,
        out_specs=(
            tuple(pl.BlockSpec(memory_space=pl.ANY if i in away else pltpu.VMEM) for i in range(len(outs)))
            if isinstance(outs, tuple)
            else pl.BlockSpec(memory_space=pltpu.VMEM)
        ),
        scratch_shapes=list(scratch),
        compiler_params=pltpu.CompilerParams(vmem_limit_bytes=56 << 20),
        cost_estimate=cost(us),
    )(*args)


def row_of(ref, lo, hi):
    return ref[lo:hi].reshape(1, hi - lo)


def pack_rows(value, scratch, groups):
    rows, lanes = value.shape
    scratch[0:rows, :] = pad_lanes(value, LANE)
    parts = [scratch[pl.ds(g, rows // groups, groups), :][:, 0:lanes] for g in range(groups)]
    return jnp.concatenate(parts, axis=1)


def pad_lanes(x, lanes):
    return jnp.concatenate([x, jnp.zeros((x.shape[0], lanes - x.shape[1]), x.dtype)], axis=1)


def layer_unit(x):
    centred = x - jnp.mean(x, axis=-1, keepdims=True)
    inverse = lax.rsqrt(jnp.mean(centred * centred, axis=-1, keepdims=True) + EPSILON)
    return centred * inverse, inverse


def pair_reduce(value, scratch, op):
    rows, lanes = value.shape
    outs = []
    for j in range(lanes // LANE):
        scratch[j, 0:rows, :] = value[:, j * LANE : (j + 1) * LANE]
    for j in range(lanes // LANE):
        outs.append(op(scratch[j, pl.ds(0, rows // 2, 2), :], scratch[j, pl.ds(1, rows // 2, 2), :]))
    return jnp.concatenate(outs, axis=1)


def join_lines(value, op):
    return jnp.concatenate(
        [op(value[a : a + GRID], value[a + GRID : a + 2 * GRID]) for a in range(0, value.shape[0], 2 * GRID)], axis=0
    )


def pair_spread(value, scratch):
    rows, lanes = value.shape
    for j in range(lanes // LANE):
        part = value[:, j * LANE : (j + 1) * LANE]
        scratch[j, pl.ds(0, rows, 2), :] = part
        scratch[j, pl.ds(1, rows, 2), :] = part
    return jnp.concatenate([scratch[j, 0 : 2 * rows, :] for j in range(lanes // LANE)], axis=1)


def norm_kernel(dims, x_ref, g_ref, b_ref, n1_ref, mx_ref, tiles):
    frames, rows = dims
    half = rows // 2
    channels = x_ref.shape[1]
    per = rows * GRID
    g = row_of(g_ref, 0, channels)
    b = row_of(b_ref, 0, channels)
    for t in range(frames):
        x = x_ref[t * per : (t + 1) * per, :].astype(f32)
        unit, _ = layer_unit(x)
        n1_ref[t * per : (t + 1) * per, :] = (unit * g + b).astype(bf)
        tall = join_lines(x, jnp.maximum)
        mx_ref[t * half * HALF : (t + 1) * half * HALF, :] = pair_reduce(tall, tiles, jnp.maximum)


def squeeze_kernel(dims, mem_ref, c_ref, cot_ref, mx_ref, out_ref, early_ref, tiles, squeezed):
    frames, rows, width, hd = dims
    half = rows // 2
    count = half * frames * VH
    odd = lax.broadcasted_iota(jnp.int32, (GRID, 1), 0) % 2 == 1
    for m in range(2):
        taps = [jnp.where(odd, c_ref[m, i, 1:2, :], c_ref[m, i, 0:1, :]) for i in range(2)]
        for s in range(MEM):
            for t in range(frames):
                parts = [
                    mem_ref[s, m, t, 2 * a].astype(f32) * taps[0] + mem_ref[s, m, t, 2 * a + 1].astype(f32) * taps[1]
                    for a in range(half)
                ]
                for a in range(half):
                    done = pair_reduce(parts[a], tiles.at[(t * half + a) % 4], jnp.add)
                    squeezed[m, s, a * frames * VH + t * VH : a * frames * VH + (t + 1) * VH, :] = done[0:VH]
            squeezed[m, s, count:LANE, :] = jnp.zeros((LANE - count, width), f32)
    for n in range(HEADS):
        cut = slice(n * hd, (n + 1) * hd)
        out_ref[n] = jnp.concatenate(
            [squeezed[0, 0, :, cut], squeezed[1, 0, :, cut], squeezed[0, 1, :, cut], squeezed[1, 1, :, cut]], axis=1
        ).astype(bf)
    cot = jnp.concatenate([cot_ref[t, a].astype(f32) for t in range(frames) for a in range(half)], axis=0)
    early_ref[:, 0:width] = cot.astype(bf)
    early_ref[:, width:] = mx_ref[...].astype(bf)


def flat_row(t, h):
    return GRID + (1 + t) * PLANE + h * GRID


def fill_grid(grid):
    zero = jnp.zeros((GRID, LANE), f32)
    grid[0 : GRID + PLANE, :] = jnp.zeros((GRID + PLANE, LANE), f32)
    grid[flat_row(FR, 0) :, :] = jnp.zeros((FLAT - flat_row(FR, 0), LANE), f32)
    for t in range(FR):
        grid[flat_row(t, VW) : flat_row(t, VW) + GRID, :] = zero


def taps9(w_ref, part):
    return [[[w_ref[(a * 3 + b) * 3 + c : (a * 3 + b) * 3 + c + 1, part * LANE : (part + 1) * LANE] for c in range(3)] for b in range(3)] for a in range(3)]


def four_rows(grid, weights, base, flip, keep=VW):
    acc = [[None] * 3 for _ in range(4)]
    for line in range(-1, 5):
        for a in range(3):
            shift = (1 - a if flip else a - 1) * PLANE + line * GRID
            cells = grid[pl.ds(pl.multiple_of(base + shift, 8), GRID), :]
            for h in range(4):
                b = (h - line + 1) if flip else (line - h + 1)
                if b < 0 or b > 2:
                    continue
                for c in range(3):
                    term = cells * weights[a][b][c]
                    acc[h][c] = term if acc[h][c] is None else acc[h][c] + term
    outs = []
    for h in range(4):
        left, mid, right = (acc[h][2], acc[h][1], acc[h][0]) if flip else (acc[h][0], acc[h][1], acc[h][2])
        outs.append((pltpu.roll(left, 1, 0) + mid + pltpu.roll(right, GRID - 1, 0))[0:keep])
    return jnp.concatenate(outs, axis=0)


def gather_blocks(dims, meta, refs, out, sems):
    frames, rows, n_height = dims
    member = meta[4]
    per = rows * GRID
    x0, x2, x4, x6a, x6b, x1, x3, x5, x7a, x7b = refs
    copies = []
    for d, parts in enumerate([[x0], [x1], [x2], [x3], [x4], [x5], [x6a, x6b], [x7a, x7b]]):
        src = member ^ d
        t = lax.div(src, n_height) * frames
        at = pl.ds(pl.multiple_of(lax.rem(src, n_height) * per, 16), per)
        for ref in parts:
            for i in range(ref.shape[0] // per):
                copies.append(pltpu.make_async_copy(ref.at[i * per : (i + 1) * per, :], out.at[t, at, :], sems.at[len(copies)]))
                t = t + 1
    return copies


def own_weights(meta, qkv_ref, out, sems):
    width, hd = qkv_ref.shape[0] // 3, out.shape[1]
    rows = [pl.ds(pl.multiple_of(p * width + meta[4] * hd, 32), hd) for p in range(3)]
    return [pltpu.make_async_copy(qkv_ref.at[rows[p], :], out.at[p], sems.at[p]) for p in range(3)]


def conv_kernel(dims, meta, w_ref, bias_ref, *refs):
    frames, rows, n_height, hd = dims
    half = rows // 2
    blocks, qkv_ref, (k_ref, v_ref, q_ref, mk, mv, gk, gv, gather, tiles, qrow, wide, sems, more) = refs[:10], refs[10], refs[11:]
    copies = own_weights(meta, qkv_ref, wide, more) + gather_blocks(dims[:3], meta, blocks, gather, sems)
    for copy in copies:
        copy.start()
    side = meta[0]
    channels = qkv_ref.shape[1]
    for grid in (gk, gv):
        fill_grid(grid)
    blank = jnp.zeros((LANE - hd, channels), bf)
    index = lax.broadcasted_iota(jnp.int32, (VW * GRID, 1), 0)
    line = (index * 2731) >> 16
    inside = ((line < side) & (index - line * GRID < side)).astype(f32)
    for copy in copies:
        copy.wait()
    weight_q = jnp.concatenate([wide[0], blank], axis=0)
    weight_kv = jnp.concatenate([wide[1], blank, wide[2], blank], axis=0)
    piece = half * HALF
    for t in range(FR):
        query = pair_reduce(join_lines(nt(gather[t], weight_q), jnp.add), tiles.at[t % 2], jnp.add) * 0.25 + bias_ref[0:1, 0:LANE]
        for h in range(n_height):
            at = (t // frames * n_height + h) * frames * piece + t % frames * piece
            qrow[at : at + piece, :] = query[h * piece : (h + 1) * piece]
        pair = ((nt(gather[t, 0 : VW * GRID, :], weight_kv) + bias_ref[0:1, LANE:]) * inside).astype(bf).astype(f32)
        gk[flat_row(t, 0) : flat_row(t, VW), :] = pair[:, 0:LANE]
        gv[flat_row(t, 0) : flat_row(t, VW), :] = pair[:, LANE:]
    q_ref[...] = qrow[...].astype(bf)
    sent = [pltpu.make_async_copy(gk, mk, more.at[3]), pltpu.make_async_copy(gv, mv, more.at[4])]
    for copy in sent:
        copy.start()
    local = lax.broadcasted_iota(jnp.int32, (4 * VW, LANE), 0)
    lane = lax.broadcasted_iota(jnp.int32, (4 * VW, LANE), 1)
    line = (local * 3277) >> 16
    column = local - line * VW
    fixed = [(lane + o == 143 - column) | (lane + o == 191 - column) for o in (0, LANE)]
    ones = (lane == hd).astype(f32)

    def step(it, carry):
        t = it // (VW // 4)
        quad = it % (VW // 4)
        base = GRID + (1 + t) * PLANE + quad * 4 * GRID
        out = pl.ds(pl.multiple_of(it * (4 * VW), 16), 4 * VW)
        mixed_k = four_rows(gk, taps9(w_ref, 0), base, False)
        mixed_v = four_rows(gv, taps9(w_ref, 1), base, False)
        h = quad * 4 + line
        bad = (h >= side) | (column >= side)
        for o in range(2):
            at = lane + o * LANE
            hit = fixed[o] | (at == 103 - t) | (at == 151 - t) | (at == 123 - h) | (at == 171 - h) | ((at == 192) & bad)
            marks = hit.astype(f32)
            k_ref[out, o * LANE : (o + 1) * LANE] = ((mixed_k + marks) if o == 0 else marks).astype(bf)
        v_ref[out, :] = (mixed_v + ones).astype(bf)
        return carry

    lax.fori_loop(0, FR * VW // 4, step, 0)
    for copy in sent:
        copy.wait()


def build_table(tab, t_ref, h_ref, w_ref):
    tab[...] = jnp.zeros(tab.shape, f32)
    for v in range(FR):
        tab[8 * v : 8 * v + FR, :] = t_ref[v : v + FR, :]
    for n, ref in ((0, h_ref), (1, w_ref)):
        for a in range(HALF):
            at = 8 * FR + (n * HALF + a) * GRID
            first = 2 * a + GRID - VW
            tab[at : at + VW, :] = ref[first : first + VW, :]


def attend_kernel(dims, meta, kc_ref, vc_ref, q_ref, y_ref, t_ref, h_ref, w_ref, place_ref, k_out, v_out, qt_ref, o_ref, l_ref, j_ref, vt, tab, k_ref, v_ref, sems):
    frames, rows, n_height, hd = dims
    half = rows // 2
    side, length = meta[0], meta[1]
    queries = q_ref.shape[0]
    scale = hd**-0.5
    k_ref[0:CUR, :] = kc_ref[...]
    v_ref[0:CUR, :] = vc_ref[...]
    count = half * frames * VH
    each = frames * VH
    lane1 = lax.broadcasted_iota(jnp.int32, (1, LANE), 1)
    at = CUR
    for src in range(HEADS):
        packed = y_ref[src].astype(f32)
        first = src % n_height * half
        used = min(max(VH - first, 0), half) * each
        if used > 0:
            halves = []
            for m in range(2):
                halves.append(jnp.concatenate([packed[0:used, m * hd : (m + 1) * hd], packed[0:used, (2 + m) * hd : (3 + m) * hd]], axis=0))
            index = lax.broadcasted_iota(jnp.int32, (2 * used, LANE), 0)
            step = (index >= used).astype(jnp.int32)
            inner = index - step * used
            a = (inner >= each).astype(jnp.int32) + (inner >= 2 * each).astype(jnp.int32)
            inner = inner - a * each
            c = inner - ((inner * 6554) >> 16) * VH
            bad = (step >= length) | (2 * (first + a) >= side) | (2 * c >= side)
            mark = (bad & (lax.broadcasted_iota(jnp.int32, (2 * used, LANE), 1) == 64)).astype(f32)
            k_ref[at : at + 2 * used, 0:LANE] = pad_lanes(halves[0], LANE).astype(bf)
            k_ref[at : at + 2 * used, LANE:] = mark.astype(bf)
            v_ref[at : at + 2 * used, :] = (pad_lanes(halves[1], LANE) + (lane1 == hd).astype(f32)).astype(bf)
            at += 2 * used
    rest = KEYS - at
    k_ref[at:, 0:LANE] = jnp.zeros((rest, LANE), bf)
    k_ref[at:, LANE:] = jnp.broadcast_to((lane1 == 64).astype(f32), (rest, LANE)).astype(bf)
    v_ref[at:, :] = jnp.zeros((rest, LANE), bf)
    for i in range(KEYS // 256):
        cut = slice(i * 256, (i + 1) * 256)
        vt[:, cut] = v_ref[cut, :].T
    sent = [pltpu.make_async_copy(k_ref, k_out, sems.at[0]), pltpu.make_async_copy(v_ref, v_out, sems.at[1])]
    for copy in sent:
        copy.start()
    pt = q_ref[...].astype(f32).T[0:hd]
    build_table(tab, t_ref, h_ref, w_ref)
    table = tab[...]
    coarse = table.astype(bf)
    turned = pt.astype(bf)
    along = nn(coarse, turned) + nn((table - coarse.astype(f32)).astype(bf), turned)
    tq, aq, cq = place_ref[0:1, :], place_ref[1:2, :], place_ref[2:3, :]
    part_t = jnp.zeros((FR, queries), f32)
    for v in range(FR):
        part_t = jnp.where(tq == v, along[8 * v : 8 * v + FR], part_t)
    parts = []
    for n, place in ((0, aq), (1, cq)):
        part = jnp.zeros((GRID, queries), f32)
        for a in range(HALF):
            row = 8 * FR + (n * HALF + a) * GRID
            part = jnp.where(place == a, along[row : row + GRID], part)
        parts.append(part[0:VW])
    bias = jnp.concatenate([part_t] + parts, axis=0) * hd**0.5
    high = bias.astype(bf)
    low = (bias - high.astype(f32)).astype(bf)
    qt_ref[0:hd, :] = pt.astype(bf)
    qt_ref[hd : hd + 48, :] = high
    qt_ref[hd + 48 : hd + 96, :] = low
    tail = lax.broadcasted_iota(jnp.int32, (64, queries), 0)
    qt_ref[192:256, :] = jnp.where(tail == 0, FAR, 0.0).astype(bf)
    factor = scale * LOG2E
    query = qt_ref[...]
    top = None
    for lo in range(0, KEYS, 1024):
        cut = slice(lo, min(lo + 1024, KEYS))
        scores = nn(k_ref[cut, :], query)
        here = jnp.max(scores.reshape(scores.shape[0] // 8, 8, queries), axis=0)
        here = jnp.max(here, axis=0, keepdims=True) * factor
        new = here if top is None else jnp.maximum(top, here)
        part = nn(vt[:, cut], jnp.exp2(scores * factor - new).astype(bf))
        total = part if top is None else total * jnp.exp2(top - new) + part
        top = new
    norm = total[hd : hd + 1]
    o_ref[...] = total[0:hd] / norm
    l_ref[...] = top + jnp.log2(norm)
    j_ref[...] = pad_lanes((o_ref[...] + pt).T, LANE).astype(bf)
    for copy in sent:
        copy.wait()


def turn_kernel(k_ref, kt_ref):
    for i in range(KEYS // 256):
        cut = slice(i * 256, (i + 1) * 256)
        kt_ref[0:LANE, cut] = k_ref[cut, 0:LANE].T
        kt_ref[LANE:BACK, cut] = k_ref[cut, LANE:].T[0 : BACK - LANE]


def mlp_kernel(dims, j_ref, early_ref, wp_ref, ws_ref, bp_ref, bs_ref, g_ref, b_ref, w1_ref, b1_ref, w2_ref, b2_ref,
               out_ref, keep_ref, act_ref, dj_ref, mg_ref,
               resid, n2, acc, ngrad, joined, gb1):
    width, hd = dims
    i = pl.program_id(0)
    per_q = early_ref.shape[0]
    block = w1_ref.shape[0]

    @pl.when(i == 0)
    def _():
        joined[...] = jnp.concatenate([j_ref[n][:, 0:hd] for n in range(HEADS)], axis=1)
        shift = row_of(bp_ref, 0, width) + row_of(bs_ref, 0, width)
        value = nt(joined[...], wp_ref[...]) + nt(early_ref[:, width:], ws_ref[...]) + shift
        resid[...] = value
        unit, _ = layer_unit(value)
        n2[...] = (unit * row_of(g_ref, 0, width) + row_of(b_ref, 0, width)).astype(bf)
        acc[...] = jnp.zeros(acc.shape, f32)
        ngrad[...] = jnp.zeros(ngrad.shape, f32)

    here = pl.ds(pl.multiple_of(i * block, LANE), block)
    hidden = nt(n2[...], w1_ref[...]) + b1_ref[here].reshape(1, block)
    gate = 0.5 * (1.0 + lax.erf(hidden * SQRT_HALF))
    act = (hidden * gate).astype(bf)
    each = act_ref.shape[2]
    for n in range(act_ref.shape[0]):
        act_ref[n, 0:per_q, :] = act[:, n * each : (n + 1) * each]
    acc[...] += nt(act, w2_ref[...])
    grad = nn(early_ref[:, 0:width], w2_ref[...])
    hgrad = (grad * (gate + hidden * jnp.exp(-0.5 * hidden * hidden) / ROOT_TWO_PI)).astype(bf)
    for n in range(act_ref.shape[0]):
        act_ref[n, per_q:, :] = hgrad[:, n * each : (n + 1) * each]
    gb1[:, here] = jnp.sum(hgrad.astype(f32), axis=0, keepdims=True)
    ngrad[...] += nn(hgrad, w1_ref[...])

    @pl.when(i == pl.num_programs(0) - 1)
    def _():
        value = resid[...]
        result = value + acc[...] + row_of(b2_ref, 0, width)
        for t in range(out_ref.shape[0]):
            for a in range(out_ref.shape[1]):
                at = (t * out_ref.shape[1] + a) * HALF
                out_ref[t, a] = result[at : at + HALF].astype(bf)
        unit, inverse = layer_unit(value)
        cot = early_ref[:, 0:width].astype(f32)
        grad = ngrad[...]
        scaled = grad * row_of(g_ref, 0, width)
        back = inverse * (
            scaled - jnp.mean(scaled, axis=-1, keepdims=True) - unit * jnp.mean(scaled * unit, axis=-1, keepdims=True)
        )
        low = (cot + back).astype(bf)
        keep_ref[:, 0:width] = n2[...]
        keep_ref[:, width:] = low
        joined_grad = nn(low, wp_ref[...])
        mg_ref[...] = nn(low, ws_ref[...])
        sums = [jnp.sum(v, axis=0, keepdims=True) for v in (low.astype(f32), grad * unit, grad, cot)] + [gb1[...]]
        flat = [v[:, k : k + width] for v in sums for k in range(0, v.shape[1], width)]
        spare = LANE - hd
        for n in range(HEADS):
            exact = jnp.concatenate([flat[n][:, k : k + spare] for k in range(0, width, spare)], axis=0)
            high = exact.astype(bf).astype(f32)
            side = jnp.concatenate([high, exact - high, jnp.zeros((per_q - 2 * exact.shape[0], spare), f32)], axis=0)
            dj_ref[n] = jnp.concatenate([joined_grad[:, n * hd : (n + 1) * hd], side], axis=1).astype(bf)


def attend_back_kernel(dims, qt_ref, q_ref, o_ref, l_ref, dj_ref, t_ref, h_ref, w_ref, place_ref, k_in, kt_in, v_in,
                       dk_ref, dv_ref, mem_ref, pq_ref, small_ref,
                       dot_ref, dq, tab, dtab, dks, dvs, delta, tables, k_ref, kt_ref, v_ref, sems):
    frames, rows, n_height, hd = dims
    half = rows // 2
    queries = q_ref.shape[0]
    scale = hd**-0.5
    factor = scale * LOG2E
    turned = dj_ref[...].astype(f32).T
    half_keys = KEYS // 2

    def brought(i):
        cut = pl.ds(pl.multiple_of(i * half_keys, LANE), half_keys)
        return [
            pltpu.make_async_copy(k_in.at[cut, :], k_ref.at[cut, :], sems.at[0, i]),
            pltpu.make_async_copy(v_in.at[cut, :], v_ref.at[cut, :], sems.at[1, i]),
            pltpu.make_async_copy(kt_in.at[:, cut], kt_ref.at[:, cut], sems.at[2, i]),
        ]

    for copy in brought(0) + brought(1):
        copy.start()
    per_q = queries // HEADS
    spare = jnp.zeros((per_q, LANE - hd), f32)
    for src in range(HEADS):
        spare = spare + dj_ref[src * per_q : (src + 1) * per_q, hd:].astype(f32)
    lines = small_ref.shape[0]
    small_ref[...] = spare[0:lines] + spare[lines : 2 * lines]
    dot_ref[0:hd, :] = turned[0:hd].astype(bf)
    dot_ref[hd:, :] = jnp.zeros((LANE - hd, queries), bf)
    delta[...] = jnp.sum(turned[0:hd] * o_ref[...], axis=0, keepdims=True)
    dq[...] = jnp.zeros(dq.shape, f32)
    def chunk(i, carry):
        cut = pl.ds(pl.multiple_of(i * half_keys, LANE), half_keys)
        for copy in brought(i):
            copy.wait()
        shares = jnp.exp2(nn(k_ref[cut, :], qt_ref[...]) * factor - l_ref[...])
        slope = nn(v_ref[cut, :], dot_ref[...])
        score = (shares * (slope - delta[...])).astype(bf)
        dvs[cut, :] = nn(shares.astype(bf), dj_ref[...])
        dks[cut, :] = nn(score, q_ref[...]) * scale
        dq[...] += nn(kt_ref[:, cut], score)
        return carry

    lax.fori_loop(0, 2, chunk, 0)
    sent = [
        pltpu.make_async_copy(dks.at[0:CUR, :], dk_ref, sems.at[3, 0]),
        pltpu.make_async_copy(dvs.at[0:CUR, :], dv_ref, sems.at[3, 1]),
    ]
    for copy in sent:
        copy.start()
    each = frames * VH
    at = CUR
    for dst in range(HEADS):
        first = dst % n_height * half
        used = min(max(VH - first, 0), half) * each
        if used > 0:
            parts = [ref[at + s * used : at + (s + 1) * used, 0:hd] for s in range(MEM) for ref in (dks, dvs)]
            packed = jnp.concatenate(parts, axis=1)
            at += 2 * used
        if used < LANE:
            zero = jnp.zeros((LANE - used, 4 * hd), f32)
            packed = jnp.concatenate([packed, zero], axis=0) if used > 0 else zero
        mem_ref[dst, 0:LANE, :] = packed.astype(bf)
    build_table(tab, t_ref, h_ref, w_ref)
    tq, aq, cq = place_ref[0:1, :], place_ref[1:2, :], place_ref[2:3, :]
    grad_t = dq[hd : hd + FR, :]
    for v in range(FR):
        dtab[8 * v : 8 * v + FR, :] = jnp.where(tq == v, grad_t, 0.0)
    for n, place in ((0, aq), (1, cq)):
        part = jnp.concatenate(
            [dq[hd + FR + n * VW : hd + FR + (n + 1) * VW, :], jnp.zeros((GRID - VW, queries), f32)], axis=0
        )
        for a in range(HALF):
            row = 8 * FR + (n * HALF + a) * GRID
            dtab[row : row + GRID, :] = jnp.where(place == a, part, 0.0)
    spread = dtab[...].astype(bf)
    pooled_grad = dq[0:hd, :] * scale + tn(tab[...].astype(bf), spread) + dot_ref[0:hd, :].astype(f32)
    pq_ref[...] = pad_lanes(pooled_grad.T * 0.25, LANE)
    grads = nn(spread, q_ref[...])
    tables[...] = jnp.zeros(tables.shape, f32)
    for v in range(FR):
        tables[v : v + FR, :] += grads[8 * v : 8 * v + FR]
    for n in range(2):
        for a in range(HALF):
            row = 8 * FR + (n * HALF + a) * GRID
            first = 2 * FR + n * 2 * GRID + 2 * a + GRID - VW
            tables[first : first + VW, :] += grads[row : row + VW]
    share = TABLE_ROWS // HEADS
    for dst in range(HEADS):
        part = jnp.concatenate([tables[dst * share : (dst + 1) * share, :], jnp.zeros((16 - share, LANE), f32)], axis=0)
        high = part.astype(bf).astype(f32)
        mem_ref[dst, LANE:, :] = jnp.concatenate([high, part - high, jnp.zeros((16, LANE), f32)], axis=1).astype(bf)
    for copy in sent:
        copy.wait()


def conv_back_kernel(dims, meta, dk_ref, dv_ref, pq_ref, w_ref, g_ref, b_ref, *refs):
    frames, rows, n_height, hd = dims
    half = rows // 2
    blocks, qkv_ref, (out_ref, stat_ref, pg, gk, gv, wide, gather, tall, own, sems, more) = refs[:10], refs[10], refs[11:]
    copies = gather_blocks(dims[:3], meta, blocks, gather, sems) + own_weights(meta, qkv_ref, own, more)
    for copy in copies:
        copy.start()
    side = meta[0]
    channels = qkv_ref.shape[1]
    for grid in (gk, gv):
        fill_grid(grid)
    for ref, grid in ((dk_ref, gk), (dv_ref, gv)):
        for t in range(FR):
            for h in range(VW):
                at = (t * VW + h) * VW
                grid[flat_row(t, h) : flat_row(t, h) + GRID, :] = jnp.concatenate(
                    [ref[at : at + VW, :], jnp.zeros((GRID - VW, LANE), f32)], axis=0
                )
    local = lax.broadcasted_iota(jnp.int32, (4 * GRID, 1), 0)
    line = (local * 2731) >> 16
    column = local - line * GRID
    empty = jnp.zeros(((GRID - VW) * GRID, 2 * LANE), bf)
    for t in range(FR):
        pg[t * GRID * GRID + VW * GRID : (t + 1) * GRID * GRID, LANE:] = empty

    def step(it, carry):
        t = it // (VW // 4)
        quad = it % (VW // 4)
        base = GRID + (1 + t) * PLANE + quad * 4 * GRID
        out = pl.ds(pl.multiple_of((t * GRID + quad * 4) * GRID, 32), 4 * GRID)
        inside = ((quad * 4 + line < side) & (column < side)).astype(f32)
        for m, grid in ((0, gk), (1, gv)):
            back = four_rows(grid, taps9(w_ref, m), base, True, GRID)
            pg[out, (1 + m) * LANE : (2 + m) * LANE] = (back * inside).astype(bf)
        return carry

    lax.fori_loop(0, FR * VW // 4, step, 0)
    queries = pq_ref.shape[0]
    wide[pl.ds(0, queries, 2), :] = pq_ref[...]
    wide[pl.ds(1, queries, 2), :] = pq_ref[...]
    per_q = queries // HEADS
    for src in range(HEADS):
        for t in range(frames):
            for a in range(half):
                at = ((src * frames + t) * half + a) * GRID
                lines = wide[at : at + GRID, :]
                row = ((src // n_height * frames + t) * GRID + src % n_height * rows + 2 * a) * GRID
                pg[row : row + 2 * GRID, 0:LANE] = jnp.concatenate([lines, lines], axis=0).astype(bf)
    span = rows * VW
    cells = span * (frames // 2)
    third = per_q // 3
    for dst in range(HEADS):
        first = dst % n_height * rows
        lines = []
        for t2 in range(frames // 2):
            parts = []
            for g in range(2):
                t = dst // n_height * frames + g * (frames // 2) + t2
                at = (t * GRID + first) * GRID
                block = pg[at : at + rows * GRID, LANE:].astype(f32)
                block = jnp.concatenate([block[h * GRID : h * GRID + VW] for h in range(rows)], axis=0)
                parts += [block[:, 0:hd], block[:, LANE : LANE + hd]]
            lines.append(jnp.concatenate(parts, axis=1))
        out_ref[dst, 0:cells, :] = jnp.concatenate(lines, axis=0).astype(bf)
        out_ref[dst, cells : cells + third, :] = jnp.concatenate(
            [pq_ref[dst * per_q + i * third : dst * per_q + (i + 1) * third, :] for i in range(3)], axis=1
        ).astype(bf)
    for copy in copies:
        copy.wait()
    total = jnp.zeros((3 * LANE, channels), f32)
    sums = jnp.zeros((1, 3 * LANE), f32)
    for t in range(FR):
        part = pg[t * GRID * GRID : (t + 1) * GRID * GRID, :]
        total = total + tn(part, gather[t])
        sums = sums + jnp.sum(part.astype(f32), axis=0, keepdims=True)
    total = jnp.concatenate([total[p * LANE : p * LANE + hd] for p in range(3)], axis=0)
    sums = jnp.concatenate([sums[:, p * LANE : p * LANE + hd] for p in range(3)], axis=1)
    cols = channels // HEADS
    packed = 3 * hd // HEADS
    rest = out_ref.shape[1] - cells - third
    for n in range(HEADS):
        value = pack_rows(total[:, n * cols : (n + 1) * cols], tall.at[n % 2], HEADS)
        out_ref[n, cells + third :, :] = jnp.concatenate([value, jnp.zeros((rest - packed, channels), f32)], axis=0).astype(bf)
    weight = jnp.concatenate([own[p].astype(f32) for p in range(3)], axis=0)
    shift = nn(jnp.broadcast_to(sums, (8, 3 * hd)), weight, precision=HI)[0:1]
    gain = jnp.sum(total * weight, axis=0, keepdims=True)
    gain = (gain - shift * row_of(b_ref, 0, channels)) / row_of(g_ref, 0, channels)
    stat_ref[0:1, :] = pad_lanes(sums, channels)
    stat_ref[1:2, :] = gain
    stat_ref[2:3, :] = shift
    stat_ref[3:8, :] = jnp.zeros((5, channels), f32)


def gather_rows(meta, refs, out, sems):
    x0, x2, x4, x6a, x6b, x1, x3, x5, x7a, x7b = refs
    copies = []
    for d, parts in enumerate([[x0], [x1], [x2], [x3], [x4], [x5], [x6a, x6b], [x7a, x7b]]):
        at = (meta[4] ^ d) * (out.shape[0] // HEADS)
        for ref in parts:
            size = ref.shape[0]
            copies.append(pltpu.make_async_copy(ref, out.at[pl.ds(pl.multiple_of(at, 16), size), :], sems.at[len(copies)]))
            at = at + size
    return copies


def weight_grad_kernel(dims, meta, ah_ref, j_ref, dmem_ref, *refs):
    width, hd, channels, per_q = dims
    early, kept = refs[:10], refs[10:20]
    fc2_ref, fc1_ref, proj_ref, short_ref, act, hgrad, tall, parts, cot_ref, keep_ref, sems = refs[20:]
    member = meta[4]
    first = gather_rows(meta, early, cot_ref, sems.at[0])
    second = gather_rows(meta, kept, keep_ref, sems.at[1])
    for copy in first + second:
        copy.start()
    for src in range(HEADS):
        cut = slice(src * per_q, (src + 1) * per_q)
        act[cut, :] = ah_ref[src, 0:per_q, :]
        hgrad[cut, :] = ah_ref[src, per_q:, :]
    for copy in first:
        copy.wait()
    fc2_ref[...] = tn(cot_ref[:, 0:width], act[...]).astype(bf)
    for copy in second:
        copy.wait()
    normed = keep_ref[:, 0:width]
    resid = keep_ref[:, width : 2 * width]
    fc1 = tn(hgrad[...], normed)
    for n in range(HEADS):
        fc1_ref[n, 0 : dmem_ref.shape[1], :] = dmem_ref[n]
        fc1_ref[n, dmem_ref.shape[1] :, :] = pack_rows(fc1[:, n * hd : (n + 1) * hd], parts.at[n % 2], channels // hd).astype(bf)
    cols = channels // HEADS
    lane = lax.broadcasted_iota(jnp.int32, (channels, LANE), 1)
    pick = (lax.broadcasted_iota(jnp.int32, (channels, LANE), 0) == lane + member * cols) & (lane < cols)
    maxima = nn(cot_ref[:, width:], pick.astype(f32).astype(bf)).astype(bf)
    both = tn(resid, jnp.concatenate([j_ref[...], maxima], axis=1))
    proj_ref[...] = pack_rows(both[:, 0:hd], tall.at[0], channels // hd).astype(bf)
    short_ref[...] = pack_rows(both[:, LANE : LANE + cols], tall.at[1], channels // cols).astype(bf)


def last_kernel(dims, x_ref, g_ref, mx_ref, mg_ref, w_in, pg_in, out_ref, full, tiles, w_ref, pg_ref, sems):
    frames, rows, width, hd = dims
    half = rows // 2
    cells = rows * VW * (frames // 2)
    third = frames * half * HALF // 3
    channels = x_ref.shape[1]
    rows_in = pg_ref.shape[1]
    copies = [pltpu.make_async_copy(w_in, w_ref, sems.at[HEADS])]
    copies += [pltpu.make_async_copy(pg_in.at[n, 0:rows_in, :], pg_ref.at[n], sems.at[n]) for n in range(HEADS)]
    for copy in copies:
        copy.start()
    copies[0].wait()
    tops = jnp.zeros((cells, channels), f32)
    lows = jnp.zeros((cells, channels), f32)
    queries = []
    for n in range(HEADS):
        weight = jnp.concatenate(
            [w_ref[width + n * hd : width + (n + 1) * hd, :], w_ref[2 * width + n * hd : 2 * width + (n + 1) * hd, :]], axis=0
        )
        copies[1 + n].wait()
        packed = pg_ref[n]
        tops = tops + nn(packed[0:cells, 0 : 2 * hd], weight)
        lows = lows + nn(packed[0:cells, 2 * hd :], weight)
        queries.append(
            jnp.concatenate([packed[cells : cells + third, i * LANE : i * LANE + hd] for i in range(3)], axis=0)
        )
    for part, value in ((0, tops), (1, lows)):
        for line in range(frames // 2 * rows):
            at = (part * (frames // 2) * rows + line) * GRID
            full[at : at + GRID, :] = jnp.concatenate(
                [value[line * VW : (line + 1) * VW], jnp.zeros((GRID - VW, channels), f32)], axis=0
            )
    query = nn(jnp.concatenate(queries, axis=1), w_ref[0:width, :])
    per = rows * GRID
    per_q = half * HALF
    g = row_of(g_ref, 0, channels)
    for t in range(frames):
        cut = slice(t * per_q, (t + 1) * per_q)
        x = x_ref[t * per : (t + 1) * per, :].astype(f32)

        def spread(value):
            wide = pair_spread(value, tiles)
            lines = []
            for a in range(half):
                lines += [wide[a * GRID : (a + 1) * GRID]] * 2
            return jnp.concatenate(lines, axis=0)

        grad = full[t * per : (t + 1) * per, :] + spread(query[cut])
        hits = (x == spread(mx_ref[cut, :])).astype(f32)
        sums = jnp.concatenate(
            [hits[2 * a * GRID : (2 * a + 1) * GRID] + hits[(2 * a + 1) * GRID : (2 * a + 2) * GRID] for a in range(half)], axis=0
        )
        number = pair_reduce(sums, tiles, jnp.add)
        pool = hits * spread(mg_ref[cut, :] / number)
        unit, inverse = layer_unit(x)
        scaled = grad * g
        back = inverse * (
            scaled - jnp.mean(scaled, axis=-1, keepdims=True) - unit * jnp.mean(scaled * unit, axis=-1, keepdims=True)
        )
        out_ref[t * per : (t + 1) * per, :] = (back + pool).astype(bf)


def conv_grad_kernel(hd, mk_in, mv_in, dk_in, dv_in, out_ref, acc, mk, mv, dks, dvs, sems):
    groups = FR // 2
    lead = GRID + 4 * PLANE

    def brought(g, first):
        if first:
            cut = pl.ds(0, lead)
        else:
            cut = pl.ds(pl.multiple_of(lead + (g - 1) * 2 * PLANE, 8), 2 * PLANE)
        rows = pl.ds(pl.multiple_of(g * (CUR // groups), 16), CUR // groups)
        pairs = [(mk_in, mk, cut), (mv_in, mv, cut), (dk_in, dks, rows), (dv_in, dvs, rows)]
        return [pltpu.make_async_copy(a.at[c, :], b.at[c, :], sems.at[i, g]) for i, (a, b, c) in enumerate(pairs)]

    for g in range(groups):
        for copy in brought(g, g == 0):
            copy.start()
    acc[...] = jnp.zeros(acc.shape, f32)
    blank = jnp.zeros((GRID - VW, LANE), f32)

    def step(it, carry):
        t = it // (VW // 4)
        base = GRID + (1 + t) * PLANE + it % (VW // 4) * 4 * GRID
        for m, ref, masked in ((0, dks, mk), (1, dvs, mv)):
            quad = ref[pl.ds(pl.multiple_of(it * (4 * VW), 16), 4 * VW), :]
            for h in range(4):
                here = jnp.concatenate([quad[h * VW : (h + 1) * VW], blank], axis=0)
                turned = [pltpu.roll(here, GRID - 1, 0), here, pltpu.roll(here, 1, 0)]
                for a in range(3):
                    for b in range(3):
                        cells = masked[pl.ds(pl.multiple_of(base + (a - 1) * PLANE + (h + b - 1) * GRID, 8), GRID), :]
                        for c in range(3):
                            prod = cells * turned[c]
                            acc[m * 27 + (a * 3 + b) * 3 + c] += prod[0:8] + prod[8:16] + prod[16:24]
        return carry

    def group(g, carry):
        @pl.when(g == 0)
        def _():
            for copy in brought(0, True):
                copy.wait()

        @pl.when(g > 0)
        def _():
            for copy in brought(g, False):
                copy.wait()

        each = 2 * VW // 4
        return lax.fori_loop(g * each, (g + 1) * each, step, carry)

    lax.fori_loop(0, groups, group, 0)
    sums = [jnp.sum(acc[tap], axis=0, keepdims=True) for tap in range(54)] + [jnp.zeros((1, LANE), f32)] * 2
    sums = jnp.concatenate(sums, axis=0)
    out_ref[0:14, :] = jnp.concatenate([sums[14 * g : 14 * (g + 1), 0:hd] for g in range(4)], axis=1)
    out_ref[14:16, :] = jnp.zeros((2, 4 * hd), f32)


def late_kernel(dims, conv_ref, stat_ref, small_ref, mem_in, p_in, late_ref, tiles, lines, mem_ref, p_ref, sems):
    frames, rows, width, hd = dims
    half = rows // 2
    channels = late_ref.shape[1]
    first = pltpu.make_async_copy(p_in.at[:, 0 : p_ref.shape[1], :], p_ref, sems.at[2 * MEM])
    copies = [pltpu.make_async_copy(mem_in.at[s, m], mem_ref.at[s, m], sems.at[m * MEM + s]) for m in range(2) for s in range(MEM)]
    for copy in [first] + copies:
        copy.start()
    first.wait()
    for m in range(2):
        sums = [jnp.zeros((GRID, width), f32) for _ in range(2)]
        for s in range(MEM):
            copies[m * MEM + s].wait()
            grads = jnp.concatenate(
                [p_ref[n][0:LANE, (2 * s + m) * hd : (2 * s + m + 1) * hd] for n in range(HEADS)], axis=1
            ).astype(f32)
            for t in range(frames):
                for a in range(half):
                    at = (a * frames + t) * VH
                    some = jnp.concatenate([grads[at : at + VH], jnp.zeros((HALF - VH, width), f32)], axis=0)
                    wide = pair_spread(some, tiles.at[(t * half + a) % 4])
                    for i in range(2):
                        sums[i] = sums[i] + mem_ref[s, m, t, 2 * a + i].astype(f32) * wide
        odd = (lax.broadcasted_iota(jnp.int32, (GRID, 1), 0) % 2 == 1).astype(f32)
        for i in range(2):
            for j, keep in ((0, 1.0 - odd), (1, odd)):
                done = jnp.sum(sums[i] * keep, axis=0, keepdims=True)
                for k in range(width // channels):
                    at = LATE_COMP + 8 * k + 4 * m + 2 * i + j
                    lines[at : at + 1, :] = done[:, k * channels : (k + 1) * channels]
    lines[0:14, :] = conv_ref[0:14, :]
    lines[14:17, :] = stat_ref[0:3, :]
    count = small_ref.shape[0] // 2
    for k in range(2):
        lines[LATE_SMALL + k : LATE_SMALL + k + 1, :] = jnp.concatenate(
            [small_ref[k * count + i : k * count + i + 1, :] for i in range(count)], axis=1
        )
    tables = jnp.zeros((16, LANE), f32)
    for n in range(HEADS):
        part = p_ref[n][LANE : LANE + 16, :].astype(f32)
        tables = tables + part[:, 0:LANE] + part[:, LANE : 2 * LANE]
    lines[LATE_TABLE : LATE_TABLE + 5, :] = jnp.concatenate([tables[5 * g : 5 * (g + 1), :] for g in range(3)], axis=1)
    late_ref[...] = lines[...].astype(bf)


def sums_kernel(dims, late_ref, g1_ref, b1_ref, bqkv_ref, conv_ref, comp_ref, t_ref, h_ref, w_ref, bp_ref, bs_ref, g2_ref, b2_ref, bf1_ref, bf2_ref, lines):
    width, hd, channels = dims
    parts = []
    for n in range(HEADS):
        parts.append(late_ref[n])
    total = parts[0]
    for n in range(1, HEADS):
        total = total + parts[n]
    for g in range(4):
        conv = jnp.concatenate([parts[n][0:14, g * hd : (g + 1) * hd] for n in range(HEADS)], axis=1)
        for r in range(14):
            i = 14 * g + r
            if i < 54:
                conv_ref[i % 27 // 9, i % 9 // 3, i % 3, i // 27 : i // 27 + 1, :] = conv[r : r + 1]
    for p in range(3):
        value = jnp.concatenate([parts[n][14:15, p * hd : (p + 1) * hd] for n in range(HEADS)], axis=1)
        bqkv_ref[p * width : (p + 1) * width] = value.reshape(width)
    g1_ref[...] = total[15:16].reshape(channels)
    b1_ref[...] = total[16:17].reshape(channels)
    for i in range(8):
        value = jnp.concatenate([total[LATE_COMP + 8 * k + i : LATE_COMP + 8 * k + i + 1] for k in range(2)], axis=1)
        comp_ref[i // 4, i % 4 // 2, i % 2 : i % 2 + 1, :] = value
    for n in range(HEADS):
        value = jnp.concatenate([parts[n][LATE_SMALL + k : LATE_SMALL + k + 1] for k in range(2)], axis=1).reshape(width)
        if n == 0:
            bp_ref[...] = value
            bs_ref[...] = value
        elif n < 4:
            (g2_ref, b2_ref, bf2_ref)[n - 1][...] = value
        else:
            bf1_ref[(n - 4) * width : (n - 3) * width] = value
    share = TABLE_ROWS // HEADS
    for n in range(HEADS):
        part = parts[n][LATE_TABLE : LATE_TABLE + 5]
        value = jnp.concatenate([part[:, g * LANE : (g + 1) * LANE] for g in range(3)], axis=0)
        lines[n * share : (n + 1) * share, :] = value[0:share]
    at = 0
    for ref, step in ((t_ref, 2 * FR), (h_ref, 2 * GRID), (w_ref, 2 * GRID)):
        ref[...] = lines[at : at + ref.shape[0], 0:hd]
        at += step


def body(clip_input, memory, mem_len, res_id, norm1_gain, norm1_bias, w_qkv, b_qkv, conv_kv, compress, rel_t, rel_h, rel_w,
         w_proj, b_proj, w_short, b_short, norm2_gain, norm2_bias, w_fc1, b_fc1, w_fc2, b_fc2, cotangent):
    _, frames, rows, grid, channels = clip_input.shape
    width = w_proj.shape[0]
    mlp = w_fc1.shape[0]
    hd = width // HEADS
    half = rows // 2
    n_clip = lax.axis_size("clip")
    n_height = lax.axis_size("height")
    tm, height = lax.axis_index("tm"), lax.axis_index("height")
    member = tm * n_height + height
    side = SIDE_SMALL + (SIDE_BIG - SIDE_SMALL) * res_id[0]
    meta = jnp.stack([side, mem_len[0], tm, height, member]).astype(jnp.int32)
    cells_all = frames * rows * GRID
    valid = frames * rows * VW
    per_q = frames * half * HALF
    third = per_q // 3
    queries = HEADS * per_q
    x = clip_input.reshape(cells_all, channels)
    mem = memory[0]

    dims = (frames, rows, width, hd)
    n1, mx = call(
        functools.partial(norm_kernel, (frames, rows)),
        (shape((cells_all, channels), bf), shape((per_q, channels), f32)),
        (x, norm1_gain, norm1_bias),
        scratch=[pltpu.VMEM((channels // LANE, rows * GRID, LANE), f32)],
        smem=0,
        us=3,
    )

    def swap(value, bit):
        if bit == 4:
            return lax.ppermute(value, "tm", [(i, i ^ 1) for i in range(lax.axis_size("tm"))])
        return lax.ppermute(value, "height", [(i, i ^ bit) for i in range(n_height)])

    def near(value):
        return swap(value, 2), swap(value, 4), swap(value, 1)

    def across(x2, x4, cut):
        return swap(x2[:cut], 4), swap(x4[cut:], 2), swap(x2, 1), swap(x4, 1)

    def last(x6a, x6b):
        return swap(x6a, 1), swap(x6b, 1)

    x2, x4, x1 = near(n1)
    pay2, early = call(
        functools.partial(squeeze_kernel, dims),
        (shape((HEADS, LANE, 4 * hd), bf), shape((per_q, width + channels), bf)),
        (mem, compress, cotangent[0], mx),
        scratch=[pltpu.VMEM((4, width // LANE, GRID, LANE), f32), pltpu.VMEM((2, MEM, LANE, width), f32)],
        smem=0,
        us=5,
    )
    x2, x4, pay2 = lax.optimization_barrier((x2, x4, pay2))
    x6a, x6b, x3, x5 = across(x2, x4, cells_all // 2)
    x7a, x7b = last(x6a, x6b)
    y2 = lax.all_to_all(pay2, G, 0, 0, tiled=True)
    early, x7a = lax.optimization_barrier((early, x7a))
    e2, e4, e1 = near(early)
    cut = -(-per_q // 32) * 16
    taps = lax.dynamic_slice_in_dim(conv_kv.reshape(2, 27, width), member * hd, hd, 2)
    taps = jnp.pad(taps, ((0, 0), (0, 5), (0, LANE - hd)))
    taps = jnp.concatenate([taps[0], taps[1]], axis=1)
    hdims = (frames, rows, n_height, hd)
    bias = lax.dynamic_slice_in_dim(b_qkv.reshape(3, width), member * hd, hd, 1)
    bias = jnp.pad(bias, ((0, 0), (0, LANE - hd))).reshape(1, 3 * LANE)
    vmem = pl.BlockSpec(memory_space=pltpu.VMEM)
    blocks = (n1, x2, x4, x6a, x6b, x1, x3, x5, x7a, x7b)
    kc, vc, q_all, mk, mv = pl.pallas_call(
        functools.partial(conv_kernel, hdims),
        out_shape=(
            shape((CUR, 2 * LANE), bf),
            shape((CUR, LANE), bf),
            shape((queries, LANE), bf),
            shape((FLAT, LANE), f32),
            shape((FLAT, LANE), f32),
        ),
        in_specs=[pl.BlockSpec(memory_space=pltpu.SMEM)] + [vmem] * 2 + [pl.BlockSpec(memory_space=pl.ANY)] * 11,
        out_specs=(vmem,) * 3 + (pl.BlockSpec(memory_space=pl.ANY),) * 2,
        scratch_shapes=[
            pltpu.VMEM((FLAT, LANE), f32),
            pltpu.VMEM((FLAT, LANE), f32),
            pltpu.VMEM((FR, GRID * GRID, channels), bf),
            pltpu.VMEM((2, 1, GRID * HALF, LANE), f32),
            pltpu.VMEM((queries, LANE), f32),
            pltpu.VMEM((3, hd, channels), bf),
            pltpu.SemaphoreType.DMA((HEADS * frames,)),
            pltpu.SemaphoreType.DMA((5,)),
        ],
        compiler_params=pltpu.CompilerParams(vmem_limit_bytes=56 << 20),
        cost_estimate=cost(18),
    )(meta, taps, bias, *blocks, w_qkv)
    index = np.arange(queries)
    src, local = index // per_q, index % per_q
    place = np.zeros((8, queries), np.int32)
    place[0] = src // n_height * frames + local // (half * HALF)
    place[1] = src % n_height * half + local // HALF % half
    place[2] = local % HALF
    place = jnp.asarray(place)
    wide = 384
    kc, e2, e4, e1 = lax.optimization_barrier((kc, e2, e4, e1))
    e6a, e6b, e3, e5 = across(e2, e4, cut)
    k_all, v_all, qt_all, o_all, l_all, joined = call(
        functools.partial(attend_kernel, hdims),
        (
            shape((KEYS, 2 * LANE), bf),
            shape((KEYS, LANE), bf),
            shape((2 * LANE, queries), bf),
            shape((hd, queries), f32),
            shape((1, queries), f32),
            shape((queries, LANE), bf),
        ),
        (meta, kc, vc, q_all, y2, rel_t, rel_h, rel_w, place),
        scratch=[
            pltpu.VMEM((LANE, KEYS), bf),
            pltpu.VMEM((TAB, hd), f32),
            pltpu.VMEM((KEYS, 2 * LANE), bf),
            pltpu.VMEM((KEYS, LANE), bf),
            pltpu.SemaphoreType.DMA((2,)),
        ],
        us=16,
        away=(0, 1),
    )
    joined_rows = lax.all_to_all(joined.reshape(HEADS, per_q, LANE), G, 0, 0, tiled=True)
    kt_all = call(turn_kernel, shape((BACK, KEYS), bf), (k_all,), smem=0, us=4)
    joined_rows, kt_all = lax.optimization_barrier((joined_rows, kt_all))
    block = mlp // HEADS
    whole = lambda *dims: pl.BlockSpec(dims, lambda i: (0,) * len(dims))
    keep_width = 2 * width
    output, keep, acthg, dj, max_grad = pl.pallas_call(
        functools.partial(mlp_kernel, (width, hd)),
        grid=(HEADS // STEP,),
        out_shape=(
            shape((frames, half, HALF, width), bf),
            shape((per_q, keep_width), bf),
            shape((HEADS, 2 * per_q, block), bf),
            shape((HEADS, per_q, LANE), bf),
            shape((per_q, channels), f32),
        ),
        in_specs=[
            whole(HEADS, per_q, LANE),
            whole(per_q, width + channels),
            whole(width, width),
            whole(width, channels),
            whole(width),
            whole(width),
            whole(width),
            whole(width),
            pl.BlockSpec((STEP * block, width), lambda i: (i, 0)),
            whole(mlp),
            pl.BlockSpec((width, STEP * block), lambda i: (0, i)),
            whole(width),
        ],
        out_specs=(
            whole(frames, half, HALF, width),
            whole(per_q, keep_width),
            pl.BlockSpec((STEP, 2 * per_q, block), lambda i: (i, 0, 0)),
            whole(HEADS, per_q, LANE),
            whole(per_q, channels),
        ),
        scratch_shapes=[
            pltpu.VMEM((per_q, width), f32),
            pltpu.VMEM((per_q, width), bf),
            pltpu.VMEM((per_q, width), f32),
            pltpu.VMEM((per_q, width), f32),
            pltpu.VMEM((per_q, width), bf),
            pltpu.VMEM((1, mlp), f32),
        ],
        compiler_params=pltpu.CompilerParams(vmem_limit_bytes=56 << 20),
        cost_estimate=cost(14),
    )(joined_rows, early, w_proj, w_short, b_proj, b_short, norm2_gain, norm2_bias, w_fc1, b_fc1, w_fc2, b_fc2)
    dj_head = lax.all_to_all(dj, G, 0, 0, tiled=True).reshape(queries, LANE)
    keep, e6a, e6b = lax.optimization_barrier((keep, e6a, e6b))
    k2, k4, k1 = near(keep)
    e7a, e7b = last(e6a, e6b)
    acthg, dj_head = lax.optimization_barrier((acthg, dj_head))
    ah_head = lax.all_to_all(acthg, G, 0, 0, tiled=True)

    dk, dv, dmem, pq, small2 = call(
        functools.partial(attend_back_kernel, hdims),
        (
            shape((CUR, LANE), f32),
            shape((CUR, LANE), f32),
            shape((HEADS, LANE + 16, 4 * hd), bf),
            shape((queries, LANE), f32),
            shape((width // (LANE - hd), LANE - hd), f32),
        ),
        (qt_all, q_all, o_all, l_all, dj_head, rel_t, rel_h, rel_w, place, k_all, kt_all, v_all),
        scratch=[
            pltpu.VMEM((LANE, queries), bf),
            pltpu.VMEM((hd + 48, queries), f32),
            pltpu.VMEM((TAB, hd), f32),
            pltpu.VMEM((TAB, queries), f32),
            pltpu.VMEM((KEYS, LANE), f32),
            pltpu.VMEM((KEYS, LANE), f32),
            pltpu.VMEM((1, queries), f32),
            pltpu.VMEM((TABLE_ROWS, LANE), f32),
            pltpu.VMEM((KEYS, 2 * LANE), bf),
            pltpu.VMEM((BACK, KEYS), bf),
            pltpu.VMEM((KEYS, LANE), bf),
            pltpu.SemaphoreType.DMA((4, 2)),
        ],
        smem=0,
        us=25,
        far=3,
        away=(0, 1),
    )
    cols = channels // HEADS
    taken = dmem.shape[1]
    mk, k2, k4, k1 = lax.optimization_barrier((mk, k2, k4, k1))
    k6a, k6b, k3, k5 = across(k2, k4, cut)
    k7a, k7b = last(k6a, k6b)
    gconv = call(
        functools.partial(conv_grad_kernel, hd),
        shape((16, 4 * hd), f32),
        (mk, mv, dk, dv),
        scratch=[pltpu.VMEM((54, 8, LANE), f32)]
        + [pltpu.VMEM((FLAT, LANE), f32)] * 2
        + [pltpu.VMEM((CUR, LANE), f32)] * 2
        + [pltpu.SemaphoreType.DMA((4, FR // 2))],
        smem=0,
        us=12,
        far=4,
    )
    dmem, gconv = lax.optimization_barrier((dmem, gconv))
    outs = (
        shape((width, block), bf),
        shape((HEADS, taken + block * hd // channels, channels), bf),
        shape((width * hd // channels, channels), bf),
        shape((width // HEADS, channels), bf),
    )
    fc2p, fc1p, projp, shortp = call(
        functools.partial(weight_grad_kernel, (width, hd, channels, per_q)),
        outs,
        (meta, ah_head, joined, dmem, early, e2, e4, e6a, e6b, e1, e3, e5, e7a, e7b, keep, k2, k4, k6a, k6b, k1, k3, k5, k7a, k7b),
        scratch=[
            pltpu.VMEM((queries, block), bf),
            pltpu.VMEM((queries, block), bf),
            pltpu.VMEM((2, width, LANE), f32),
            pltpu.VMEM((2, block, LANE), f32),
            pltpu.VMEM((queries, width + channels), bf),
            pltpu.VMEM((queries, 2 * width), bf),
            pltpu.SemaphoreType.DMA((2, 10)),
        ],
        us=9,
        far=20,
    )

    def over_four(sent):
        got = [lax.ppermute(sent[k], "clip", [(i, i ^ k) for i in range(n_clip)]) for k in range(1, n_clip)]
        first, second, third_, fourth = [v.astype(f32) for v in [sent[0]] + got]
        return (first + second) + (third_ + fourth)

    clip = lax.axis_index("clip")

    def send_four(block):
        return [block(clip)] + [lax.ppermute(block(clip ^ k), "clip", [(i, i ^ k) for i in range(n_clip)]) for k in range(1, n_clip)]

    def add(got):
        return (got[0].astype(f32) + got[1].astype(f32)) + (got[2].astype(f32) + got[3].astype(f32))

    dk, fc1p = lax.optimization_barrier((dk, fc1p))
    first_back = lax.all_to_all(fc1p, G, 0, 0, tiled=True)
    own = [v.reshape(n_clip, v.shape[0] // n_clip, channels) for v in (fc2p, projp, shortp)]
    if n_clip == 4:
        together = jnp.concatenate(own, axis=1)
        got2 = send_four(lambda c: lax.dynamic_index_in_dim(together, c, 0, keepdims=False))
    else:
        got2 = lax.all_to_all(jnp.concatenate(own, axis=1), "clip", 0, 0, tiled=True)
    sent = valid // 2 + third
    pgp, stats = pl.pallas_call(
        functools.partial(conv_back_kernel, hdims),
        out_shape=(shape((HEADS, sent + 48, 4 * hd), bf), shape((8, channels), f32)),
        in_specs=[pl.BlockSpec(memory_space=pltpu.SMEM)] + [vmem] * 6 + [pl.BlockSpec(memory_space=pl.ANY)] * 11,
        out_specs=(vmem,) * 2,
        scratch_shapes=[
            pltpu.VMEM((FR * GRID * GRID, 3 * LANE), bf),
            pltpu.VMEM((FLAT, LANE), f32),
            pltpu.VMEM((FLAT, LANE), f32),
            pltpu.VMEM((2 * queries, LANE), f32),
            pltpu.VMEM((FR, GRID * GRID, channels), bf),
            pltpu.VMEM((2, 3 * hd, LANE), f32),
            pltpu.VMEM((3, hd, channels), bf),
            pltpu.SemaphoreType.DMA((HEADS * frames,)),
            pltpu.SemaphoreType.DMA((3,)),
        ],
        compiler_params=pltpu.CompilerParams(vmem_limit_bytes=56 << 20),
        cost_estimate=cost(18),
    )(meta, dk, dv, pq, taps, norm1_gain, norm1_bias, *blocks, w_qkv)
    pgp, first_back, got2 = lax.optimization_barrier((pgp, first_back, got2))
    pg_rows = lax.all_to_all(pgp, G, 0, 0, tiled=True)
    if n_clip == 4:
        each = HEADS // n_clip
        got1 = send_four(
            lambda c: lax.dynamic_slice(first_back, (c * each, taken, 0), (each, first_back.shape[1] - taken, channels))
        )
    else:
        got1 = lax.all_to_all(first_back[:, taken:].reshape(n_clip, -1, channels), "clip", 0, 0, tiled=True)
    late = call(
        functools.partial(late_kernel, dims),
        shape((LATE, channels), bf),
        (gconv, stats, small2, mem, first_back),
        scratch=[
            pltpu.VMEM((4, width // LANE, GRID, LANE), f32),
            pltpu.VMEM((LATE, channels), f32),
            pltpu.VMEM(mem.shape, bf),
            pltpu.VMEM((HEADS, taken, channels), bf),
            pltpu.SemaphoreType.DMA((2 * MEM + 1,)),
        ],
        smem=0,
        us=5,
        far=2,
    )
    if n_clip == 4:
        late = over_four([late] * n_clip)
    else:
        late = jnp.sum(lax.all_gather(late, "clip", axis=0).astype(f32), axis=0)
    late_full = lax.all_gather(late, G, axis=0)
    vector = lambda n: shape((n,), f32)
    g1, b1, gbq, gconv, gcomp, gt, gh, gw, gbp, gbs, g2, b2, gb1, gb2 = call(
        functools.partial(sums_kernel, (width, hd, channels)),
        (
            vector(channels), vector(channels), vector(3 * width), shape((3, 3, 3, 2, width), f32), shape(compress.shape, f32),
            shape(rel_t.shape, f32), shape(rel_h.shape, f32), shape(rel_w.shape, f32),
            vector(width), vector(width), vector(width), vector(width), vector(mlp), vector(width),
        ),
        (late_full,),
        scratch=[pltpu.VMEM((TABLE_ROWS, LANE), f32)],
        smem=0,
        us=3,
    )
    pg_rows, gb1, got1 = lax.optimization_barrier((pg_rows, gb1, got1))
    qkv_rows = pg_rows[:, sent : sent + 3 * hd // HEADS]
    qkv_rows = qkv_rows.reshape(HEADS, 3, hd // HEADS, channels).transpose(1, 0, 2, 3).reshape(-1, channels)
    got = lax.all_to_all(qkv_rows.reshape(n_clip, -1, channels), "clip", 0, 0, tiled=True)
    input_grad = call(
        functools.partial(last_kernel, dims),
        shape((cells_all, channels), bf),
        (x, norm1_gain, mx, max_grad, w_qkv, pg_rows),
        scratch=[
            pltpu.VMEM((cells_all, channels), f32),
            pltpu.VMEM((width // LANE, rows * GRID, LANE), f32),
            pltpu.VMEM(w_qkv.shape, bf),
            pltpu.VMEM((HEADS, sent, channels), bf),
            pltpu.SemaphoreType.DMA((HEADS + 1,)),
        ],
        smem=0,
        us=5,
        far=2,
    )
    if n_clip == 4:
        part_fc1, part2 = add(got1), add(got2)
    else:
        part_fc1, part2 = (jnp.sum(v.astype(f32), axis=0) for v in (got1, got2))
    part_qkv = jnp.sum(got.astype(f32), axis=0)
    ends = np.cumsum([v.shape[1] for v in own])
    part_fc2, part_proj, part_short = part2[: ends[0]], part2[ends[0] : ends[1]], part2[ends[1] :]
    return (
        output[None],
        input_grad.reshape(clip_input.shape),
        g1,
        b1,
        part_qkv.reshape(-1, cols),
        gbq,
        jnp.moveaxis(gconv, 3, 0),
        gcomp,
        gt,
        gh,
        gw,
        part_proj.reshape(-1, hd),
        gbp,
        part_short.reshape(-1, cols),
        gbs,
        g2,
        b2,
        part_fc1.reshape(-1, hd),
        gb1,
        part_fc2,
        gb2,
    )


def solution(mesh):
    split = P("clip", "tm", "height", None, None)
    shared = P()
    weight = P("clip", ("tm", "height"))
    placed = (split, P("clip", None, None, "tm", "height", None, None), P("clip"), P("clip")) + (shared,) * 19 + (split,)
    outs = (split, split, shared, shared, weight) + (shared,) * 6 + (weight, shared, weight, shared, shared, shared, weight, shared, weight, shared)
    return jax.shard_map(body, mesh=mesh, in_specs=placed, out_specs=outs, check_vma=False)
```

```python
import functools

import jax
import jax.numpy as jnp
import numpy as np
from jax import lax
from jax.experimental import pallas as pl
from jax.experimental.pallas import tpu as pltpu
from jax.sharding import PartitionSpec as P

HEADS = 8
SIDE_SMALL = 14
SIDE_BIG = 20
MEM = 2
EPSILON = 1e-06
SQRT_HALF = 0.7071067811865476
ROOT_TWO_PI = 2.5066282746310002
LOG2E = 1.4426950408889634
FAR = -1e30

GRID = 24
FR = 8
HALF = GRID // 2
VW = SIDE_BIG
VH = VW // 2
LANE = 128
PLANE = (VW + 1) * GRID
FLAT = GRID + (FR + 2) * PLANE
CUR = FR * VW * VW
KEYS_USED = CUR + MEM * FR * VH * VH
KEYS = -(-KEYS_USED // 256) * 256
BACK = 144
LATE_COMP, LATE_SMALL, LATE_TABLE, LATE = 17, 33, 35, 40
STEP = 4
TABLE_ROWS = 2 * FR + 4 * GRID
TAB = 8 * FR + 2 * GRID * HALF

bf = jnp.bfloat16
f32 = jnp.float32
HI = lax.Precision.HIGHEST
G = ("tm", "height")


def nn(a, b, **kw):
    return lax.dot_general(a, b, (((1,), (0,)), ((), ())), preferred_element_type=f32, **kw)


def nt(a, b, **kw):
    return lax.dot_general(a, b, (((1,), (1,)), ((), ())), preferred_element_type=f32, **kw)


def tn(a, b, **kw):
    return lax.dot_general(a, b, (((0,), (0,)), ((), ())), preferred_element_type=f32, **kw)


def shape(dims, dtype):
    return jax.ShapeDtypeStruct(dims, dtype)


def cost(us):
    return pl.CostEstimate(flops=int(us * 1e9), bytes_accessed=0, transcendentals=0)


def call(kernel, outs, args, scratch=(), smem=1, us=5, far=0, away=()):
    specs = [pl.BlockSpec(memory_space=pltpu.SMEM)] * smem
    specs += [pl.BlockSpec(memory_space=pltpu.VMEM)] * (len(args) - smem - far)
    specs += [pl.BlockSpec(memory_space=pl.ANY)] * far
    return pl.pallas_call(
        kernel,
        out_shape=outs,
        in_specs=specs,
        out_specs=(
            tuple(pl.BlockSpec(memory_space=pl.ANY if i in away else pltpu.VMEM) for i in range(len(outs)))
            if isinstance(outs, tuple)
            else pl.BlockSpec(memory_space=pltpu.VMEM)
        ),
        scratch_shapes=list(scratch),
        compiler_params=pltpu.CompilerParams(vmem_limit_bytes=56 << 20),
        cost_estimate=cost(us),
    )(*args)


def row_of(ref, lo, hi):
    return ref[lo:hi].reshape(1, hi - lo)


def pack_rows(value, scratch, groups):
    rows, lanes = value.shape
    scratch[0:rows, :] = pad_lanes(value, LANE)
    parts = [scratch[pl.ds(g, rows // groups, groups), :][:, 0:lanes] for g in range(groups)]
    return jnp.concatenate(parts, axis=1)


def pad_lanes(x, lanes):
    return jnp.concatenate([x, jnp.zeros((x.shape[0], lanes - x.shape[1]), x.dtype)], axis=1)


def layer_unit(x):
    centred = x - jnp.mean(x, axis=-1, keepdims=True)
    inverse = lax.rsqrt(jnp.mean(centred * centred, axis=-1, keepdims=True) + EPSILON)
    return centred * inverse, inverse


def pair_reduce(value, scratch, op):
    rows, lanes = value.shape
    outs = []
    for j in range(lanes // LANE):
        scratch[j, 0:rows, :] = value[:, j * LANE : (j + 1) * LANE]
    for j in range(lanes // LANE):
        outs.append(op(scratch[j, pl.ds(0, rows // 2, 2), :], scratch[j, pl.ds(1, rows // 2, 2), :]))
    return jnp.concatenate(outs, axis=1)


def join_lines(value, op):
    return jnp.concatenate(
        [op(value[a : a + GRID], value[a + GRID : a + 2 * GRID]) for a in range(0, value.shape[0], 2 * GRID)], axis=0
    )


def pair_spread(value, scratch):
    rows, lanes = value.shape
    for j in range(lanes // LANE):
        part = value[:, j * LANE : (j + 1) * LANE]
        scratch[j, pl.ds(0, rows, 2), :] = part
        scratch[j, pl.ds(1, rows, 2), :] = part
    return jnp.concatenate([scratch[j, 0 : 2 * rows, :] for j in range(lanes // LANE)], axis=1)


def norm_kernel(dims, x_ref, g_ref, b_ref, n1_ref, mx_ref, tiles):
    frames, rows = dims
    half = rows // 2
    channels = x_ref.shape[1]
    per = rows * GRID
    g = row_of(g_ref, 0, channels)
    b = row_of(b_ref, 0, channels)
    for t in range(frames):
        x = x_ref[t * per : (t + 1) * per, :].astype(f32)
        unit, _ = layer_unit(x)
        n1_ref[t * per : (t + 1) * per, :] = (unit * g + b).astype(bf)
        tall = join_lines(x, jnp.maximum)
        mx_ref[t * half * HALF : (t + 1) * half * HALF, :] = pair_reduce(tall, tiles, jnp.maximum)


def squeeze_kernel(dims, mem_ref, c_ref, cot_ref, mx_ref, out_ref, early_ref, tiles, squeezed):
    frames, rows, width, hd = dims
    half = rows // 2
    count = half * frames * VH
    odd = lax.broadcasted_iota(jnp.int32, (GRID, 1), 0) % 2 == 1
    for m in range(2):
        taps = [jnp.where(odd, c_ref[m, i, 1:2, :], c_ref[m, i, 0:1, :]) for i in range(2)]
        for s in range(MEM):
            for t in range(frames):
                parts = [
                    mem_ref[s, m, t, 2 * a].astype(f32) * taps[0] + mem_ref[s, m, t, 2 * a + 1].astype(f32) * taps[1]
                    for a in range(half)
                ]
                for a in range(half):
                    done = pair_reduce(parts[a], tiles.at[(t * half + a) % 4], jnp.add)
                    squeezed[m, s, a * frames * VH + t * VH : a * frames * VH + (t + 1) * VH, :] = done[0:VH]
            squeezed[m, s, count:LANE, :] = jnp.zeros((LANE - count, width), f32)
    for n in range(HEADS):
        cut = slice(n * hd, (n + 1) * hd)
        out_ref[n] = jnp.concatenate(
            [squeezed[0, 0, :, cut], squeezed[1, 0, :, cut], squeezed[0, 1, :, cut], squeezed[1, 1, :, cut]], axis=1
        ).astype(bf)
    cot = jnp.concatenate([cot_ref[t, a].astype(f32) for t in range(frames) for a in range(half)], axis=0)
    early_ref[:, 0:width] = cot.astype(bf)
    early_ref[:, width:] = mx_ref[...].astype(bf)


def flat_row(t, h):
    return GRID + (1 + t) * PLANE + h * GRID


def fill_grid(grid):
    zero = jnp.zeros((GRID, LANE), f32)
    grid[0 : GRID + PLANE, :] = jnp.zeros((GRID + PLANE, LANE), f32)
    grid[flat_row(FR, 0) :, :] = jnp.zeros((FLAT - flat_row(FR, 0), LANE), f32)
    for t in range(FR):
        grid[flat_row(t, VW) : flat_row(t, VW) + GRID, :] = zero


def taps9(w_ref, part):
    return [[[w_ref[(a * 3 + b) * 3 + c : (a * 3 + b) * 3 + c + 1, part * LANE : (part + 1) * LANE] for c in range(3)] for b in range(3)] for a in range(3)]


def four_rows(grid, weights, base, flip, keep=VW):
    acc = [[None] * 3 for _ in range(4)]
    for line in range(-1, 5):
        for a in range(3):
            shift = (1 - a if flip else a - 1) * PLANE + line * GRID
            cells = grid[pl.ds(pl.multiple_of(base + shift, 8), GRID), :]
            for h in range(4):
                b = (h - line + 1) if flip else (line - h + 1)
                if b < 0 or b > 2:
                    continue
                for c in range(3):
                    term = cells * weights[a][b][c]
                    acc[h][c] = term if acc[h][c] is None else acc[h][c] + term
    outs = []
    for h in range(4):
        left, mid, right = (acc[h][2], acc[h][1], acc[h][0]) if flip else (acc[h][0], acc[h][1], acc[h][2])
        outs.append((pltpu.roll(left, 1, 0) + mid + pltpu.roll(right, GRID - 1, 0))[0:keep])
    return jnp.concatenate(outs, axis=0)


def gather_blocks(dims, meta, refs, out, sems):
    frames, rows, n_height = dims
    member = meta[4]
    per = rows * GRID
    x0, x2, x4, x6a, x6b, x1, x3, x5, x7a, x7b = refs
    copies = []
    for d, parts in enumerate([[x0], [x1], [x2], [x3], [x4], [x5], [x6a, x6b], [x7a, x7b]]):
        src = member ^ d
        t = lax.div(src, n_height) * frames
        at = pl.ds(pl.multiple_of(lax.rem(src, n_height) * per, 16), per)
        for ref in parts:
            for i in range(ref.shape[0] // per):
                copies.append(pltpu.make_async_copy(ref.at[i * per : (i + 1) * per, :], out.at[t, at, :], sems.at[len(copies)]))
                t = t + 1
    return copies


def own_weights(meta, qkv_ref, out, sems):
    width, hd = qkv_ref.shape[0] // 3, out.shape[1]
    rows = [pl.ds(pl.multiple_of(p * width + meta[4] * hd, 32), hd) for p in range(3)]
    return [pltpu.make_async_copy(qkv_ref.at[rows[p], :], out.at[p], sems.at[p]) for p in range(3)]


def conv_kernel(dims, meta, w_ref, bias_ref, *refs):
    frames, rows, n_height, hd = dims
    half = rows // 2
    blocks, qkv_ref, (k_ref, v_ref, q_ref, mk, mv, gk, gv, gather, tiles, qrow, wide, sems, more) = refs[:10], refs[10], refs[11:]
    copies = own_weights(meta, qkv_ref, wide, more) + gather_blocks(dims[:3], meta, blocks, gather, sems)
    for copy in copies:
        copy.start()
    side = meta[0]
    channels = qkv_ref.shape[1]
    for grid in (gk, gv):
        fill_grid(grid)
    blank = jnp.zeros((LANE - hd, channels), bf)
    index = lax.broadcasted_iota(jnp.int32, (VW * GRID, 1), 0)
    line = (index * 2731) >> 16
    inside = ((line < side) & (index - line * GRID < side)).astype(f32)
    for copy in copies:
        copy.wait()
    weight_q = jnp.concatenate([wide[0], blank], axis=0)
    weight_kv = jnp.concatenate([wide[1], blank, wide[2], blank], axis=0)
    piece = half * HALF
    for t in range(FR):
        query = pair_reduce(join_lines(nt(gather[t], weight_q), jnp.add), tiles.at[t % 2], jnp.add) * 0.25 + bias_ref[0:1, 0:LANE]
        for h in range(n_height):
            at = (t // frames * n_height + h) * frames * piece + t % frames * piece
            qrow[at : at + piece, :] = query[h * piece : (h + 1) * piece]
        pair = ((nt(gather[t, 0 : VW * GRID, :], weight_kv) + bias_ref[0:1, LANE:]) * inside).astype(bf).astype(f32)
        gk[flat_row(t, 0) : flat_row(t, VW), :] = pair[:, 0:LANE]
        gv[flat_row(t, 0) : flat_row(t, VW), :] = pair[:, LANE:]
    q_ref[...] = qrow[...].astype(bf)
    sent = [pltpu.make_async_copy(gk, mk, more.at[3]), pltpu.make_async_copy(gv, mv, more.at[4])]
    for copy in sent:
        copy.start()
    local = lax.broadcasted_iota(jnp.int32, (4 * VW, LANE), 0)
    lane = lax.broadcasted_iota(jnp.int32, (4 * VW, LANE), 1)
    line = (local * 3277) >> 16
    column = local - line * VW
    fixed = [(lane + o == 143 - column) | (lane + o == 191 - column) for o in (0, LANE)]
    ones = (lane == hd).astype(f32)

    def step(it, carry):
        t = it // (VW // 4)
        quad = it % (VW // 4)
        base = GRID + (1 + t) * PLANE + quad * 4 * GRID
        out = pl.ds(pl.multiple_of(it * (4 * VW), 16), 4 * VW)
        mixed_k = four_rows(gk, taps9(w_ref, 0), base, False)
        mixed_v = four_rows(gv, taps9(w_ref, 1), base, False)
        h = quad * 4 + line
        bad = (h >= side) | (column >= side)
        for o in range(2):
            at = lane + o * LANE
            hit = fixed[o] | (at == 103 - t) | (at == 151 - t) | (at == 123 - h) | (at == 171 - h) | ((at == 192) & bad)
            marks = hit.astype(f32)
            k_ref[out, o * LANE : (o + 1) * LANE] = ((mixed_k + marks) if o == 0 else marks).astype(bf)
        v_ref[out, :] = (mixed_v + ones).astype(bf)
        return carry

    lax.fori_loop(0, FR * VW // 4, step, 0)
    for copy in sent:
        copy.wait()


def build_table(tab, t_ref, h_ref, w_ref):
    tab[...] = jnp.zeros(tab.shape, f32)
    for v in range(FR):
        tab[8 * v : 8 * v + FR, :] = t_ref[v : v + FR, :]
    for n, ref in ((0, h_ref), (1, w_ref)):
        for a in range(HALF):
            at = 8 * FR + (n * HALF + a) * GRID
            first = 2 * a + GRID - VW
            tab[at : at + VW, :] = ref[first : first + VW, :]


def attend_kernel(dims, meta, kc_ref, vc_ref, q_ref, y_ref, t_ref, h_ref, w_ref, place_ref, k_out, v_out, qt_ref, o_ref, l_ref, j_ref, vt, tab, k_ref, v_ref, sems):
    frames, rows, n_height, hd = dims
    half = rows // 2
    side, length = meta[0], meta[1]
    queries = q_ref.shape[0]
    scale = hd**-0.5
    k_ref[0:CUR, :] = kc_ref[...]
    v_ref[0:CUR, :] = vc_ref[...]
    count = half * frames * VH
    each = frames * VH
    lane1 = lax.broadcasted_iota(jnp.int32, (1, LANE), 1)
    at = CUR
    for src in range(HEADS):
        packed = y_ref[src].astype(f32)
        first = src % n_height * half
        used = min(max(VH - first, 0), half) * each
        if used > 0:
            halves = []
            for m in range(2):
                halves.append(jnp.concatenate([packed[0:used, m * hd : (m + 1) * hd], packed[0:used, (2 + m) * hd : (3 + m) * hd]], axis=0))
            index = lax.broadcasted_iota(jnp.int32, (2 * used, LANE), 0)
            step = (index >= used).astype(jnp.int32)
            inner = index - step * used
            a = (inner >= each).astype(jnp.int32) + (inner >= 2 * each).astype(jnp.int32)
            inner = inner - a * each
            c = inner - ((inner * 6554) >> 16) * VH
            bad = (step >= length) | (2 * (first + a) >= side) | (2 * c >= side)
            mark = (bad & (lax.broadcasted_iota(jnp.int32, (2 * used, LANE), 1) == 64)).astype(f32)
            k_ref[at : at + 2 * used, 0:LANE] = pad_lanes(halves[0], LANE).astype(bf)
            k_ref[at : at + 2 * used, LANE:] = mark.astype(bf)
            v_ref[at : at + 2 * used, :] = (pad_lanes(halves[1], LANE) + (lane1 == hd).astype(f32)).astype(bf)
            at += 2 * used
    rest = KEYS - at
    k_ref[at:, 0:LANE] = jnp.zeros((rest, LANE), bf)
    k_ref[at:, LANE:] = jnp.broadcast_to((lane1 == 64).astype(f32), (rest, LANE)).astype(bf)
    v_ref[at:, :] = jnp.zeros((rest, LANE), bf)
    for i in range(KEYS // 256):
        cut = slice(i * 256, (i + 1) * 256)
        vt[:, cut] = v_ref[cut, :].T
    sent = [pltpu.make_async_copy(k_ref, k_out, sems.at[0]), pltpu.make_async_copy(v_ref, v_out, sems.at[1])]
    for copy in sent:
        copy.start()
    pt = q_ref[...].astype(f32).T[0:hd]
    build_table(tab, t_ref, h_ref, w_ref)
    table = tab[...]
    coarse = table.astype(bf)
    turned = pt.astype(bf)
    along = nn(coarse, turned) + nn((table - coarse.astype(f32)).astype(bf), turned)
    tq, aq, cq = place_ref[0:1, :], place_ref[1:2, :], place_ref[2:3, :]
    part_t = jnp.zeros((FR, queries), f32)
    for v in range(FR):
        part_t = jnp.where(tq == v, along[8 * v : 8 * v + FR], part_t)
    parts = []
    for n, place in ((0, aq), (1, cq)):
        part = jnp.zeros((GRID, queries), f32)
        for a in range(HALF):
            row = 8 * FR + (n * HALF + a) * GRID
            part = jnp.where(place == a, along[row : row + GRID], part)
        parts.append(part[0:VW])
    bias = jnp.concatenate([part_t] + parts, axis=0) * hd**0.5
    high = bias.astype(bf)
    low = (bias - high.astype(f32)).astype(bf)
    qt_ref[0:hd, :] = pt.astype(bf)
    qt_ref[hd : hd + 48, :] = high
    qt_ref[hd + 48 : hd + 96, :] = low
    tail = lax.broadcasted_iota(jnp.int32, (64, queries), 0)
    qt_ref[192:256, :] = jnp.where(tail == 0, FAR, 0.0).astype(bf)
    factor = scale * LOG2E
    query = qt_ref[...]
    top = None
    for lo in range(0, KEYS, 1024):
        cut = slice(lo, min(lo + 1024, KEYS))
        scores = nn(k_ref[cut, :], query)
        here = jnp.max(scores.reshape(scores.shape[0] // 8, 8, queries), axis=0)
        here = jnp.max(here, axis=0, keepdims=True) * factor
        new = here if top is None else jnp.maximum(top, here)
        part = nn(vt[:, cut], jnp.exp2(scores * factor - new).astype(bf))
        total = part if top is None else total * jnp.exp2(top - new) + part
        top = new
    norm = total[hd : hd + 1]
    o_ref[...] = total[0:hd] / norm
    l_ref[...] = top + jnp.log2(norm)
    j_ref[...] = pad_lanes((o_ref[...] + pt).T, LANE).astype(bf)
    for copy in sent:
        copy.wait()


def turn_kernel(k_ref, kt_ref):
    for i in range(KEYS // 256):
        cut = slice(i * 256, (i + 1) * 256)
        kt_ref[0:LANE, cut] = k_ref[cut, 0:LANE].T
        kt_ref[LANE:BACK, cut] = k_ref[cut, LANE:].T[0 : BACK - LANE]


def mlp_kernel(dims, j_ref, early_ref, wp_ref, ws_ref, bp_ref, bs_ref, g_ref, b_ref, w1_ref, b1_ref, w2_ref, b2_ref,
               out_ref, keep_ref, act_ref, dj_ref, mg_ref,
               resid, n2, acc, ngrad, joined, gb1):
    width, hd = dims
    i = pl.program_id(0)
    per_q = early_ref.shape[0]
    block = w1_ref.shape[0]

    @pl.when(i == 0)
    def _():
        joined[...] = jnp.concatenate([j_ref[n][:, 0:hd] for n in range(HEADS)], axis=1)
        shift = row_of(bp_ref, 0, width) + row_of(bs_ref, 0, width)
        value = nt(joined[...], wp_ref[...]) + nt(early_ref[:, width:], ws_ref[...]) + shift
        resid[...] = value
        unit, _ = layer_unit(value)
        n2[...] = (unit * row_of(g_ref, 0, width) + row_of(b_ref, 0, width)).astype(bf)
        acc[...] = jnp.zeros(acc.shape, f32)
        ngrad[...] = jnp.zeros(ngrad.shape, f32)

    here = pl.ds(pl.multiple_of(i * block, LANE), block)
    hidden = nt(n2[...], w1_ref[...]) + b1_ref[here].reshape(1, block)
    gate = 0.5 * (1.0 + lax.erf(hidden * SQRT_HALF))
    act = (hidden * gate).astype(bf)
    each = act_ref.shape[2]
    for n in range(act_ref.shape[0]):
        act_ref[n, 0:per_q, :] = act[:, n * each : (n + 1) * each]
    acc[...] += nt(act, w2_ref[...])
    grad = nn(early_ref[:, 0:width], w2_ref[...])
    hgrad = (grad * (gate + hidden * jnp.exp(-0.5 * hidden * hidden) / ROOT_TWO_PI)).astype(bf)
    for n in range(act_ref.shape[0]):
        act_ref[n, per_q:, :] = hgrad[:, n * each : (n + 1) * each]
    gb1[:, here] = jnp.sum(hgrad.astype(f32), axis=0, keepdims=True)
    ngrad[...] += nn(hgrad, w1_ref[...])

    @pl.when(i == pl.num_programs(0) - 1)
    def _():
        value = resid[...]
        result = value + acc[...] + row_of(b2_ref, 0, width)
        for t in range(out_ref.shape[0]):
            for a in range(out_ref.shape[1]):
                at = (t * out_ref.shape[1] + a) * HALF
                out_ref[t, a] = result[at : at + HALF].astype(bf)
        unit, inverse = layer_unit(value)
        cot = early_ref[:, 0:width].astype(f32)
        grad = ngrad[...]
        scaled = grad * row_of(g_ref, 0, width)
        back = inverse * (
            scaled - jnp.mean(scaled, axis=-1, keepdims=True) - unit * jnp.mean(scaled * unit, axis=-1, keepdims=True)
        )
        low = (cot + back).astype(bf)
        keep_ref[:, 0:width] = n2[...]
        keep_ref[:, width:] = low
        joined_grad = nn(low, wp_ref[...])
        mg_ref[...] = nn(low, ws_ref[...])
        sums = [jnp.sum(v, axis=0, keepdims=True) for v in (low.astype(f32), grad * unit, grad, cot)] + [gb1[...]]
        flat = [v[:, k : k + width] for v in sums for k in range(0, v.shape[1], width)]
        spare = LANE - hd
        for n in range(HEADS):
            exact = jnp.concatenate([flat[n][:, k : k + spare] for k in range(0, width, spare)], axis=0)
            high = exact.astype(bf).astype(f32)
            side = jnp.concatenate([high, exact - high, jnp.zeros((per_q - 2 * exact.shape[0], spare), f32)], axis=0)
            dj_ref[n] = jnp.concatenate([joined_grad[:, n * hd : (n + 1) * hd], side], axis=1).astype(bf)


def attend_back_kernel(dims, qt_ref, q_ref, o_ref, l_ref, dj_ref, t_ref, h_ref, w_ref, place_ref, k_in, kt_in, v_in,
                       dk_ref, dv_ref, mem_ref, pq_ref, small_ref,
                       dot_ref, dq, tab, dtab, dks, dvs, delta, tables, k_ref, kt_ref, v_ref, sems):
    frames, rows, n_height, hd = dims
    half = rows // 2
    queries = q_ref.shape[0]
    scale = hd**-0.5
    factor = scale * LOG2E
    turned = dj_ref[...].astype(f32).T
    half_keys = KEYS // 2

    def brought(i):
        cut = pl.ds(pl.multiple_of(i * half_keys, LANE), half_keys)
        return [
            pltpu.make_async_copy(k_in.at[cut, :], k_ref.at[cut, :], sems.at[0, i]),
            pltpu.make_async_copy(v_in.at[cut, :], v_ref.at[cut, :], sems.at[1, i]),
            pltpu.make_async_copy(kt_in.at[:, cut], kt_ref.at[:, cut], sems.at[2, i]),
        ]

    for copy in brought(0) + brought(1):
        copy.start()
    per_q = queries // HEADS
    spare = jnp.zeros((per_q, LANE - hd), f32)
    for src in range(HEADS):
        spare = spare + dj_ref[src * per_q : (src + 1) * per_q, hd:].astype(f32)
    lines = small_ref.shape[0]
    small_ref[...] = spare[0:lines] + spare[lines : 2 * lines]
    dot_ref[0:hd, :] = turned[0:hd].astype(bf)
    dot_ref[hd:, :] = jnp.zeros((LANE - hd, queries), bf)
    delta[...] = jnp.sum(turned[0:hd] * o_ref[...], axis=0, keepdims=True)
    dq[...] = jnp.zeros(dq.shape, f32)
    def chunk(i, carry):
        cut = pl.ds(pl.multiple_of(i * half_keys, LANE), half_keys)
        for copy in brought(i):
            copy.wait()
        shares = jnp.exp2(nn(k_ref[cut, :], qt_ref[...]) * factor - l_ref[...])
        slope = nn(v_ref[cut, :], dot_ref[...])
        score = (shares * (slope - delta[...])).astype(bf)
        dvs[cut, :] = nn(shares.astype(bf), dj_ref[...])
        dks[cut, :] = nn(score, q_ref[...]) * scale
        dq[...] += nn(kt_ref[:, cut], score)
        return carry

    lax.fori_loop(0, 2, chunk, 0)
    sent = [
        pltpu.make_async_copy(dks.at[0:CUR, :], dk_ref, sems.at[3, 0]),
        pltpu.make_async_copy(dvs.at[0:CUR, :], dv_ref, sems.at[3, 1]),
    ]
    for copy in sent:
        copy.start()
    each = frames * VH
    at = CUR
    for dst in range(HEADS):
        first = dst % n_height * half
        used = min(max(VH - first, 0), half) * each
        if used > 0:
            parts = [ref[at + s * used : at + (s + 1) * used, 0:hd] for s in range(MEM) for ref in (dks, dvs)]
            packed = jnp.concatenate(parts, axis=1)
            at += 2 * used
        if used < LANE:
            zero = jnp.zeros((LANE - used, 4 * hd), f32)
            packed = jnp.concatenate([packed, zero], axis=0) if used > 0 else zero
        mem_ref[dst, 0:LANE, :] = packed.astype(bf)
    build_table(tab, t_ref, h_ref, w_ref)
    tq, aq, cq = place_ref[0:1, :], place_ref[1:2, :], place_ref[2:3, :]
    grad_t = dq[hd : hd + FR, :]
    for v in range(FR):
        dtab[8 * v : 8 * v + FR, :] = jnp.where(tq == v, grad_t, 0.0)
    for n, place in ((0, aq), (1, cq)):
        part = jnp.concatenate(
            [dq[hd + FR + n * VW : hd + FR + (n + 1) * VW, :], jnp.zeros((GRID - VW, queries), f32)], axis=0
        )
        for a in range(HALF):
            row = 8 * FR + (n * HALF + a) * GRID
            dtab[row : row + GRID, :] = jnp.where(place == a, part, 0.0)
    spread = dtab[...].astype(bf)
    pooled_grad = dq[0:hd, :] * scale + tn(tab[...].astype(bf), spread) + dot_ref[0:hd, :].astype(f32)
    pq_ref[...] = pad_lanes(pooled_grad.T * 0.25, LANE)
    grads = nn(spread, q_ref[...])
    tables[...] = jnp.zeros(tables.shape, f32)
    for v in range(FR):
        tables[v : v + FR, :] += grads[8 * v : 8 * v + FR]
    for n in range(2):
        for a in range(HALF):
            row = 8 * FR + (n * HALF + a) * GRID
            first = 2 * FR + n * 2 * GRID + 2 * a + GRID - VW
            tables[first : first + VW, :] += grads[row : row + VW]
    share = TABLE_ROWS // HEADS
    for dst in range(HEADS):
        part = jnp.concatenate([tables[dst * share : (dst + 1) * share, :], jnp.zeros((16 - share, LANE), f32)], axis=0)
        high = part.astype(bf).astype(f32)
        mem_ref[dst, LANE:, :] = jnp.concatenate([high, part - high, jnp.zeros((16, LANE), f32)], axis=1).astype(bf)
    for copy in sent:
        copy.wait()


def conv_back_kernel(dims, meta, dk_ref, dv_ref, pq_ref, w_ref, g_ref, b_ref, *refs):
    frames, rows, n_height, hd = dims
    half = rows // 2
    blocks, qkv_ref, (out_ref, stat_ref, pg, gk, gv, wide, gather, tall, own, sems, more) = refs[:10], refs[10], refs[11:]
    copies = gather_blocks(dims[:3], meta, blocks, gather, sems) + own_weights(meta, qkv_ref, own, more)
    for copy in copies:
        copy.start()
    side = meta[0]
    channels = qkv_ref.shape[1]
    for grid in (gk, gv):
        fill_grid(grid)
    for ref, grid in ((dk_ref, gk), (dv_ref, gv)):
        for t in range(FR):
            for h in range(VW):
                at = (t * VW + h) * VW
                grid[flat_row(t, h) : flat_row(t, h) + GRID, :] = jnp.concatenate(
                    [ref[at : at + VW, :], jnp.zeros((GRID - VW, LANE), f32)], axis=0
                )
    local = lax.broadcasted_iota(jnp.int32, (4 * GRID, 1), 0)
    line = (local * 2731) >> 16
    column = local - line * GRID
    empty = jnp.zeros(((GRID - VW) * GRID, 2 * LANE), bf)
    for t in range(FR):
        pg[t * GRID * GRID + VW * GRID : (t + 1) * GRID * GRID, LANE:] = empty

    def step(it, carry):
        t = it // (VW // 4)
        quad = it % (VW // 4)
        base = GRID + (1 + t) * PLANE + quad * 4 * GRID
        out = pl.ds(pl.multiple_of((t * GRID + quad * 4) * GRID, 32), 4 * GRID)
        inside = ((quad * 4 + line < side) & (column < side)).astype(f32)
        for m, grid in ((0, gk), (1, gv)):
            back = four_rows(grid, taps9(w_ref, m), base, True, GRID)
            pg[out, (1 + m) * LANE : (2 + m) * LANE] = (back * inside).astype(bf)
        return carry

    lax.fori_loop(0, FR * VW // 4, step, 0)
    queries = pq_ref.shape[0]
    wide[pl.ds(0, queries, 2), :] = pq_ref[...]
    wide[pl.ds(1, queries, 2), :] = pq_ref[...]
    per_q = queries // HEADS
    for src in range(HEADS):
        for t in range(frames):
            for a in range(half):
                at = ((src * frames + t) * half + a) * GRID
                lines = wide[at : at + GRID, :]
                row = ((src // n_height * frames + t) * GRID + src % n_height * rows + 2 * a) * GRID
                pg[row : row + 2 * GRID, 0:LANE] = jnp.concatenate([lines, lines], axis=0).astype(bf)
    span = rows * VW
    cells = span * (frames // 2)
    third = per_q // 3
    for dst in range(HEADS):
        first = dst % n_height * rows
        lines = []
        for t2 in range(frames // 2):
            parts = []
            for g in range(2):
                t = dst // n_height * frames + g * (frames // 2) + t2
                at = (t * GRID + first) * GRID
                block = pg[at : at + rows * GRID, LANE:].astype(f32)
                block = jnp.concatenate([block[h * GRID : h * GRID + VW] for h in range(rows)], axis=0)
                parts += [block[:, 0:hd], block[:, LANE : LANE + hd]]
            lines.append(jnp.concatenate(parts, axis=1))
        out_ref[dst, 0:cells, :] = jnp.concatenate(lines, axis=0).astype(bf)
        out_ref[dst, cells : cells + third, :] = jnp.concatenate(
            [pq_ref[dst * per_q + i * third : dst * per_q + (i + 1) * third, :] for i in range(3)], axis=1
        ).astype(bf)
    for copy in copies:
        copy.wait()
    total = jnp.zeros((3 * LANE, channels), f32)
    sums = jnp.zeros((1, 3 * LANE), f32)
    for t in range(FR):
        part = pg[t * GRID * GRID : (t + 1) * GRID * GRID, :]
        total = total + tn(part, gather[t])
        sums = sums + jnp.sum(part.astype(f32), axis=0, keepdims=True)
    total = jnp.concatenate([total[p * LANE : p * LANE + hd] for p in range(3)], axis=0)
    sums = jnp.concatenate([sums[:, p * LANE : p * LANE + hd] for p in range(3)], axis=1)
    cols = channels // HEADS
    packed = 3 * hd // HEADS
    rest = out_ref.shape[1] - cells - third
    for n in range(HEADS):
        value = pack_rows(total[:, n * cols : (n + 1) * cols], tall.at[n % 2], HEADS)
        out_ref[n, cells + third :, :] = jnp.concatenate([value, jnp.zeros((rest - packed, channels), f32)], axis=0).astype(bf)
    weight = jnp.concatenate([own[p].astype(f32) for p in range(3)], axis=0)
    shift = nn(jnp.broadcast_to(sums, (8, 3 * hd)), weight, precision=HI)[0:1]
    gain = jnp.sum(total * weight, axis=0, keepdims=True)
    gain = (gain - shift * row_of(b_ref, 0, channels)) / row_of(g_ref, 0, channels)
    stat_ref[0:1, :] = pad_lanes(sums, channels)
    stat_ref[1:2, :] = gain
    stat_ref[2:3, :] = shift
    stat_ref[3:8, :] = jnp.zeros((5, channels), f32)


def gather_rows(meta, refs, out, sems):
    x0, x2, x4, x6a, x6b, x1, x3, x5, x7a, x7b = refs
    copies = []
    for d, parts in enumerate([[x0], [x1], [x2], [x3], [x4], [x5], [x6a, x6b], [x7a, x7b]]):
        at = (meta[4] ^ d) * (out.shape[0] // HEADS)
        for ref in parts:
            size = ref.shape[0]
            copies.append(pltpu.make_async_copy(ref, out.at[pl.ds(pl.multiple_of(at, 16), size), :], sems.at[len(copies)]))
            at = at + size
    return copies


def weight_grad_kernel(dims, meta, ah_ref, j_ref, dmem_ref, *refs):
    width, hd, channels, per_q = dims
    early, kept = refs[:10], refs[10:20]
    fc2_ref, fc1_ref, proj_ref, short_ref, act, hgrad, tall, parts, cot_ref, keep_ref, sems = refs[20:]
    member = meta[4]
    first = gather_rows(meta, early, cot_ref, sems.at[0])
    second = gather_rows(meta, kept, keep_ref, sems.at[1])
    for copy in first + second:
        copy.start()
    for src in range(HEADS):
        cut = slice(src * per_q, (src + 1) * per_q)
        act[cut, :] = ah_ref[src, 0:per_q, :]
        hgrad[cut, :] = ah_ref[src, per_q:, :]
    for copy in first:
        copy.wait()
    fc2_ref[...] = tn(cot_ref[:, 0:width], act[...]).astype(bf)
    for copy in second:
        copy.wait()
    normed = keep_ref[:, 0:width]
    resid = keep_ref[:, width : 2 * width]
    fc1 = tn(hgrad[...], normed)
    for n in range(HEADS):
        fc1_ref[n, 0 : dmem_ref.shape[1], :] = dmem_ref[n]
        fc1_ref[n, dmem_ref.shape[1] :, :] = pack_rows(fc1[:, n * hd : (n + 1) * hd], parts.at[n % 2], channels // hd).astype(bf)
    cols = channels // HEADS
    lane = lax.broadcasted_iota(jnp.int32, (channels, LANE), 1)
    pick = (lax.broadcasted_iota(jnp.int32, (channels, LANE), 0) == lane + member * cols) & (lane < cols)
    maxima = nn(cot_ref[:, width:], pick.astype(f32).astype(bf)).astype(bf)
    both = tn(resid, jnp.concatenate([j_ref[...], maxima], axis=1))
    proj_ref[...] = pack_rows(both[:, 0:hd], tall.at[0], channels // hd).astype(bf)
    short_ref[...] = pack_rows(both[:, LANE : LANE + cols], tall.at[1], channels // cols).astype(bf)


def last_kernel(dims, x_ref, g_ref, mx_ref, mg_ref, w_in, pg_in, out_ref, full, tiles, w_ref, pg_ref, sems):
    frames, rows, width, hd = dims
    half = rows // 2
    cells = rows * VW * (frames // 2)
    third = frames * half * HALF // 3
    channels = x_ref.shape[1]
    rows_in = pg_ref.shape[1]
    copies = [pltpu.make_async_copy(w_in, w_ref, sems.at[HEADS])]
    copies += [pltpu.make_async_copy(pg_in.at[n, 0:rows_in, :], pg_ref.at[n], sems.at[n]) for n in range(HEADS)]
    for copy in copies:
        copy.start()
    copies[0].wait()
    tops = jnp.zeros((cells, channels), f32)
    lows = jnp.zeros((cells, channels), f32)
    queries = []
    for n in range(HEADS):
        weight = jnp.concatenate(
            [w_ref[width + n * hd : width + (n + 1) * hd, :], w_ref[2 * width + n * hd : 2 * width + (n + 1) * hd, :]], axis=0
        )
        copies[1 + n].wait()
        packed = pg_ref[n]
        tops = tops + nn(packed[0:cells, 0 : 2 * hd], weight)
        lows = lows + nn(packed[0:cells, 2 * hd :], weight)
        queries.append(
            jnp.concatenate([packed[cells : cells + third, i * LANE : i * LANE + hd] for i in range(3)], axis=0)
        )
    for part, value in ((0, tops), (1, lows)):
        for line in range(frames // 2 * rows):
            at = (part * (frames // 2) * rows + line) * GRID
            full[at : at + GRID, :] = jnp.concatenate(
                [value[line * VW : (line + 1) * VW], jnp.zeros((GRID - VW, channels), f32)], axis=0
            )
    query = nn(jnp.concatenate(queries, axis=1), w_ref[0:width, :])
    per = rows * GRID
    per_q = half * HALF
    g = row_of(g_ref, 0, channels)
    for t in range(frames):
        cut = slice(t * per_q, (t + 1) * per_q)
        x = x_ref[t * per : (t + 1) * per, :].astype(f32)

        def spread(value):
            wide = pair_spread(value, tiles)
            lines = []
            for a in range(half):
                lines += [wide[a * GRID : (a + 1) * GRID]] * 2
            return jnp.concatenate(lines, axis=0)

        grad = full[t * per : (t + 1) * per, :] + spread(query[cut])
        hits = (x == spread(mx_ref[cut, :])).astype(f32)
        sums = jnp.concatenate(
            [hits[2 * a * GRID : (2 * a + 1) * GRID] + hits[(2 * a + 1) * GRID : (2 * a + 2) * GRID] for a in range(half)], axis=0
        )
        number = pair_reduce(sums, tiles, jnp.add)
        pool = hits * spread(mg_ref[cut, :] / number)
        unit, inverse = layer_unit(x)
        scaled = grad * g
        back = inverse * (
            scaled - jnp.mean(scaled, axis=-1, keepdims=True) - unit * jnp.mean(scaled * unit, axis=-1, keepdims=True)
        )
        out_ref[t * per : (t + 1) * per, :] = (back + pool).astype(bf)


def conv_grad_kernel(hd, mk_in, mv_in, dk_in, dv_in, out_ref, acc, mk, mv, dks, dvs, sems):
    groups = FR // 2
    lead = GRID + 4 * PLANE

    def brought(g, first):
        if first:
            cut = pl.ds(0, lead)
        else:
            cut = pl.ds(pl.multiple_of(lead + (g - 1) * 2 * PLANE, 8), 2 * PLANE)
        rows = pl.ds(pl.multiple_of(g * (CUR // groups), 16), CUR // groups)
        pairs = [(mk_in, mk, cut), (mv_in, mv, cut), (dk_in, dks, rows), (dv_in, dvs, rows)]
        return [pltpu.make_async_copy(a.at[c, :], b.at[c, :], sems.at[i, g]) for i, (a, b, c) in enumerate(pairs)]

    for g in range(groups):
        for copy in brought(g, g == 0):
            copy.start()
    acc[...] = jnp.zeros(acc.shape, f32)
    blank = jnp.zeros((GRID - VW, LANE), f32)

    def step(it, carry):
        t = it // (VW // 4)
        base = GRID + (1 + t) * PLANE + it % (VW // 4) * 4 * GRID
        for m, ref, masked in ((0, dks, mk), (1, dvs, mv)):
            quad = ref[pl.ds(pl.multiple_of(it * (4 * VW), 16), 4 * VW), :]
            for h in range(4):
                here = jnp.concatenate([quad[h * VW : (h + 1) * VW], blank], axis=0)
                turned = [pltpu.roll(here, GRID - 1, 0), here, pltpu.roll(here, 1, 0)]
                for a in range(3):
                    for b in range(3):
                        cells = masked[pl.ds(pl.multiple_of(base + (a - 1) * PLANE + (h + b - 1) * GRID, 8), GRID), :]
                        for c in range(3):
                            prod = cells * turned[c]
                            acc[m * 27 + (a * 3 + b) * 3 + c] += prod[0:8] + prod[8:16] + prod[16:24]
        return carry

    def group(g, carry):
        @pl.when(g == 0)
        def _():
            for copy in brought(0, True):
                copy.wait()

        @pl.when(g > 0)
        def _():
            for copy in brought(g, False):
                copy.wait()

        each = 2 * VW // 4
        return lax.fori_loop(g * each, (g + 1) * each, step, carry)

    lax.fori_loop(0, groups, group, 0)
    sums = [jnp.sum(acc[tap], axis=0, keepdims=True) for tap in range(54)] + [jnp.zeros((1, LANE), f32)] * 2
    sums = jnp.concatenate(sums, axis=0)
    out_ref[0:14, :] = jnp.concatenate([sums[14 * g : 14 * (g + 1), 0:hd] for g in range(4)], axis=1)
    out_ref[14:16, :] = jnp.zeros((2, 4 * hd), f32)


def late_kernel(dims, conv_ref, stat_ref, small_ref, mem_in, p_in, late_ref, tiles, lines, mem_ref, p_ref, sems):
    frames, rows, width, hd = dims
    half = rows // 2
    channels = late_ref.shape[1]
    first = pltpu.make_async_copy(p_in.at[:, 0 : p_ref.shape[1], :], p_ref, sems.at[2 * MEM])
    copies = [pltpu.make_async_copy(mem_in.at[s, m], mem_ref.at[s, m], sems.at[m * MEM + s]) for m in range(2) for s in range(MEM)]
    for copy in [first] + copies:
        copy.start()
    first.wait()
    for m in range(2):
        sums = [jnp.zeros((GRID, width), f32) for _ in range(2)]
        for s in range(MEM):
            copies[m * MEM + s].wait()
            grads = jnp.concatenate(
                [p_ref[n][0:LANE, (2 * s + m) * hd : (2 * s + m + 1) * hd] for n in range(HEADS)], axis=1
            ).astype(f32)
            for t in range(frames):
                for a in range(half):
                    at = (a * frames + t) * VH
                    some = jnp.concatenate([grads[at : at + VH], jnp.zeros((HALF - VH, width), f32)], axis=0)
                    wide = pair_spread(some, tiles.at[(t * half + a) % 4])
                    for i in range(2):
                        sums[i] = sums[i] + mem_ref[s, m, t, 2 * a + i].astype(f32) * wide
        odd = (lax.broadcasted_iota(jnp.int32, (GRID, 1), 0) % 2 == 1).astype(f32)
        for i in range(2):
            for j, keep in ((0, 1.0 - odd), (1, odd)):
                done = jnp.sum(sums[i] * keep, axis=0, keepdims=True)
                for k in range(width // channels):
                    at = LATE_COMP + 8 * k + 4 * m + 2 * i + j
                    lines[at : at + 1, :] = done[:, k * channels : (k + 1) * channels]
    lines[0:14, :] = conv_ref[0:14, :]
    lines[14:17, :] = stat_ref[0:3, :]
    count = small_ref.shape[0] // 2
    for k in range(2):
        lines[LATE_SMALL + k : LATE_SMALL + k + 1, :] = jnp.concatenate(
            [small_ref[k * count + i : k * count + i + 1, :] for i in range(count)], axis=1
        )
    tables = jnp.zeros((16, LANE), f32)
    for n in range(HEADS):
        part = p_ref[n][LANE : LANE + 16, :].astype(f32)
        tables = tables + part[:, 0:LANE] + part[:, LANE : 2 * LANE]
    lines[LATE_TABLE : LATE_TABLE + 5, :] = jnp.concatenate([tables[5 * g : 5 * (g + 1), :] for g in range(3)], axis=1)
    late_ref[...] = lines[...].astype(bf)


def add_four(got, lo, hi):
    a, b, c, d = [v[lo:hi, :].astype(f32) for v in got]
    return (a + b) + (c + d)


def unpack_rows(value, rows, lanes):
    groups = value.shape[1] // lanes
    for g in range(groups):
        rows[pl.ds(g, value.shape[0], groups), :] = pad_lanes(value[:, g * lanes : (g + 1) * lanes], LANE)


def second_kernel(dims, *refs):
    hd, cols, channels = dims
    got, (fc2_ref, proj_ref, short_ref, rows) = refs[0:4], refs[4:]
    count = proj_ref.shape[0]
    ends = np.cumsum([0, fc2_ref.shape[0], count * hd // channels, count * cols // channels])
    fc2_ref[...] = add_four(got, ends[0], ends[1])
    unpack_rows(add_four(got, ends[1], ends[2]), rows, hd)
    proj_ref[...] = rows[0:count, 0:hd]
    unpack_rows(add_four(got, ends[2], ends[3]), rows, cols)
    short_ref[...] = rows[...].T[0:cols, 0:count]


def first_kernel(hd, *refs):
    got, (fc1_ref, rows) = refs[0:4], refs[4:]
    unpack_rows(add_four(got, 0, got[0].shape[0]), rows, hd)
    fc1_ref[...] = rows[...].T[0:hd]


def sums_kernel(dims, late_ref, g1_ref, b1_ref, bqkv_ref, conv_ref, comp_ref, t_ref, h_ref, w_ref, bp_ref, bs_ref, g2_ref, b2_ref, bf1_ref, bf2_ref, lines):
    width, hd, channels = dims
    parts = []
    for n in range(HEADS):
        parts.append(late_ref[n])
    total = parts[0]
    for n in range(1, HEADS):
        total = total + parts[n]
    for g in range(4):
        conv = jnp.concatenate([parts[n][0:14, g * hd : (g + 1) * hd] for n in range(HEADS)], axis=1)
        for r in range(14):
            i = 14 * g + r
            if i < 54:
                conv_ref[i % 27 // 9, i % 9 // 3, i % 3, i // 27 : i // 27 + 1, :] = conv[r : r + 1]
    for p in range(3):
        value = jnp.concatenate([parts[n][14:15, p * hd : (p + 1) * hd] for n in range(HEADS)], axis=1)
        bqkv_ref[p * width : (p + 1) * width] = value.reshape(width)
    g1_ref[...] = total[15:16].reshape(channels)
    b1_ref[...] = total[16:17].reshape(channels)
    for i in range(8):
        value = jnp.concatenate([total[LATE_COMP + 8 * k + i : LATE_COMP + 8 * k + i + 1] for k in range(2)], axis=1)
        comp_ref[i // 4, i % 4 // 2, i % 2 : i % 2 + 1, :] = value
    for n in range(HEADS):
        value = jnp.concatenate([parts[n][LATE_SMALL + k : LATE_SMALL + k + 1] for k in range(2)], axis=1).reshape(width)
        if n == 0:
            bp_ref[...] = value
            bs_ref[...] = value
        elif n < 4:
            (g2_ref, b2_ref, bf2_ref)[n - 1][...] = value
        else:
            bf1_ref[(n - 4) * width : (n - 3) * width] = value
    share = TABLE_ROWS // HEADS
    for n in range(HEADS):
        part = parts[n][LATE_TABLE : LATE_TABLE + 5]
        value = jnp.concatenate([part[:, g * LANE : (g + 1) * LANE] for g in range(3)], axis=0)
        lines[n * share : (n + 1) * share, :] = value[0:share]
    at = 0
    for ref, step in ((t_ref, 2 * FR), (h_ref, 2 * GRID), (w_ref, 2 * GRID)):
        ref[...] = lines[at : at + ref.shape[0], 0:hd]
        at += step


def tail_kernel(dims, sums_dims, four, *refs):
    ins, refs = refs[: 7 + four], refs[7 + four :]
    x, gain, mx, mg, late = ins[0:5]
    got, (w_in, pg_in) = ins[5 : 5 + four], ins[5 + four :]
    outs, refs = refs[: 15 + four // 4], refs[15 + four // 4 :]
    full, tiles, w_ref, pg_ref, sems, lines = refs[:6]
    last_kernel(dims, x, gain, mx, mg, w_in, pg_in, outs[0], full, tiles, w_ref, pg_ref, sems)
    sums_kernel(sums_dims, late, *outs[1:15], lines)
    if four:
        first_kernel(sums_dims[1], *got, outs[15], refs[6])


def body(clip_input, memory, mem_len, res_id, norm1_gain, norm1_bias, w_qkv, b_qkv, conv_kv, compress, rel_t, rel_h, rel_w,
         w_proj, b_proj, w_short, b_short, norm2_gain, norm2_bias, w_fc1, b_fc1, w_fc2, b_fc2, cotangent):
    _, frames, rows, grid, channels = clip_input.shape
    width = w_proj.shape[0]
    mlp = w_fc1.shape[0]
    hd = width // HEADS
    half = rows // 2
    n_clip = lax.axis_size("clip")
    n_height = lax.axis_size("height")
    tm, height = lax.axis_index("tm"), lax.axis_index("height")
    member = tm * n_height + height
    side = SIDE_SMALL + (SIDE_BIG - SIDE_SMALL) * res_id[0]
    meta = jnp.stack([side, mem_len[0], tm, height, member]).astype(jnp.int32)
    cells_all = frames * rows * GRID
    valid = frames * rows * VW
    per_q = frames * half * HALF
    third = per_q // 3
    queries = HEADS * per_q
    x = clip_input.reshape(cells_all, channels)
    mem = memory[0]

    dims = (frames, rows, width, hd)
    n1, mx = call(
        functools.partial(norm_kernel, (frames, rows)),
        (shape((cells_all, channels), bf), shape((per_q, channels), f32)),
        (x, norm1_gain, norm1_bias),
        scratch=[pltpu.VMEM((channels // LANE, rows * GRID, LANE), f32)],
        smem=0,
        us=3,
    )

    def swap(value, bit):
        if bit == 4:
            return lax.ppermute(value, "tm", [(i, i ^ 1) for i in range(lax.axis_size("tm"))])
        return lax.ppermute(value, "height", [(i, i ^ bit) for i in range(n_height)])

    def near(value):
        return swap(value, 2), swap(value, 4), swap(value, 1)

    def across(x2, x4, cut):
        return swap(x2[:cut], 4), swap(x4[cut:], 2), swap(x2, 1), swap(x4, 1)

    def last(x6a, x6b):
        return swap(x6a, 1), swap(x6b, 1)

    x2, x4, x1 = near(n1)
    pay2, early = call(
        functools.partial(squeeze_kernel, dims),
        (shape((HEADS, LANE, 4 * hd), bf), shape((per_q, width + channels), bf)),
        (mem, compress, cotangent[0], mx),
        scratch=[pltpu.VMEM((4, width // LANE, GRID, LANE), f32), pltpu.VMEM((2, MEM, LANE, width), f32)],
        smem=0,
        us=5,
    )
    x2, x4, pay2 = lax.optimization_barrier((x2, x4, pay2))
    x6a, x6b, x3, x5 = across(x2, x4, cells_all // 2)
    x7a, x7b = last(x6a, x6b)
    y2 = lax.all_to_all(pay2, G, 0, 0, tiled=True)
    early, x7a = lax.optimization_barrier((early, x7a))
    e2, e4, e1 = near(early)
    cut = -(-per_q // 32) * 16
    taps = lax.dynamic_slice_in_dim(conv_kv.reshape(2, 27, width), member * hd, hd, 2)
    taps = jnp.pad(taps, ((0, 0), (0, 5), (0, LANE - hd)))
    taps = jnp.concatenate([taps[0], taps[1]], axis=1)
    hdims = (frames, rows, n_height, hd)
    bias = lax.dynamic_slice_in_dim(b_qkv.reshape(3, width), member * hd, hd, 1)
    bias = jnp.pad(bias, ((0, 0), (0, LANE - hd))).reshape(1, 3 * LANE)
    vmem = pl.BlockSpec(memory_space=pltpu.VMEM)
    blocks = (n1, x2, x4, x6a, x6b, x1, x3, x5, x7a, x7b)
    kc, vc, q_all, mk, mv = pl.pallas_call(
        functools.partial(conv_kernel, hdims),
        out_shape=(
            shape((CUR, 2 * LANE), bf),
            shape((CUR, LANE), bf),
            shape((queries, LANE), bf),
            shape((FLAT, LANE), f32),
            shape((FLAT, LANE), f32),
        ),
        in_specs=[pl.BlockSpec(memory_space=pltpu.SMEM)] + [vmem] * 2 + [pl.BlockSpec(memory_space=pl.ANY)] * 11,
        out_specs=(vmem,) * 3 + (pl.BlockSpec(memory_space=pl.ANY),) * 2,
        scratch_shapes=[
            pltpu.VMEM((FLAT, LANE), f32),
            pltpu.VMEM((FLAT, LANE), f32),
            pltpu.VMEM((FR, GRID * GRID, channels), bf),
            pltpu.VMEM((2, 1, GRID * HALF, LANE), f32),
            pltpu.VMEM((queries, LANE), f32),
            pltpu.VMEM((3, hd, channels), bf),
            pltpu.SemaphoreType.DMA((HEADS * frames,)),
            pltpu.SemaphoreType.DMA((5,)),
        ],
        compiler_params=pltpu.CompilerParams(vmem_limit_bytes=56 << 20),
        cost_estimate=cost(18),
    )(meta, taps, bias, *blocks, w_qkv)
    index = np.arange(queries)
    src, local = index // per_q, index % per_q
    place = np.zeros((8, queries), np.int32)
    place[0] = src // n_height * frames + local // (half * HALF)
    place[1] = src % n_height * half + local // HALF % half
    place[2] = local % HALF
    place = jnp.asarray(place)
    wide = 384
    kc, e2, e4, e1 = lax.optimization_barrier((kc, e2, e4, e1))
    e6a, e6b, e3, e5 = across(e2, e4, cut)
    k_all, v_all, qt_all, o_all, l_all, joined = call(
        functools.partial(attend_kernel, hdims),
        (
            shape((KEYS, 2 * LANE), bf),
            shape((KEYS, LANE), bf),
            shape((2 * LANE, queries), bf),
            shape((hd, queries), f32),
            shape((1, queries), f32),
            shape((queries, LANE), bf),
        ),
        (meta, kc, vc, q_all, y2, rel_t, rel_h, rel_w, place),
        scratch=[
            pltpu.VMEM((LANE, KEYS), bf),
            pltpu.VMEM((TAB, hd), f32),
            pltpu.VMEM((KEYS, 2 * LANE), bf),
            pltpu.VMEM((KEYS, LANE), bf),
            pltpu.SemaphoreType.DMA((2,)),
        ],
        us=16,
        away=(0, 1),
    )
    joined_rows = lax.all_to_all(joined.reshape(HEADS, per_q, LANE), G, 0, 0, tiled=True)
    k_all, joined_rows = lax.optimization_barrier((k_all, joined_rows))
    kt_all = call(turn_kernel, shape((BACK, KEYS), bf), (k_all,), smem=0, us=4)
    block = mlp // HEADS
    whole = lambda *dims: pl.BlockSpec(dims, lambda i: (0,) * len(dims))
    keep_width = 2 * width
    output, keep, acthg, dj, max_grad = pl.pallas_call(
        functools.partial(mlp_kernel, (width, hd)),
        grid=(HEADS // STEP,),
        out_shape=(
            shape((frames, half, HALF, width), bf),
            shape((per_q, keep_width), bf),
            shape((HEADS, 2 * per_q, block), bf),
            shape((HEADS, per_q, LANE), bf),
            shape((per_q, channels), f32),
        ),
        in_specs=[
            whole(HEADS, per_q, LANE),
            whole(per_q, width + channels),
            whole(width, width),
            whole(width, channels),
            whole(width),
            whole(width),
            whole(width),
            whole(width),
            pl.BlockSpec((STEP * block, width), lambda i: (i, 0)),
            whole(mlp),
            pl.BlockSpec((width, STEP * block), lambda i: (0, i)),
            whole(width),
        ],
        out_specs=(
            whole(frames, half, HALF, width),
            whole(per_q, keep_width),
            pl.BlockSpec((STEP, 2 * per_q, block), lambda i: (i, 0, 0)),
            whole(HEADS, per_q, LANE),
            whole(per_q, channels),
        ),
        scratch_shapes=[
            pltpu.VMEM((per_q, width), f32),
            pltpu.VMEM((per_q, width), bf),
            pltpu.VMEM((per_q, width), f32),
            pltpu.VMEM((per_q, width), f32),
            pltpu.VMEM((per_q, width), bf),
            pltpu.VMEM((1, mlp), f32),
        ],
        compiler_params=pltpu.CompilerParams(vmem_limit_bytes=56 << 20),
        cost_estimate=cost(14),
    )(joined_rows, early, w_proj, w_short, b_proj, b_short, norm2_gain, norm2_bias, w_fc1, b_fc1, w_fc2, b_fc2)
    dj_head = lax.all_to_all(dj, G, 0, 0, tiled=True).reshape(queries, LANE)
    keep, e6a, e6b = lax.optimization_barrier((keep, e6a, e6b))
    k2, k4, k1 = near(keep)
    e7a, e7b = last(e6a, e6b)
    output = output.transpose(1, 2, 0, 3)
    acthg, dj_head, kt_all, output = lax.optimization_barrier((acthg, dj_head, kt_all, output))
    ah_head = lax.all_to_all(acthg, G, 0, 0, tiled=True)

    dk, dv, dmem, pq, small2 = call(
        functools.partial(attend_back_kernel, hdims),
        (
            shape((CUR, LANE), f32),
            shape((CUR, LANE), f32),
            shape((HEADS, LANE + 16, 4 * hd), bf),
            shape((queries, LANE), f32),
            shape((width // (LANE - hd), LANE - hd), f32),
        ),
        (qt_all, q_all, o_all, l_all, dj_head, rel_t, rel_h, rel_w, place, k_all, kt_all, v_all),
        scratch=[
            pltpu.VMEM((LANE, queries), bf),
            pltpu.VMEM((hd + 48, queries), f32),
            pltpu.VMEM((TAB, hd), f32),
            pltpu.VMEM((TAB, queries), f32),
            pltpu.VMEM((KEYS, LANE), f32),
            pltpu.VMEM((KEYS, LANE), f32),
            pltpu.VMEM((1, queries), f32),
            pltpu.VMEM((TABLE_ROWS, LANE), f32),
            pltpu.VMEM((KEYS, 2 * LANE), bf),
            pltpu.VMEM((BACK, KEYS), bf),
            pltpu.VMEM((KEYS, LANE), bf),
            pltpu.SemaphoreType.DMA((4, 2)),
        ],
        smem=0,
        us=25,
        far=3,
        away=(0, 1),
    )
    cols = channels // HEADS
    taken = dmem.shape[1]
    mk, k2, k4, k1 = lax.optimization_barrier((mk, k2, k4, k1))
    k6a, k6b, k3, k5 = across(k2, k4, cut)
    k7a, k7b = last(k6a, k6b)
    gconv = call(
        functools.partial(conv_grad_kernel, hd),
        shape((16, 4 * hd), f32),
        (mk, mv, dk, dv),
        scratch=[pltpu.VMEM((54, 8, LANE), f32)]
        + [pltpu.VMEM((FLAT, LANE), f32)] * 2
        + [pltpu.VMEM((CUR, LANE), f32)] * 2
        + [pltpu.SemaphoreType.DMA((4, FR // 2))],
        smem=0,
        us=12,
        far=4,
    )
    dmem, gconv = lax.optimization_barrier((dmem, gconv))
    outs = (
        shape((width, block), bf),
        shape((HEADS, taken + block * hd // channels, channels), bf),
        shape((width * hd // channels, channels), bf),
        shape((width // HEADS, channels), bf),
    )
    fc2p, fc1p, projp, shortp = call(
        functools.partial(weight_grad_kernel, (width, hd, channels, per_q)),
        outs,
        (meta, ah_head, joined, dmem, early, e2, e4, e6a, e6b, e1, e3, e5, e7a, e7b, keep, k2, k4, k6a, k6b, k1, k3, k5, k7a, k7b),
        scratch=[
            pltpu.VMEM((queries, block), bf),
            pltpu.VMEM((queries, block), bf),
            pltpu.VMEM((2, width, LANE), f32),
            pltpu.VMEM((2, block, LANE), f32),
            pltpu.VMEM((queries, width + channels), bf),
            pltpu.VMEM((queries, 2 * width), bf),
            pltpu.SemaphoreType.DMA((2, 10)),
        ],
        us=9,
        far=20,
    )

    def over_four(sent):
        got = [lax.ppermute(sent[k], "clip", [(i, i ^ k) for i in range(n_clip)]) for k in range(1, n_clip)]
        first, second, third_, fourth = [v.astype(f32) for v in [sent[0]] + got]
        return (first + second) + (third_ + fourth)

    clip = lax.axis_index("clip")

    def send_four(block):
        return [block(clip)] + [lax.ppermute(block(clip ^ k), "clip", [(i, i ^ k) for i in range(n_clip)]) for k in range(1, n_clip)]

    def add(got):
        return (got[0].astype(f32) + got[1].astype(f32)) + (got[2].astype(f32) + got[3].astype(f32))

    dk, fc1p = lax.optimization_barrier((dk, fc1p))
    first_back = lax.all_to_all(fc1p, G, 0, 0, tiled=True)
    own = [v.reshape(n_clip, v.shape[0] // n_clip, channels) for v in (fc2p, projp, shortp)]
    if n_clip == 4:
        together = jnp.concatenate(own, axis=1)
        got2 = send_four(lambda c: lax.dynamic_index_in_dim(together, c, 0, keepdims=False))
    else:
        got2 = lax.all_to_all(jnp.concatenate(own, axis=1), "clip", 0, 0, tiled=True)
    sent = valid // 2 + third
    pgp, stats = pl.pallas_call(
        functools.partial(conv_back_kernel, hdims),
        out_shape=(shape((HEADS, sent + 48, 4 * hd), bf), shape((8, channels), f32)),
        in_specs=[pl.BlockSpec(memory_space=pltpu.SMEM)] + [vmem] * 6 + [pl.BlockSpec(memory_space=pl.ANY)] * 11,
        out_specs=(vmem,) * 2,
        scratch_shapes=[
            pltpu.VMEM((FR * GRID * GRID, 3 * LANE), bf),
            pltpu.VMEM((FLAT, LANE), f32),
            pltpu.VMEM((FLAT, LANE), f32),
            pltpu.VMEM((2 * queries, LANE), f32),
            pltpu.VMEM((FR, GRID * GRID, channels), bf),
            pltpu.VMEM((2, 3 * hd, LANE), f32),
            pltpu.VMEM((3, hd, channels), bf),
            pltpu.SemaphoreType.DMA((HEADS * frames,)),
            pltpu.SemaphoreType.DMA((3,)),
        ],
        compiler_params=pltpu.CompilerParams(vmem_limit_bytes=56 << 20),
        cost_estimate=cost(18),
    )(meta, dk, dv, pq, taps, norm1_gain, norm1_bias, *blocks, w_qkv)
    pgp, first_back, got2 = lax.optimization_barrier((pgp, first_back, got2))
    pg_rows = lax.all_to_all(pgp, G, 0, 0, tiled=True)
    if n_clip == 4:
        each = HEADS // n_clip
        got1 = send_four(
            lambda c: lax.dynamic_slice(first_back, (c * each, taken, 0), (each, first_back.shape[1] - taken, channels))
        )
    else:
        got1 = lax.all_to_all(first_back[:, taken:].reshape(n_clip, -1, channels), "clip", 0, 0, tiled=True)
    late = call(
        functools.partial(late_kernel, dims),
        shape((LATE, channels), bf),
        (gconv, stats, small2, mem, first_back),
        scratch=[
            pltpu.VMEM((4, width // LANE, GRID, LANE), f32),
            pltpu.VMEM((LATE, channels), f32),
            pltpu.VMEM(mem.shape, bf),
            pltpu.VMEM((HEADS, taken, channels), bf),
            pltpu.SemaphoreType.DMA((2 * MEM + 1,)),
        ],
        smem=0,
        us=5,
        far=2,
    )
    if n_clip == 4:
        late = over_four([late] * n_clip)
    else:
        late = jnp.sum(lax.all_gather(late, "clip", axis=0).astype(f32), axis=0)
    if n_clip == 4:
        count = width // n_clip
        part_fc2, part_proj, part_short = call(
            functools.partial(second_kernel, (hd, cols, channels)),
            (shape((count, block), f32), shape((count, hd), f32), shape((cols, count), f32)),
            tuple(got2),
            scratch=[pltpu.VMEM((-(-count // LANE) * LANE, LANE), f32)],
            smem=0,
            us=2,
        )
        late, part_fc2 = lax.optimization_barrier((late, part_fc2))
    late_full = lax.all_gather(late, G, axis=0)
    pg_rows, late_full, got1 = lax.optimization_barrier((pg_rows, late_full, got1))
    vector = lambda n: shape((n,), f32)
    qkv_rows = pg_rows[:, sent : sent + 3 * hd // HEADS]
    qkv_rows = qkv_rows.reshape(HEADS, 3, hd // HEADS, channels).transpose(1, 0, 2, 3).reshape(-1, channels)
    got = lax.all_to_all(qkv_rows.reshape(n_clip, -1, channels), "clip", 0, 0, tiled=True)
    four = 4 if n_clip == 4 else 0
    results = call(
        functools.partial(tail_kernel, dims, (width, hd, channels), four),
        (
            shape((cells_all, channels), bf),
            vector(channels), vector(channels), vector(3 * width), shape((3, 3, 3, 2, width), f32), shape(compress.shape, f32),
            shape(rel_t.shape, f32), shape(rel_h.shape, f32), shape(rel_w.shape, f32),
            vector(width), vector(width), vector(width), vector(width), vector(mlp), vector(width),
        )
        + ((shape((hd, mlp // n_clip), f32),) if four else ()),
        (x, norm1_gain, mx, max_grad, late_full)
        + (tuple(v.reshape(-1, channels) for v in got1) if four else ())
        + (w_qkv, pg_rows),
        scratch=[
            pltpu.VMEM((cells_all, channels), f32),
            pltpu.VMEM((width // LANE, rows * GRID, LANE), f32),
            pltpu.VMEM(w_qkv.shape, bf),
            pltpu.VMEM((HEADS, sent, channels), bf),
            pltpu.SemaphoreType.DMA((HEADS + 1,)),
            pltpu.VMEM((TABLE_ROWS, LANE), f32),
        ]
        + ([pltpu.VMEM((mlp // n_clip, LANE), f32)] if four else []),
        smem=0,
        us=9,
        far=2,
    )
    input_grad, g1, b1, gbq, gconv, gcomp, gt, gh, gw, gbp, gbs, g2, b2, gb1, gb2 = results[:15]
    part_qkv = jnp.sum(got.astype(f32), axis=0).reshape(-1, cols)
    if n_clip == 4:
        part_fc1 = results[15].T
        part_short = part_short.T
    else:
        part_fc1, part2 = (jnp.sum(v.astype(f32), axis=0) for v in (got1, got2))
        ends = np.cumsum([v.shape[1] for v in own])
        part_fc2, part_proj, part_short = part2[: ends[0]], part2[ends[0] : ends[1]], part2[ends[1] :]
        part_fc1, part_proj, part_short = part_fc1.reshape(-1, hd), part_proj.reshape(-1, hd), part_short.reshape(-1, cols)
    return (
        output.transpose(2, 0, 1, 3)[None],
        input_grad.reshape(clip_input.shape),
        g1,
        b1,
        part_qkv,
        gbq,
        jnp.moveaxis(gconv, 3, 0),
        gcomp,
        gt,
        gh,
        gw,
        part_proj,
        gbp,
        part_short,
        gbs,
        g2,
        b2,
        part_fc1,
        gb1,
        part_fc2,
        gb2,
    )


def solution(mesh):
    split = P("clip", "tm", "height", None, None)
    shared = P()
    weight = P("clip", ("tm", "height"))
    placed = (split, P("clip", None, None, "tm", "height", None, None), P("clip"), P("clip")) + (shared,) * 19 + (split,)
    outs = (split, split, shared, shared, weight) + (shared,) * 6 + (weight, shared, weight, shared, shared, shared, weight, shared, weight, shared)
    return jax.shard_map(body, mesh=mesh, in_specs=placed, out_specs=outs, check_vma=False)
```

```python
import functools

import jax
import jax.numpy as jnp
import numpy as np
from jax import lax
from jax.experimental import pallas as pl
from jax.experimental.pallas import tpu as pltpu
from jax.sharding import PartitionSpec as P

HEADS = 8
SIDE_SMALL = 14
SIDE_BIG = 20
MEM = 2
EPSILON = 1e-06
SQRT_HALF = 0.7071067811865476
ROOT_TWO_PI = 2.5066282746310002
LOG2E = 1.4426950408889634
FAR = -1e30

GRID = 24
FR = 8
HALF = GRID // 2
VW = SIDE_BIG
VH = VW // 2
LANE = 128
PLANE = (VW + 1) * GRID
FLAT = GRID + (FR + 2) * PLANE
CUR = FR * VW * VW
KEYS_USED = CUR + MEM * FR * VH * VH
KEYS = -(-KEYS_USED // 256) * 256
BACK = 144
LATE_COMP, LATE_SMALL, LATE_TABLE, LATE = 17, 33, 35, 40
STEP = 4
TABLE_ROWS = 2 * FR + 4 * GRID
TAB = 8 * FR + 2 * GRID * HALF

bf = jnp.bfloat16
f32 = jnp.float32
HI = lax.Precision.HIGHEST
G = ("tm", "height")


def nn(a, b, **kw):
    return lax.dot_general(a, b, (((1,), (0,)), ((), ())), preferred_element_type=f32, **kw)


def nt(a, b, **kw):
    return lax.dot_general(a, b, (((1,), (1,)), ((), ())), preferred_element_type=f32, **kw)


def tn(a, b, **kw):
    return lax.dot_general(a, b, (((0,), (0,)), ((), ())), preferred_element_type=f32, **kw)


def shape(dims, dtype):
    return jax.ShapeDtypeStruct(dims, dtype)


def cost(us):
    return pl.CostEstimate(flops=int(us * 1e9), bytes_accessed=0, transcendentals=0)


def call(kernel, outs, args, scratch=(), smem=1, us=5, far=0, away=()):
    specs = [pl.BlockSpec(memory_space=pltpu.SMEM)] * smem
    specs += [pl.BlockSpec(memory_space=pltpu.VMEM)] * (len(args) - smem - far)
    specs += [pl.BlockSpec(memory_space=pl.ANY)] * far
    return pl.pallas_call(
        kernel,
        out_shape=outs,
        in_specs=specs,
        out_specs=(
            tuple(pl.BlockSpec(memory_space=pl.ANY if i in away else pltpu.VMEM) for i in range(len(outs)))
            if isinstance(outs, tuple)
            else pl.BlockSpec(memory_space=pltpu.VMEM)
        ),
        scratch_shapes=list(scratch),
        compiler_params=pltpu.CompilerParams(vmem_limit_bytes=56 << 20),
        cost_estimate=cost(us),
    )(*args)


def row_of(ref, lo, hi):
    return ref[lo:hi].reshape(1, hi - lo)


def pack_rows(value, scratch, groups):
    rows, lanes = value.shape
    scratch[0:rows, :] = pad_lanes(value, LANE)
    parts = [scratch[pl.ds(g, rows // groups, groups), :][:, 0:lanes] for g in range(groups)]
    return jnp.concatenate(parts, axis=1)


def pad_lanes(x, lanes):
    return jnp.concatenate([x, jnp.zeros((x.shape[0], lanes - x.shape[1]), x.dtype)], axis=1)


def layer_unit(x):
    centred = x - jnp.mean(x, axis=-1, keepdims=True)
    inverse = lax.rsqrt(jnp.mean(centred * centred, axis=-1, keepdims=True) + EPSILON)
    return centred * inverse, inverse


def pair_reduce(value, scratch, op):
    rows, lanes = value.shape
    outs = []
    for j in range(lanes // LANE):
        scratch[j, 0:rows, :] = value[:, j * LANE : (j + 1) * LANE]
    for j in range(lanes // LANE):
        outs.append(op(scratch[j, pl.ds(0, rows // 2, 2), :], scratch[j, pl.ds(1, rows // 2, 2), :]))
    return jnp.concatenate(outs, axis=1)


def join_lines(value, op):
    return jnp.concatenate(
        [op(value[a : a + GRID], value[a + GRID : a + 2 * GRID]) for a in range(0, value.shape[0], 2 * GRID)], axis=0
    )


def pair_spread(value, scratch):
    rows, lanes = value.shape
    for j in range(lanes // LANE):
        part = value[:, j * LANE : (j + 1) * LANE]
        scratch[j, pl.ds(0, rows, 2), :] = part
        scratch[j, pl.ds(1, rows, 2), :] = part
    return jnp.concatenate([scratch[j, 0 : 2 * rows, :] for j in range(lanes // LANE)], axis=1)


def norm_kernel(dims, x_ref, g_ref, b_ref, n1_ref, mx_ref, tiles):
    frames, rows = dims
    half = rows // 2
    channels = x_ref.shape[1]
    per = rows * GRID
    g = row_of(g_ref, 0, channels)
    b = row_of(b_ref, 0, channels)
    for t in range(frames):
        x = x_ref[t * per : (t + 1) * per, :].astype(f32)
        unit, _ = layer_unit(x)
        n1_ref[t * per : (t + 1) * per, :] = (unit * g + b).astype(bf)
        tall = join_lines(x, jnp.maximum)
        mx_ref[t * half * HALF : (t + 1) * half * HALF, :] = pair_reduce(tall, tiles, jnp.maximum)


def squeeze_kernel(dims, mem_ref, c_ref, cot_ref, mx_ref, out_ref, early_ref, tiles, squeezed):
    frames, rows, width, hd = dims
    half = rows // 2
    count = half * frames * VH
    odd = lax.broadcasted_iota(jnp.int32, (GRID, 1), 0) % 2 == 1
    for m in range(2):
        taps = [jnp.where(odd, c_ref[m, i, 1:2, :], c_ref[m, i, 0:1, :]) for i in range(2)]
        for s in range(MEM):
            for t in range(frames):
                parts = [
                    mem_ref[s, m, t, 2 * a].astype(f32) * taps[0] + mem_ref[s, m, t, 2 * a + 1].astype(f32) * taps[1]
                    for a in range(half)
                ]
                for a in range(half):
                    done = pair_reduce(parts[a], tiles.at[(t * half + a) % 4], jnp.add)
                    squeezed[m, s, a * frames * VH + t * VH : a * frames * VH + (t + 1) * VH, :] = done[0:VH]
            squeezed[m, s, count:LANE, :] = jnp.zeros((LANE - count, width), f32)
    for n in range(HEADS):
        cut = slice(n * hd, (n + 1) * hd)
        out_ref[n] = jnp.concatenate(
            [squeezed[0, 0, :, cut], squeezed[1, 0, :, cut], squeezed[0, 1, :, cut], squeezed[1, 1, :, cut]], axis=1
        ).astype(bf)
    cot = jnp.concatenate([cot_ref[t, a].astype(f32) for t in range(frames) for a in range(half)], axis=0)
    early_ref[:, 0:width] = cot.astype(bf)
    early_ref[:, width:] = mx_ref[...].astype(bf)


def flat_row(t, h):
    return GRID + (1 + t) * PLANE + h * GRID


def fill_grid(grid):
    zero = jnp.zeros((GRID, LANE), f32)
    grid[0 : GRID + PLANE, :] = jnp.zeros((GRID + PLANE, LANE), f32)
    grid[flat_row(FR, 0) :, :] = jnp.zeros((FLAT - flat_row(FR, 0), LANE), f32)
    for t in range(FR):
        grid[flat_row(t, VW) : flat_row(t, VW) + GRID, :] = zero


def taps9(w_ref, part):
    return [[[w_ref[(a * 3 + b) * 3 + c : (a * 3 + b) * 3 + c + 1, part * LANE : (part + 1) * LANE] for c in range(3)] for b in range(3)] for a in range(3)]


def four_rows(grid, weights, base, flip, keep=VW):
    acc = [[None] * 3 for _ in range(4)]
    for line in range(-1, 5):
        for a in range(3):
            shift = (1 - a if flip else a - 1) * PLANE + line * GRID
            cells = grid[pl.ds(pl.multiple_of(base + shift, 8), GRID), :]
            for h in range(4):
                b = (h - line + 1) if flip else (line - h + 1)
                if b < 0 or b > 2:
                    continue
                for c in range(3):
                    term = cells * weights[a][b][c]
                    acc[h][c] = term if acc[h][c] is None else acc[h][c] + term
    outs = []
    for h in range(4):
        left, mid, right = (acc[h][2], acc[h][1], acc[h][0]) if flip else (acc[h][0], acc[h][1], acc[h][2])
        outs.append((pltpu.roll(left, 1, 0) + mid + pltpu.roll(right, GRID - 1, 0))[0:keep])
    return jnp.concatenate(outs, axis=0)


def gather_blocks(dims, meta, refs, out, sems):
    frames, rows, n_height = dims
    member = meta[4]
    per = rows * GRID
    x0, x2, x4, x6a, x6b, x1, x3, x5, x7a, x7b = refs
    copies = []
    for d, parts in enumerate([[x0], [x1], [x2], [x3], [x4], [x5], [x6a, x6b], [x7a, x7b]]):
        src = member ^ d
        t = lax.div(src, n_height) * frames
        at = pl.ds(pl.multiple_of(lax.rem(src, n_height) * per, 16), per)
        for ref in parts:
            for i in range(ref.shape[0] // per):
                copies.append(pltpu.make_async_copy(ref.at[i * per : (i + 1) * per, :], out.at[t, at, :], sems.at[len(copies)]))
                t = t + 1
    return copies


def own_weights(meta, qkv_ref, out, sems):
    width, hd = qkv_ref.shape[0] // 3, out.shape[1]
    rows = [pl.ds(pl.multiple_of(p * width + meta[4] * hd, 32), hd) for p in range(3)]
    return [pltpu.make_async_copy(qkv_ref.at[rows[p], :], out.at[p], sems.at[p]) for p in range(3)]


def conv_kernel(dims, meta, w_ref, bias_ref, *refs):
    frames, rows, n_height, hd = dims
    half = rows // 2
    blocks, qkv_ref, (k_ref, v_ref, q_ref, mk, mv, gk, gv, gather, tiles, qrow, wide, sems, more) = refs[:10], refs[10], refs[11:]
    copies = own_weights(meta, qkv_ref, wide, more) + gather_blocks(dims[:3], meta, blocks, gather, sems)
    for copy in copies:
        copy.start()
    side = meta[0]
    channels = qkv_ref.shape[1]
    for grid in (gk, gv):
        fill_grid(grid)
    blank = jnp.zeros((LANE - hd, channels), bf)
    index = lax.broadcasted_iota(jnp.int32, (VW * GRID, 1), 0)
    line = (index * 2731) >> 16
    inside = ((line < side) & (index - line * GRID < side)).astype(f32)
    for copy in copies:
        copy.wait()
    weight_q = jnp.concatenate([wide[0], blank], axis=0)
    weight_kv = jnp.concatenate([wide[1], blank, wide[2], blank], axis=0)
    piece = half * HALF
    for t in range(FR):
        query = pair_reduce(join_lines(nt(gather[t], weight_q), jnp.add), tiles.at[t % 2], jnp.add) * 0.25 + bias_ref[0:1, 0:LANE]
        for h in range(n_height):
            at = (t // frames * n_height + h) * frames * piece + t % frames * piece
            qrow[at : at + piece, :] = query[h * piece : (h + 1) * piece]
        pair = ((nt(gather[t, 0 : VW * GRID, :], weight_kv) + bias_ref[0:1, LANE:]) * inside).astype(bf).astype(f32)
        gk[flat_row(t, 0) : flat_row(t, VW), :] = pair[:, 0:LANE]
        gv[flat_row(t, 0) : flat_row(t, VW), :] = pair[:, LANE:]
    q_ref[...] = qrow[...].astype(bf)
    sent = [pltpu.make_async_copy(gk, mk, more.at[3]), pltpu.make_async_copy(gv, mv, more.at[4])]
    for copy in sent:
        copy.start()
    local = lax.broadcasted_iota(jnp.int32, (4 * VW, LANE), 0)
    lane = lax.broadcasted_iota(jnp.int32, (4 * VW, LANE), 1)
    line = (local * 3277) >> 16
    column = local - line * VW
    fixed = [(lane + o == 143 - column) | (lane + o == 191 - column) for o in (0, LANE)]
    ones = (lane == hd).astype(f32)

    def step(it, carry):
        t = it // (VW // 4)
        quad = it % (VW // 4)
        base = GRID + (1 + t) * PLANE + quad * 4 * GRID
        out = pl.ds(pl.multiple_of(it * (4 * VW), 16), 4 * VW)
        mixed_k = four_rows(gk, taps9(w_ref, 0), base, False)
        mixed_v = four_rows(gv, taps9(w_ref, 1), base, False)
        h = quad * 4 + line
        bad = (h >= side) | (column >= side)
        for o in range(2):
            at = lane + o * LANE
            hit = fixed[o] | (at == 103 - t) | (at == 151 - t) | (at == 123 - h) | (at == 171 - h) | ((at == 192) & bad)
            marks = hit.astype(f32)
            k_ref[out, o * LANE : (o + 1) * LANE] = ((mixed_k + marks) if o == 0 else marks).astype(bf)
        v_ref[out, :] = (mixed_v + ones).astype(bf)
        return carry

    lax.fori_loop(0, FR * VW // 4, step, 0)
    for copy in sent:
        copy.wait()


def build_table(tab, t_ref, h_ref, w_ref):
    tab[...] = jnp.zeros(tab.shape, f32)
    for v in range(FR):
        tab[8 * v : 8 * v + FR, :] = t_ref[v : v + FR, :]
    for n, ref in ((0, h_ref), (1, w_ref)):
        for a in range(HALF):
            at = 8 * FR + (n * HALF + a) * GRID
            first = 2 * a + GRID - VW
            tab[at : at + VW, :] = ref[first : first + VW, :]


def attend_kernel(dims, meta, kc_ref, vc_ref, q_ref, y_ref, t_ref, h_ref, w_ref, place_ref, k_out, v_out, qt_ref, o_ref, l_ref, j_ref, vt, tab, k_ref, v_ref, sems):
    frames, rows, n_height, hd = dims
    half = rows // 2
    side, length = meta[0], meta[1]
    queries = q_ref.shape[0]
    scale = hd**-0.5
    k_ref[0:CUR, :] = kc_ref[...]
    v_ref[0:CUR, :] = vc_ref[...]
    count = half * frames * VH
    each = frames * VH
    lane1 = lax.broadcasted_iota(jnp.int32, (1, LANE), 1)
    at = CUR
    for src in range(HEADS):
        packed = y_ref[src].astype(f32)
        first = src % n_height * half
        used = min(max(VH - first, 0), half) * each
        if used > 0:
            halves = []
            for m in range(2):
                halves.append(jnp.concatenate([packed[0:used, m * hd : (m + 1) * hd], packed[0:used, (2 + m) * hd : (3 + m) * hd]], axis=0))
            index = lax.broadcasted_iota(jnp.int32, (2 * used, LANE), 0)
            step = (index >= used).astype(jnp.int32)
            inner = index - step * used
            a = (inner >= each).astype(jnp.int32) + (inner >= 2 * each).astype(jnp.int32)
            inner = inner - a * each
            c = inner - ((inner * 6554) >> 16) * VH
            bad = (step >= length) | (2 * (first + a) >= side) | (2 * c >= side)
            mark = (bad & (lax.broadcasted_iota(jnp.int32, (2 * used, LANE), 1) == 64)).astype(f32)
            k_ref[at : at + 2 * used, 0:LANE] = pad_lanes(halves[0], LANE).astype(bf)
            k_ref[at : at + 2 * used, LANE:] = mark.astype(bf)
            v_ref[at : at + 2 * used, :] = (pad_lanes(halves[1], LANE) + (lane1 == hd).astype(f32)).astype(bf)
            at += 2 * used
    rest = KEYS - at
    k_ref[at:, 0:LANE] = jnp.zeros((rest, LANE), bf)
    k_ref[at:, LANE:] = jnp.broadcast_to((lane1 == 64).astype(f32), (rest, LANE)).astype(bf)
    v_ref[at:, :] = jnp.zeros((rest, LANE), bf)
    for i in range(KEYS // 256):
        cut = slice(i * 256, (i + 1) * 256)
        vt[:, cut] = v_ref[cut, :].T
    sent = [pltpu.make_async_copy(k_ref, k_out, sems.at[0]), pltpu.make_async_copy(v_ref, v_out, sems.at[1])]
    for copy in sent:
        copy.start()
    pt = q_ref[...].astype(f32).T[0:hd]
    build_table(tab, t_ref, h_ref, w_ref)
    table = tab[...]
    coarse = table.astype(bf)
    turned = pt.astype(bf)
    along = nn(coarse, turned) + nn((table - coarse.astype(f32)).astype(bf), turned)
    tq, aq, cq = place_ref[0:1, :], place_ref[1:2, :], place_ref[2:3, :]
    part_t = jnp.zeros((FR, queries), f32)
    for v in range(FR):
        part_t = jnp.where(tq == v, along[8 * v : 8 * v + FR], part_t)
    parts = []
    for n, place in ((0, aq), (1, cq)):
        part = jnp.zeros((GRID, queries), f32)
        for a in range(HALF):
            row = 8 * FR + (n * HALF + a) * GRID
            part = jnp.where(place == a, along[row : row + GRID], part)
        parts.append(part[0:VW])
    bias = jnp.concatenate([part_t] + parts, axis=0) * hd**0.5
    high = bias.astype(bf)
    low = (bias - high.astype(f32)).astype(bf)
    qt_ref[0:hd, :] = pt.astype(bf)
    qt_ref[hd : hd + 48, :] = high
    qt_ref[hd + 48 : hd + 96, :] = low
    tail = lax.broadcasted_iota(jnp.int32, (64, queries), 0)
    qt_ref[192:256, :] = jnp.where(tail == 0, FAR, 0.0).astype(bf)
    factor = scale * LOG2E
    query = qt_ref[...]
    top = None
    for lo in range(0, KEYS, 1024):
        cut = slice(lo, min(lo + 1024, KEYS))
        scores = nn(k_ref[cut, :], query)
        here = jnp.max(scores.reshape(scores.shape[0] // 8, 8, queries), axis=0)
        here = jnp.max(here, axis=0, keepdims=True) * factor
        new = here if top is None else jnp.maximum(top, here)
        part = nn(vt[:, cut], jnp.exp2(scores * factor - new).astype(bf))
        total = part if top is None else total * jnp.exp2(top - new) + part
        top = new
    norm = total[hd : hd + 1]
    o_ref[...] = total[0:hd] / norm
    l_ref[...] = top + jnp.log2(norm)
    j_ref[...] = pad_lanes((o_ref[...] + pt).T, LANE).astype(bf)
    for copy in sent:
        copy.wait()


def turn_kernel(k_ref, kt_ref):
    for i in range(KEYS // 256):
        cut = slice(i * 256, (i + 1) * 256)
        kt_ref[0:LANE, cut] = k_ref[cut, 0:LANE].T
        kt_ref[LANE:BACK, cut] = k_ref[cut, LANE:].T[0 : BACK - LANE]


def mlp_kernel(dims, j_ref, early_ref, wp_ref, ws_ref, bp_ref, bs_ref, g_ref, b_ref, w1_ref, b1_ref, w2_ref, b2_ref,
               out_ref, keep_ref, act_ref, dj_ref, mg_ref,
               resid, n2, acc, ngrad, joined, gb1):
    width, hd = dims
    i = pl.program_id(0)
    per_q = early_ref.shape[0]
    block = w1_ref.shape[0]

    @pl.when(i == 0)
    def _():
        joined[...] = jnp.concatenate([j_ref[n][:, 0:hd] for n in range(HEADS)], axis=1)
        shift = row_of(bp_ref, 0, width) + row_of(bs_ref, 0, width)
        value = nt(joined[...], wp_ref[...]) + nt(early_ref[:, width:], ws_ref[...]) + shift
        resid[...] = value
        unit, _ = layer_unit(value)
        n2[...] = (unit * row_of(g_ref, 0, width) + row_of(b_ref, 0, width)).astype(bf)
        acc[...] = jnp.zeros(acc.shape, f32)
        ngrad[...] = jnp.zeros(ngrad.shape, f32)

    here = pl.ds(pl.multiple_of(i * block, LANE), block)
    hidden = nt(n2[...], w1_ref[...]) + b1_ref[here].reshape(1, block)
    gate = 0.5 * (1.0 + lax.erf(hidden * SQRT_HALF))
    act = (hidden * gate).astype(bf)
    each = act_ref.shape[2]
    for n in range(act_ref.shape[0]):
        act_ref[n, 0:per_q, :] = act[:, n * each : (n + 1) * each]
    acc[...] += nt(act, w2_ref[...])
    grad = nn(early_ref[:, 0:width], w2_ref[...])
    hgrad = (grad * (gate + hidden * jnp.exp(-0.5 * hidden * hidden) / ROOT_TWO_PI)).astype(bf)
    for n in range(act_ref.shape[0]):
        act_ref[n, per_q:, :] = hgrad[:, n * each : (n + 1) * each]
    gb1[:, here] = jnp.sum(hgrad.astype(f32), axis=0, keepdims=True)
    ngrad[...] += nn(hgrad, w1_ref[...])

    @pl.when(i == pl.num_programs(0) - 1)
    def _():
        value = resid[...]
        result = value + acc[...] + row_of(b2_ref, 0, width)
        for t in range(out_ref.shape[0]):
            for a in range(out_ref.shape[1]):
                at = (t * out_ref.shape[1] + a) * HALF
                out_ref[t, a] = result[at : at + HALF].astype(bf)
        unit, inverse = layer_unit(value)
        cot = early_ref[:, 0:width].astype(f32)
        grad = ngrad[...]
        scaled = grad * row_of(g_ref, 0, width)
        back = inverse * (
            scaled - jnp.mean(scaled, axis=-1, keepdims=True) - unit * jnp.mean(scaled * unit, axis=-1, keepdims=True)
        )
        low = (cot + back).astype(bf)
        keep_ref[:, 0:width] = n2[...]
        keep_ref[:, width:] = low
        joined_grad = nn(low, wp_ref[...])
        mg_ref[...] = nn(low, ws_ref[...])
        sums = [jnp.sum(v, axis=0, keepdims=True) for v in (low.astype(f32), grad * unit, grad, cot)] + [gb1[...]]
        flat = [v[:, k : k + width] for v in sums for k in range(0, v.shape[1], width)]
        spare = LANE - hd
        for n in range(HEADS):
            exact = jnp.concatenate([flat[n][:, k : k + spare] for k in range(0, width, spare)], axis=0)
            high = exact.astype(bf).astype(f32)
            side = jnp.concatenate([high, exact - high, jnp.zeros((per_q - 2 * exact.shape[0], spare), f32)], axis=0)
            dj_ref[n] = jnp.concatenate([joined_grad[:, n * hd : (n + 1) * hd], side], axis=1).astype(bf)


def attend_back_kernel(dims, qt_ref, q_ref, o_ref, l_ref, dj_ref, t_ref, h_ref, w_ref, place_ref, k_in, kt_in, v_in,
                       dk_ref, dv_ref, mem_ref, pq_ref, small_ref,
                       dot_ref, dq, tab, dtab, dks, dvs, delta, tables, k_ref, kt_ref, v_ref, sems):
    frames, rows, n_height, hd = dims
    half = rows // 2
    queries = q_ref.shape[0]
    scale = hd**-0.5
    factor = scale * LOG2E
    turned = dj_ref[...].astype(f32).T
    half_keys = KEYS // 2

    def brought(i):
        cut = pl.ds(pl.multiple_of(i * half_keys, LANE), half_keys)
        return [
            pltpu.make_async_copy(k_in.at[cut, :], k_ref.at[cut, :], sems.at[0, i]),
            pltpu.make_async_copy(v_in.at[cut, :], v_ref.at[cut, :], sems.at[1, i]),
            pltpu.make_async_copy(kt_in.at[:, cut], kt_ref.at[:, cut], sems.at[2, i]),
        ]

    for copy in brought(0) + brought(1):
        copy.start()
    per_q = queries // HEADS
    spare = jnp.zeros((per_q, LANE - hd), f32)
    for src in range(HEADS):
        spare = spare + dj_ref[src * per_q : (src + 1) * per_q, hd:].astype(f32)
    lines = small_ref.shape[0]
    small_ref[...] = spare[0:lines] + spare[lines : 2 * lines]
    dot_ref[0:hd, :] = turned[0:hd].astype(bf)
    dot_ref[hd:, :] = jnp.zeros((LANE - hd, queries), bf)
    delta[...] = jnp.sum(turned[0:hd] * o_ref[...], axis=0, keepdims=True)
    dq[...] = jnp.zeros(dq.shape, f32)
    def chunk(i, carry):
        cut = pl.ds(pl.multiple_of(i * half_keys, LANE), half_keys)
        for copy in brought(i):
            copy.wait()
        shares = jnp.exp2(nn(k_ref[cut, :], qt_ref[...]) * factor - l_ref[...])
        slope = nn(v_ref[cut, :], dot_ref[...])
        score = (shares * (slope - delta[...])).astype(bf)
        dvs[cut, :] = nn(shares.astype(bf), dj_ref[...])
        dks[cut, :] = nn(score, q_ref[...]) * scale
        dq[...] += nn(kt_ref[:, cut], score)
        return carry

    lax.fori_loop(0, 2, chunk, 0)
    sent = [
        pltpu.make_async_copy(dks.at[0:CUR, :], dk_ref, sems.at[3, 0]),
        pltpu.make_async_copy(dvs.at[0:CUR, :], dv_ref, sems.at[3, 1]),
    ]
    for copy in sent:
        copy.start()
    each = frames * VH
    at = CUR
    for dst in range(HEADS):
        first = dst % n_height * half
        used = min(max(VH - first, 0), half) * each
        if used > 0:
            parts = [ref[at + s * used : at + (s + 1) * used, 0:hd] for s in range(MEM) for ref in (dks, dvs)]
            packed = jnp.concatenate(parts, axis=1)
            at += 2 * used
        if used < LANE:
            zero = jnp.zeros((LANE - used, 4 * hd), f32)
            packed = jnp.concatenate([packed, zero], axis=0) if used > 0 else zero
        mem_ref[dst, 0:LANE, :] = packed.astype(bf)
    build_table(tab, t_ref, h_ref, w_ref)
    tq, aq, cq = place_ref[0:1, :], place_ref[1:2, :], place_ref[2:3, :]
    grad_t = dq[hd : hd + FR, :]
    for v in range(FR):
        dtab[8 * v : 8 * v + FR, :] = jnp.where(tq == v, grad_t, 0.0)
    for n, place in ((0, aq), (1, cq)):
        part = jnp.concatenate(
            [dq[hd + FR + n * VW : hd + FR + (n + 1) * VW, :], jnp.zeros((GRID - VW, queries), f32)], axis=0
        )
        for a in range(HALF):
            row = 8 * FR + (n * HALF + a) * GRID
            dtab[row : row + GRID, :] = jnp.where(place == a, part, 0.0)
    spread = dtab[...].astype(bf)
    pooled_grad = dq[0:hd, :] * scale + tn(tab[...].astype(bf), spread) + dot_ref[0:hd, :].astype(f32)
    pq_ref[...] = pad_lanes(pooled_grad.T * 0.25, LANE)
    grads = nn(spread, q_ref[...])
    tables[...] = jnp.zeros(tables.shape, f32)
    for v in range(FR):
        tables[v : v + FR, :] += grads[8 * v : 8 * v + FR]
    for n in range(2):
        for a in range(HALF):
            row = 8 * FR + (n * HALF + a) * GRID
            first = 2 * FR + n * 2 * GRID + 2 * a + GRID - VW
            tables[first : first + VW, :] += grads[row : row + VW]
    share = TABLE_ROWS // HEADS
    for dst in range(HEADS):
        part = jnp.concatenate([tables[dst * share : (dst + 1) * share, :], jnp.zeros((16 - share, LANE), f32)], axis=0)
        high = part.astype(bf).astype(f32)
        mem_ref[dst, LANE:, :] = jnp.concatenate([high, part - high, jnp.zeros((16, LANE), f32)], axis=1).astype(bf)
    for copy in sent:
        copy.wait()


def conv_back_kernel(dims, meta, dk_ref, dv_ref, pq_ref, w_ref, g_ref, b_ref, *refs):
    frames, rows, n_height, hd = dims
    half = rows // 2
    blocks, qkv_ref, (out_ref, stat_ref, pg, gk, gv, wide, gather, tall, own, sems, more) = refs[:10], refs[10], refs[11:]
    copies = gather_blocks(dims[:3], meta, blocks, gather, sems) + own_weights(meta, qkv_ref, own, more)
    for copy in copies:
        copy.start()
    side = meta[0]
    channels = qkv_ref.shape[1]
    for grid in (gk, gv):
        fill_grid(grid)
    for ref, grid in ((dk_ref, gk), (dv_ref, gv)):
        for t in range(FR):
            for h in range(VW):
                at = (t * VW + h) * VW
                grid[flat_row(t, h) : flat_row(t, h) + GRID, :] = jnp.concatenate(
                    [ref[at : at + VW, :], jnp.zeros((GRID - VW, LANE), f32)], axis=0
                )
    local = lax.broadcasted_iota(jnp.int32, (4 * GRID, 1), 0)
    line = (local * 2731) >> 16
    column = local - line * GRID
    empty = jnp.zeros(((GRID - VW) * GRID, 2 * LANE), bf)
    for t in range(FR):
        pg[t * GRID * GRID + VW * GRID : (t + 1) * GRID * GRID, LANE:] = empty

    def step(it, carry):
        t = it // (VW // 4)
        quad = it % (VW // 4)
        base = GRID + (1 + t) * PLANE + quad * 4 * GRID
        out = pl.ds(pl.multiple_of((t * GRID + quad * 4) * GRID, 32), 4 * GRID)
        inside = ((quad * 4 + line < side) & (column < side)).astype(f32)
        for m, grid in ((0, gk), (1, gv)):
            back = four_rows(grid, taps9(w_ref, m), base, True, GRID)
            pg[out, (1 + m) * LANE : (2 + m) * LANE] = (back * inside).astype(bf)
        return carry

    lax.fori_loop(0, FR * VW // 4, step, 0)
    queries = pq_ref.shape[0]
    wide[pl.ds(0, queries, 2), :] = pq_ref[...]
    wide[pl.ds(1, queries, 2), :] = pq_ref[...]
    per_q = queries // HEADS
    for src in range(HEADS):
        for t in range(frames):
            for a in range(half):
                at = ((src * frames + t) * half + a) * GRID
                lines = wide[at : at + GRID, :]
                row = ((src // n_height * frames + t) * GRID + src % n_height * rows + 2 * a) * GRID
                pg[row : row + 2 * GRID, 0:LANE] = jnp.concatenate([lines, lines], axis=0).astype(bf)
    span = rows * VW
    cells = span * (frames // 2)
    third = per_q // 3
    for dst in range(HEADS):
        first = dst % n_height * rows
        lines = []
        for t2 in range(frames // 2):
            parts = []
            for g in range(2):
                t = dst // n_height * frames + g * (frames // 2) + t2
                at = (t * GRID + first) * GRID
                block = pg[at : at + rows * GRID, LANE:].astype(f32)
                block = jnp.concatenate([block[h * GRID : h * GRID + VW] for h in range(rows)], axis=0)
                parts += [block[:, 0:hd], block[:, LANE : LANE + hd]]
            lines.append(jnp.concatenate(parts, axis=1))
        out_ref[dst, 0:cells, :] = jnp.concatenate(lines, axis=0).astype(bf)
        out_ref[dst, cells : cells + third, :] = jnp.concatenate(
            [pq_ref[dst * per_q + i * third : dst * per_q + (i + 1) * third, :] for i in range(3)], axis=1
        ).astype(bf)
    for copy in copies:
        copy.wait()
    total = jnp.zeros((3 * LANE, channels), f32)
    sums = jnp.zeros((1, 3 * LANE), f32)
    for t in range(FR):
        part = pg[t * GRID * GRID : (t + 1) * GRID * GRID, :]
        total = total + tn(part, gather[t])
        sums = sums + jnp.sum(part.astype(f32), axis=0, keepdims=True)
    total = jnp.concatenate([total[p * LANE : p * LANE + hd] for p in range(3)], axis=0)
    sums = jnp.concatenate([sums[:, p * LANE : p * LANE + hd] for p in range(3)], axis=1)
    cols = channels // HEADS
    packed = 3 * hd // HEADS
    rest = out_ref.shape[1] - cells - third
    for n in range(HEADS):
        value = pack_rows(total[:, n * cols : (n + 1) * cols], tall.at[n % 2], HEADS)
        out_ref[n, cells + third :, :] = jnp.concatenate([value, jnp.zeros((rest - packed, channels), f32)], axis=0).astype(bf)
    weight = jnp.concatenate([own[p].astype(f32) for p in range(3)], axis=0)
    shift = nn(jnp.broadcast_to(sums, (8, 3 * hd)), weight, precision=HI)[0:1]
    gain = jnp.sum(total * weight, axis=0, keepdims=True)
    gain = (gain - shift * row_of(b_ref, 0, channels)) / row_of(g_ref, 0, channels)
    stat_ref[0:1, :] = pad_lanes(sums, channels)
    stat_ref[1:2, :] = gain
    stat_ref[2:3, :] = shift
    stat_ref[3:8, :] = jnp.zeros((5, channels), f32)


def gather_rows(meta, refs, out, sems):
    x0, x2, x4, x6a, x6b, x1, x3, x5, x7a, x7b = refs
    copies = []
    for d, parts in enumerate([[x0], [x1], [x2], [x3], [x4], [x5], [x6a, x6b], [x7a, x7b]]):
        at = (meta[4] ^ d) * (out.shape[0] // HEADS)
        for ref in parts:
            size = ref.shape[0]
            copies.append(pltpu.make_async_copy(ref, out.at[pl.ds(pl.multiple_of(at, 16), size), :], sems.at[len(copies)]))
            at = at + size
    return copies


def weight_grad_kernel(dims, meta, ah_ref, j_ref, dmem_ref, *refs):
    width, hd, channels, per_q = dims
    early, kept = refs[:10], refs[10:20]
    fc2_ref, fc1_ref, proj_ref, short_ref, act, hgrad, tall, parts, cot_ref, keep_ref, sems = refs[20:]
    member = meta[4]
    first = gather_rows(meta, early, cot_ref, sems.at[0])
    second = gather_rows(meta, kept, keep_ref, sems.at[1])
    for copy in first + second:
        copy.start()
    for src in range(HEADS):
        cut = slice(src * per_q, (src + 1) * per_q)
        act[cut, :] = ah_ref[src, 0:per_q, :]
        hgrad[cut, :] = ah_ref[src, per_q:, :]
    for copy in first:
        copy.wait()
    fc2_ref[...] = tn(cot_ref[:, 0:width], act[...]).astype(bf)
    for copy in second:
        copy.wait()
    normed = keep_ref[:, 0:width]
    resid = keep_ref[:, width : 2 * width]
    fc1 = tn(hgrad[...], normed)
    for n in range(HEADS):
        fc1_ref[n, 0 : dmem_ref.shape[1], :] = dmem_ref[n]
        fc1_ref[n, dmem_ref.shape[1] :, :] = pack_rows(fc1[:, n * hd : (n + 1) * hd], parts.at[n % 2], channels // hd).astype(bf)
    cols = channels // HEADS
    lane = lax.broadcasted_iota(jnp.int32, (channels, LANE), 1)
    pick = (lax.broadcasted_iota(jnp.int32, (channels, LANE), 0) == lane + member * cols) & (lane < cols)
    maxima = nn(cot_ref[:, width:], pick.astype(f32).astype(bf)).astype(bf)
    both = tn(resid, jnp.concatenate([j_ref[...], maxima], axis=1))
    proj_ref[...] = pack_rows(both[:, 0:hd], tall.at[0], channels // hd).astype(bf)
    short_ref[...] = pack_rows(both[:, LANE : LANE + cols], tall.at[1], channels // cols).astype(bf)


def last_kernel(dims, x_ref, g_ref, mx_ref, mg_ref, w_in, pg_in, out_ref, full, tiles, w_ref, pg_ref, sems):
    frames, rows, width, hd = dims
    half = rows // 2
    cells = rows * VW * (frames // 2)
    third = frames * half * HALF // 3
    channels = x_ref.shape[1]
    rows_in = pg_ref.shape[1]
    copies = [pltpu.make_async_copy(w_in, w_ref, sems.at[HEADS])]
    copies += [pltpu.make_async_copy(pg_in.at[n, 0:rows_in, :], pg_ref.at[n], sems.at[n]) for n in range(HEADS)]
    for copy in copies:
        copy.start()
    copies[0].wait()
    tops = jnp.zeros((cells, channels), f32)
    lows = jnp.zeros((cells, channels), f32)
    queries = []
    for n in range(HEADS):
        weight = jnp.concatenate(
            [w_ref[width + n * hd : width + (n + 1) * hd, :], w_ref[2 * width + n * hd : 2 * width + (n + 1) * hd, :]], axis=0
        )
        copies[1 + n].wait()
        packed = pg_ref[n]
        tops = tops + nn(packed[0:cells, 0 : 2 * hd], weight)
        lows = lows + nn(packed[0:cells, 2 * hd :], weight)
        queries.append(
            jnp.concatenate([packed[cells : cells + third, i * LANE : i * LANE + hd] for i in range(3)], axis=0)
        )
    for part, value in ((0, tops), (1, lows)):
        for line in range(frames // 2 * rows):
            at = (part * (frames // 2) * rows + line) * GRID
            full[at : at + GRID, :] = jnp.concatenate(
                [value[line * VW : (line + 1) * VW], jnp.zeros((GRID - VW, channels), f32)], axis=0
            )
    query = nn(jnp.concatenate(queries, axis=1), w_ref[0:width, :])
    per = rows * GRID
    per_q = half * HALF
    g = row_of(g_ref, 0, channels)
    for t in range(frames):
        cut = slice(t * per_q, (t + 1) * per_q)
        x = x_ref[t * per : (t + 1) * per, :].astype(f32)

        def spread(value):
            wide = pair_spread(value, tiles)
            lines = []
            for a in range(half):
                lines += [wide[a * GRID : (a + 1) * GRID]] * 2
            return jnp.concatenate(lines, axis=0)

        grad = full[t * per : (t + 1) * per, :] + spread(query[cut])
        hits = (x == spread(mx_ref[cut, :])).astype(f32)
        sums = jnp.concatenate(
            [hits[2 * a * GRID : (2 * a + 1) * GRID] + hits[(2 * a + 1) * GRID : (2 * a + 2) * GRID] for a in range(half)], axis=0
        )
        number = pair_reduce(sums, tiles, jnp.add)
        pool = hits * spread(mg_ref[cut, :] / number)
        unit, inverse = layer_unit(x)
        scaled = grad * g
        back = inverse * (
            scaled - jnp.mean(scaled, axis=-1, keepdims=True) - unit * jnp.mean(scaled * unit, axis=-1, keepdims=True)
        )
        out_ref[t * per : (t + 1) * per, :] = (back + pool).astype(bf)


def conv_grad_kernel(hd, mk_in, mv_in, dk_in, dv_in, out_ref, acc, mk, mv, dks, dvs, sems):
    groups = FR // 2
    lead = GRID + 4 * PLANE

    def brought(g, first):
        if first:
            cut = pl.ds(0, lead)
        else:
            cut = pl.ds(pl.multiple_of(lead + (g - 1) * 2 * PLANE, 8), 2 * PLANE)
        rows = pl.ds(pl.multiple_of(g * (CUR // groups), 16), CUR // groups)
        pairs = [(mk_in, mk, cut), (mv_in, mv, cut), (dk_in, dks, rows), (dv_in, dvs, rows)]
        return [pltpu.make_async_copy(a.at[c, :], b.at[c, :], sems.at[i, g]) for i, (a, b, c) in enumerate(pairs)]

    for g in range(groups):
        for copy in brought(g, g == 0):
            copy.start()
    acc[...] = jnp.zeros(acc.shape, f32)
    blank = jnp.zeros((GRID - VW, LANE), f32)

    def step(it, carry):
        t = it // (VW // 4)
        base = GRID + (1 + t) * PLANE + it % (VW // 4) * 4 * GRID
        for m, ref, masked in ((0, dks, mk), (1, dvs, mv)):
            quad = ref[pl.ds(pl.multiple_of(it * (4 * VW), 16), 4 * VW), :]
            for h in range(4):
                here = jnp.concatenate([quad[h * VW : (h + 1) * VW], blank], axis=0)
                turned = [pltpu.roll(here, GRID - 1, 0), here, pltpu.roll(here, 1, 0)]
                for a in range(3):
                    for b in range(3):
                        cells = masked[pl.ds(pl.multiple_of(base + (a - 1) * PLANE + (h + b - 1) * GRID, 8), GRID), :]
                        for c in range(3):
                            prod = cells * turned[c]
                            acc[m * 27 + (a * 3 + b) * 3 + c] += prod[0:8] + prod[8:16] + prod[16:24]
        return carry

    def group(g, carry):
        @pl.when(g == 0)
        def _():
            for copy in brought(0, True):
                copy.wait()

        @pl.when(g > 0)
        def _():
            for copy in brought(g, False):
                copy.wait()

        each = 2 * VW // 4
        return lax.fori_loop(g * each, (g + 1) * each, step, carry)

    lax.fori_loop(0, groups, group, 0)
    sums = [jnp.sum(acc[tap], axis=0, keepdims=True) for tap in range(54)] + [jnp.zeros((1, LANE), f32)] * 2
    sums = jnp.concatenate(sums, axis=0)
    out_ref[0:14, :] = jnp.concatenate([sums[14 * g : 14 * (g + 1), 0:hd] for g in range(4)], axis=1)
    out_ref[14:16, :] = jnp.zeros((2, 4 * hd), f32)


def late_kernel(dims, conv_ref, stat_ref, small_ref, mem_in, p_in, late_ref, tiles, lines, mem_ref, p_ref, sems):
    frames, rows, width, hd = dims
    half = rows // 2
    channels = late_ref.shape[1]
    first = pltpu.make_async_copy(p_in.at[:, 0 : p_ref.shape[1], :], p_ref, sems.at[2 * MEM])
    copies = [pltpu.make_async_copy(mem_in.at[s, m], mem_ref.at[s, m], sems.at[m * MEM + s]) for m in range(2) for s in range(MEM)]
    for copy in [first] + copies:
        copy.start()
    first.wait()
    for m in range(2):
        sums = [jnp.zeros((GRID, width), f32) for _ in range(2)]
        for s in range(MEM):
            copies[m * MEM + s].wait()
            grads = jnp.concatenate(
                [p_ref[n][0:LANE, (2 * s + m) * hd : (2 * s + m + 1) * hd] for n in range(HEADS)], axis=1
            ).astype(f32)
            for t in range(frames):
                for a in range(half):
                    at = (a * frames + t) * VH
                    some = jnp.concatenate([grads[at : at + VH], jnp.zeros((HALF - VH, width), f32)], axis=0)
                    wide = pair_spread(some, tiles.at[(t * half + a) % 4])
                    for i in range(2):
                        sums[i] = sums[i] + mem_ref[s, m, t, 2 * a + i].astype(f32) * wide
        odd = (lax.broadcasted_iota(jnp.int32, (GRID, 1), 0) % 2 == 1).astype(f32)
        for i in range(2):
            for j, keep in ((0, 1.0 - odd), (1, odd)):
                done = jnp.sum(sums[i] * keep, axis=0, keepdims=True)
                for k in range(width // channels):
                    at = LATE_COMP + 8 * k + 4 * m + 2 * i + j
                    lines[at : at + 1, :] = done[:, k * channels : (k + 1) * channels]
    lines[0:14, :] = conv_ref[0:14, :]
    lines[14:17, :] = stat_ref[0:3, :]
    count = small_ref.shape[0] // 2
    for k in range(2):
        lines[LATE_SMALL + k : LATE_SMALL + k + 1, :] = jnp.concatenate(
            [small_ref[k * count + i : k * count + i + 1, :] for i in range(count)], axis=1
        )
    tables = jnp.zeros((16, LANE), f32)
    for n in range(HEADS):
        part = p_ref[n][LANE : LANE + 16, :].astype(f32)
        tables = tables + part[:, 0:LANE] + part[:, LANE : 2 * LANE]
    lines[LATE_TABLE : LATE_TABLE + 5, :] = jnp.concatenate([tables[5 * g : 5 * (g + 1), :] for g in range(3)], axis=1)
    late_ref[...] = lines[...].astype(bf)


def add_four(got, lo, hi):
    a, b, c, d = [v[lo:hi, :].astype(f32) for v in got]
    return (a + b) + (c + d)


def unpack_rows(value, rows, lanes):
    groups = value.shape[1] // lanes
    for g in range(groups):
        rows[pl.ds(g, value.shape[0], groups), :] = pad_lanes(value[:, g * lanes : (g + 1) * lanes], LANE)


def second_kernel(dims, *refs):
    hd, cols, channels = dims
    got, (fc2_ref, proj_ref, short_ref, rows) = refs[0:4], refs[4:]
    count = proj_ref.shape[0]
    ends = np.cumsum([0, fc2_ref.shape[0], count * hd // channels, count * cols // channels])
    fc2_ref[...] = add_four(got, ends[0], ends[1])
    unpack_rows(add_four(got, ends[1], ends[2]), rows, hd)
    proj_ref[...] = rows[0:count, 0:hd]
    unpack_rows(add_four(got, ends[2], ends[3]), rows, cols)
    short_ref[...] = rows[...].T[0:cols, 0:count]


def first_kernel(hd, *refs):
    got, (fc1_ref, rows) = refs[0:4], refs[4:]
    unpack_rows(add_four(got, 0, got[0].shape[0]), rows, hd)
    fc1_ref[...] = rows[...].T[0:hd]


def sums_kernel(dims, late_ref, g1_ref, b1_ref, bqkv_ref, conv_ref, comp_ref, t_ref, h_ref, w_ref, bp_ref, bs_ref, g2_ref, b2_ref, bf1_ref, bf2_ref, lines):
    width, hd, channels = dims
    parts = []
    for n in range(HEADS):
        parts.append(late_ref[n])
    total = parts[0]
    for n in range(1, HEADS):
        total = total + parts[n]
    for g in range(4):
        conv = jnp.concatenate([parts[n][0:14, g * hd : (g + 1) * hd] for n in range(HEADS)], axis=1)
        for r in range(14):
            i = 14 * g + r
            if i < 54:
                conv_ref[i % 27 // 9, i % 9 // 3, i % 3, i // 27 : i // 27 + 1, :] = conv[r : r + 1]
    for p in range(3):
        value = jnp.concatenate([parts[n][14:15, p * hd : (p + 1) * hd] for n in range(HEADS)], axis=1)
        bqkv_ref[p * width : (p + 1) * width] = value.reshape(width)
    g1_ref[...] = total[15:16].reshape(channels)
    b1_ref[...] = total[16:17].reshape(channels)
    for i in range(8):
        value = jnp.concatenate([total[LATE_COMP + 8 * k + i : LATE_COMP + 8 * k + i + 1] for k in range(2)], axis=1)
        comp_ref[i // 4, i % 4 // 2, i % 2 : i % 2 + 1, :] = value
    for n in range(HEADS):
        value = jnp.concatenate([parts[n][LATE_SMALL + k : LATE_SMALL + k + 1] for k in range(2)], axis=1).reshape(width)
        if n == 0:
            bp_ref[...] = value
            bs_ref[...] = value
        elif n < 4:
            (g2_ref, b2_ref, bf2_ref)[n - 1][...] = value
        else:
            bf1_ref[(n - 4) * width : (n - 3) * width] = value
    share = TABLE_ROWS // HEADS
    for n in range(HEADS):
        part = parts[n][LATE_TABLE : LATE_TABLE + 5]
        value = jnp.concatenate([part[:, g * LANE : (g + 1) * LANE] for g in range(3)], axis=0)
        lines[n * share : (n + 1) * share, :] = value[0:share]
    at = 0
    for ref, step in ((t_ref, 2 * FR), (h_ref, 2 * GRID), (w_ref, 2 * GRID)):
        ref[...] = lines[at : at + ref.shape[0], 0:hd]
        at += step


def tail_kernel(dims, sums_dims, four, *refs):
    ins, refs = refs[: 7 + four], refs[7 + four :]
    x, gain, mx, mg, late = ins[0:5]
    got, (w_in, pg_in) = ins[5 : 5 + four], ins[5 + four :]
    outs, refs = refs[: 15 + four // 4], refs[15 + four // 4 :]
    full, tiles, w_ref, pg_ref, sems, lines = refs[:6]
    last_kernel(dims, x, gain, mx, mg, w_in, pg_in, outs[0], full, tiles, w_ref, pg_ref, sems)
    sums_kernel(sums_dims, late, *outs[1:15], lines)
    if four:
        first_kernel(sums_dims[1], *got, outs[15], refs[6])


def body(clip_input, memory, mem_len, res_id, norm1_gain, norm1_bias, w_qkv, b_qkv, conv_kv, compress, rel_t, rel_h, rel_w,
         w_proj, b_proj, w_short, b_short, norm2_gain, norm2_bias, w_fc1, b_fc1, w_fc2, b_fc2, cotangent):
    _, frames, rows, grid, channels = clip_input.shape
    width = w_proj.shape[0]
    mlp = w_fc1.shape[0]
    hd = width // HEADS
    half = rows // 2
    n_clip = lax.axis_size("clip")
    n_height = lax.axis_size("height")
    tm, height = lax.axis_index("tm"), lax.axis_index("height")
    member = tm * n_height + height
    side = SIDE_SMALL + (SIDE_BIG - SIDE_SMALL) * res_id[0]
    meta = jnp.stack([side, mem_len[0], tm, height, member]).astype(jnp.int32)
    cells_all = frames * rows * GRID
    valid = frames * rows * VW
    per_q = frames * half * HALF
    third = per_q // 3
    queries = HEADS * per_q
    x = clip_input.reshape(cells_all, channels)
    mem = memory[0]

    dims = (frames, rows, width, hd)
    n1, mx = call(
        functools.partial(norm_kernel, (frames, rows)),
        (shape((cells_all, channels), bf), shape((per_q, channels), f32)),
        (x, norm1_gain, norm1_bias),
        scratch=[pltpu.VMEM((channels // LANE, rows * GRID, LANE), f32)],
        smem=0,
        us=3,
    )

    def swap(value, bit):
        if bit == 4:
            return lax.ppermute(value, "tm", [(i, i ^ 1) for i in range(lax.axis_size("tm"))])
        return lax.ppermute(value, "height", [(i, i ^ bit) for i in range(n_height)])

    def near(value):
        return swap(value, 2), swap(value, 4), swap(value, 1)

    def across(x2, x4, cut):
        return swap(x2[:cut], 4), swap(x4[cut:], 2), swap(x2, 1), swap(x4, 1)

    def last(x6a, x6b):
        return swap(x6a, 1), swap(x6b, 1)

    x2, x4, x1 = near(n1)
    pay2, early = call(
        functools.partial(squeeze_kernel, dims),
        (shape((HEADS, LANE, 4 * hd), bf), shape((per_q, width + channels), bf)),
        (mem, compress, cotangent[0], mx),
        scratch=[pltpu.VMEM((4, width // LANE, GRID, LANE), f32), pltpu.VMEM((2, MEM, LANE, width), f32)],
        smem=0,
        us=5,
    )
    x2, x4, pay2 = lax.optimization_barrier((x2, x4, pay2))
    x6a, x6b, x3, x5 = across(x2, x4, cells_all // 2)
    x7a, x7b = last(x6a, x6b)
    y2 = lax.all_to_all(pay2, G, 0, 0, tiled=True)
    cut = -(-per_q // 32) * 16
    taps = lax.dynamic_slice_in_dim(conv_kv.reshape(2, 27, width), member * hd, hd, 2)
    taps = jnp.pad(taps, ((0, 0), (0, 5), (0, LANE - hd)))
    taps = jnp.concatenate([taps[0], taps[1]], axis=1)
    hdims = (frames, rows, n_height, hd)
    bias = lax.dynamic_slice_in_dim(b_qkv.reshape(3, width), member * hd, hd, 1)
    bias = jnp.pad(bias, ((0, 0), (0, LANE - hd))).reshape(1, 3 * LANE)
    vmem = pl.BlockSpec(memory_space=pltpu.VMEM)
    blocks = (n1, x2, x4, x6a, x6b, x1, x3, x5, x7a, x7b)
    kc, vc, q_all, mk, mv = pl.pallas_call(
        functools.partial(conv_kernel, hdims),
        out_shape=(
            shape((CUR, 2 * LANE), bf),
            shape((CUR, LANE), bf),
            shape((queries, LANE), bf),
            shape((FLAT, LANE), f32),
            shape((FLAT, LANE), f32),
        ),
        in_specs=[pl.BlockSpec(memory_space=pltpu.SMEM)] + [vmem] * 2 + [pl.BlockSpec(memory_space=pl.ANY)] * 11,
        out_specs=(vmem,) * 3 + (pl.BlockSpec(memory_space=pl.ANY),) * 2,
        scratch_shapes=[
            pltpu.VMEM((FLAT, LANE), f32),
            pltpu.VMEM((FLAT, LANE), f32),
            pltpu.VMEM((FR, GRID * GRID, channels), bf),
            pltpu.VMEM((2, 1, GRID * HALF, LANE), f32),
            pltpu.VMEM((queries, LANE), f32),
            pltpu.VMEM((3, hd, channels), bf),
            pltpu.SemaphoreType.DMA((HEADS * frames,)),
            pltpu.SemaphoreType.DMA((5,)),
        ],
        compiler_params=pltpu.CompilerParams(vmem_limit_bytes=56 << 20),
        cost_estimate=cost(18),
    )(meta, taps, bias, *blocks, w_qkv)
    index = np.arange(queries)
    src, local = index // per_q, index % per_q
    place = np.zeros((8, queries), np.int32)
    place[0] = src // n_height * frames + local // (half * HALF)
    place[1] = src % n_height * half + local // HALF % half
    place[2] = local % HALF
    place = jnp.asarray(place)
    wide = 384
    k_all, v_all, qt_all, o_all, l_all, joined = call(
        functools.partial(attend_kernel, hdims),
        (
            shape((KEYS, 2 * LANE), bf),
            shape((KEYS, LANE), bf),
            shape((2 * LANE, queries), bf),
            shape((hd, queries), f32),
            shape((1, queries), f32),
            shape((queries, LANE), bf),
        ),
        (meta, kc, vc, q_all, y2, rel_t, rel_h, rel_w, place),
        scratch=[
            pltpu.VMEM((LANE, KEYS), bf),
            pltpu.VMEM((TAB, hd), f32),
            pltpu.VMEM((KEYS, 2 * LANE), bf),
            pltpu.VMEM((KEYS, LANE), bf),
            pltpu.SemaphoreType.DMA((2,)),
        ],
        us=16,
        away=(0, 1),
    )
    early, joined = lax.optimization_barrier((early, joined))
    e2, e4, e1 = near(early)
    joined_rows = lax.all_to_all(joined.reshape(HEADS, per_q, LANE), G, 0, 0, tiled=True)
    k_all, joined_rows = lax.optimization_barrier((k_all, joined_rows))
    kt_all = call(turn_kernel, shape((BACK, KEYS), bf), (k_all,), smem=0, us=4)
    block = mlp // HEADS
    whole = lambda *dims: pl.BlockSpec(dims, lambda i: (0,) * len(dims))
    keep_width = 2 * width
    output, keep, acthg, dj, max_grad = pl.pallas_call(
        functools.partial(mlp_kernel, (width, hd)),
        grid=(HEADS // STEP,),
        out_shape=(
            shape((frames, half, HALF, width), bf),
            shape((per_q, keep_width), bf),
            shape((HEADS, 2 * per_q, block), bf),
            shape((HEADS, per_q, LANE), bf),
            shape((per_q, channels), f32),
        ),
        in_specs=[
            whole(HEADS, per_q, LANE),
            whole(per_q, width + channels),
            whole(width, width),
            whole(width, channels),
            whole(width),
            whole(width),
            whole(width),
            whole(width),
            pl.BlockSpec((STEP * block, width), lambda i: (i, 0)),
            whole(mlp),
            pl.BlockSpec((width, STEP * block), lambda i: (0, i)),
            whole(width),
        ],
        out_specs=(
            whole(frames, half, HALF, width),
            whole(per_q, keep_width),
            pl.BlockSpec((STEP, 2 * per_q, block), lambda i: (i, 0, 0)),
            whole(HEADS, per_q, LANE),
            whole(per_q, channels),
        ),
        scratch_shapes=[
            pltpu.VMEM((per_q, width), f32),
            pltpu.VMEM((per_q, width), bf),
            pltpu.VMEM((per_q, width), f32),
            pltpu.VMEM((per_q, width), f32),
            pltpu.VMEM((per_q, width), bf),
            pltpu.VMEM((1, mlp), f32),
        ],
        compiler_params=pltpu.CompilerParams(vmem_limit_bytes=56 << 20),
        cost_estimate=cost(14),
    )(joined_rows, early, w_proj, w_short, b_proj, b_short, norm2_gain, norm2_bias, w_fc1, b_fc1, w_fc2, b_fc2)
    dj_head = lax.all_to_all(dj, G, 0, 0, tiled=True).reshape(queries, LANE)
    keep, e2, e4, e1 = lax.optimization_barrier((keep, e2, e4, e1))
    e6a, e6b, e3, e5 = across(e2, e4, cut)
    k2, k4, k1 = near(keep)
    e7a, e7b = last(e6a, e6b)
    output = output.transpose(1, 2, 0, 3)
    acthg, dj_head, kt_all, output = lax.optimization_barrier((acthg, dj_head, kt_all, output))
    ah_head = lax.all_to_all(acthg, G, 0, 0, tiled=True)

    dk, dv, dmem, pq, small2 = call(
        functools.partial(attend_back_kernel, hdims),
        (
            shape((CUR, LANE), f32),
            shape((CUR, LANE), f32),
            shape((HEADS, LANE + 16, 4 * hd), bf),
            shape((queries, LANE), f32),
            shape((width // (LANE - hd), LANE - hd), f32),
        ),
        (qt_all, q_all, o_all, l_all, dj_head, rel_t, rel_h, rel_w, place, k_all, kt_all, v_all),
        scratch=[
            pltpu.VMEM((LANE, queries), bf),
            pltpu.VMEM((hd + 48, queries), f32),
            pltpu.VMEM((TAB, hd), f32),
            pltpu.VMEM((TAB, queries), f32),
            pltpu.VMEM((KEYS, LANE), f32),
            pltpu.VMEM((KEYS, LANE), f32),
            pltpu.VMEM((1, queries), f32),
            pltpu.VMEM((TABLE_ROWS, LANE), f32),
            pltpu.VMEM((KEYS, 2 * LANE), bf),
            pltpu.VMEM((BACK, KEYS), bf),
            pltpu.VMEM((KEYS, LANE), bf),
            pltpu.SemaphoreType.DMA((4, 2)),
        ],
        smem=0,
        us=25,
        far=3,
        away=(0, 1),
    )
    cols = channels // HEADS
    taken = dmem.shape[1]
    mk, k2, k4, k1 = lax.optimization_barrier((mk, k2, k4, k1))
    k6a, k6b, k3, k5 = across(k2, k4, cut)
    k7a, k7b = last(k6a, k6b)
    gconv = call(
        functools.partial(conv_grad_kernel, hd),
        shape((16, 4 * hd), f32),
        (mk, mv, dk, dv),
        scratch=[pltpu.VMEM((54, 8, LANE), f32)]
        + [pltpu.VMEM((FLAT, LANE), f32)] * 2
        + [pltpu.VMEM((CUR, LANE), f32)] * 2
        + [pltpu.SemaphoreType.DMA((4, FR // 2))],
        smem=0,
        us=12,
        far=4,
    )
    dmem, gconv = lax.optimization_barrier((dmem, gconv))
    outs = (
        shape((width, block), bf),
        shape((HEADS, taken + block * hd // channels, channels), bf),
        shape((width * hd // channels, channels), bf),
        shape((width // HEADS, channels), bf),
    )
    fc2p, fc1p, projp, shortp = call(
        functools.partial(weight_grad_kernel, (width, hd, channels, per_q)),
        outs,
        (meta, ah_head, joined, dmem, early, e2, e4, e6a, e6b, e1, e3, e5, e7a, e7b, keep, k2, k4, k6a, k6b, k1, k3, k5, k7a, k7b),
        scratch=[
            pltpu.VMEM((queries, block), bf),
            pltpu.VMEM((queries, block), bf),
            pltpu.VMEM((2, width, LANE), f32),
            pltpu.VMEM((2, block, LANE), f32),
            pltpu.VMEM((queries, width + channels), bf),
            pltpu.VMEM((queries, 2 * width), bf),
            pltpu.SemaphoreType.DMA((2, 10)),
        ],
        us=9,
        far=20,
    )

    def over_four(sent):
        got = [lax.ppermute(sent[k], "clip", [(i, i ^ k) for i in range(n_clip)]) for k in range(1, n_clip)]
        first, second, third_, fourth = [v.astype(f32) for v in [sent[0]] + got]
        return (first + second) + (third_ + fourth)

    clip = lax.axis_index("clip")

    def send_four(block):
        return [block(clip)] + [lax.ppermute(block(clip ^ k), "clip", [(i, i ^ k) for i in range(n_clip)]) for k in range(1, n_clip)]

    def add(got):
        return (got[0].astype(f32) + got[1].astype(f32)) + (got[2].astype(f32) + got[3].astype(f32))

    dk, fc1p = lax.optimization_barrier((dk, fc1p))
    first_back = lax.all_to_all(fc1p, G, 0, 0, tiled=True)
    own = [v.reshape(n_clip, v.shape[0] // n_clip, channels) for v in (fc2p, projp, shortp)]
    if n_clip == 4:
        together = jnp.concatenate(own, axis=1)
        got2 = send_four(lambda c: lax.dynamic_index_in_dim(together, c, 0, keepdims=False))
    else:
        got2 = lax.all_to_all(jnp.concatenate(own, axis=1), "clip", 0, 0, tiled=True)
    sent = valid // 2 + third
    pgp, stats = pl.pallas_call(
        functools.partial(conv_back_kernel, hdims),
        out_shape=(shape((HEADS, sent + 48, 4 * hd), bf), shape((8, channels), f32)),
        in_specs=[pl.BlockSpec(memory_space=pltpu.SMEM)] + [vmem] * 6 + [pl.BlockSpec(memory_space=pl.ANY)] * 11,
        out_specs=(vmem,) * 2,
        scratch_shapes=[
            pltpu.VMEM((FR * GRID * GRID, 3 * LANE), bf),
            pltpu.VMEM((FLAT, LANE), f32),
            pltpu.VMEM((FLAT, LANE), f32),
            pltpu.VMEM((2 * queries, LANE), f32),
            pltpu.VMEM((FR, GRID * GRID, channels), bf),
            pltpu.VMEM((2, 3 * hd, LANE), f32),
            pltpu.VMEM((3, hd, channels), bf),
            pltpu.SemaphoreType.DMA((HEADS * frames,)),
            pltpu.SemaphoreType.DMA((3,)),
        ],
        compiler_params=pltpu.CompilerParams(vmem_limit_bytes=56 << 20),
        cost_estimate=cost(18),
    )(meta, dk, dv, pq, taps, norm1_gain, norm1_bias, *blocks, w_qkv)
    pgp, first_back, got2 = lax.optimization_barrier((pgp, first_back, got2))
    pg_rows = lax.all_to_all(pgp, G, 0, 0, tiled=True)
    if n_clip == 4:
        each = HEADS // n_clip
        got1 = send_four(
            lambda c: lax.dynamic_slice(first_back, (c * each, taken, 0), (each, first_back.shape[1] - taken, channels))
        )
    else:
        got1 = lax.all_to_all(first_back[:, taken:].reshape(n_clip, -1, channels), "clip", 0, 0, tiled=True)
    late = call(
        functools.partial(late_kernel, dims),
        shape((LATE, channels), bf),
        (gconv, stats, small2, mem, first_back),
        scratch=[
            pltpu.VMEM((4, width // LANE, GRID, LANE), f32),
            pltpu.VMEM((LATE, channels), f32),
            pltpu.VMEM(mem.shape, bf),
            pltpu.VMEM((HEADS, taken, channels), bf),
            pltpu.SemaphoreType.DMA((2 * MEM + 1,)),
        ],
        smem=0,
        us=5,
        far=2,
    )
    if n_clip == 4:
        late = over_four([late] * n_clip)
    else:
        late = jnp.sum(lax.all_gather(late, "clip", axis=0).astype(f32), axis=0)
    if n_clip == 4:
        count = width // n_clip
        part_fc2, part_proj, part_short = call(
            functools.partial(second_kernel, (hd, cols, channels)),
            (shape((count, block), f32), shape((count, hd), f32), shape((cols, count), f32)),
            tuple(got2),
            scratch=[pltpu.VMEM((-(-count // LANE) * LANE, LANE), f32)],
            smem=0,
            us=2,
        )
        late, part_fc2 = lax.optimization_barrier((late, part_fc2))
    late_full = lax.all_gather(late, G, axis=0)
    pg_rows, late_full, got1 = lax.optimization_barrier((pg_rows, late_full, got1))
    vector = lambda n: shape((n,), f32)
    qkv_rows = pg_rows[:, sent : sent + 3 * hd // HEADS]
    qkv_rows = qkv_rows.reshape(HEADS, 3, hd // HEADS, channels).transpose(1, 0, 2, 3).reshape(-1, channels)
    got = lax.all_to_all(qkv_rows.reshape(n_clip, -1, channels), "clip", 0, 0, tiled=True)
    four = 4 if n_clip == 4 else 0
    results = call(
        functools.partial(tail_kernel, dims, (width, hd, channels), four),
        (
            shape((cells_all, channels), bf),
            vector(channels), vector(channels), vector(3 * width), shape((3, 3, 3, 2, width), f32), shape(compress.shape, f32),
            shape(rel_t.shape, f32), shape(rel_h.shape, f32), shape(rel_w.shape, f32),
            vector(width), vector(width), vector(width), vector(width), vector(mlp), vector(width),
        )
        + ((shape((hd, mlp // n_clip), f32),) if four else ()),
        (x, norm1_gain, mx, max_grad, late_full)
        + (tuple(v.reshape(-1, channels) for v in got1) if four else ())
        + (w_qkv, pg_rows),
        scratch=[
            pltpu.VMEM((cells_all, channels), f32),
            pltpu.VMEM((width // LANE, rows * GRID, LANE), f32),
            pltpu.VMEM(w_qkv.shape, bf),
            pltpu.VMEM((HEADS, sent, channels), bf),
            pltpu.SemaphoreType.DMA((HEADS + 1,)),
            pltpu.VMEM((TABLE_ROWS, LANE), f32),
        ]
        + ([pltpu.VMEM((mlp // n_clip, LANE), f32)] if four else []),
        smem=0,
        us=9,
        far=2,
    )
    input_grad, g1, b1, gbq, gconv, gcomp, gt, gh, gw, gbp, gbs, g2, b2, gb1, gb2 = results[:15]
    part_qkv = jnp.sum(got.astype(f32), axis=0).reshape(-1, cols)
    if n_clip == 4:
        part_fc1 = results[15].T
        part_short = part_short.T
    else:
        part_fc1, part2 = (jnp.sum(v.astype(f32), axis=0) for v in (got1, got2))
        ends = np.cumsum([v.shape[1] for v in own])
        part_fc2, part_proj, part_short = part2[: ends[0]], part2[ends[0] : ends[1]], part2[ends[1] :]
        part_fc1, part_proj, part_short = part_fc1.reshape(-1, hd), part_proj.reshape(-1, hd), part_short.reshape(-1, cols)
    return (
        output.transpose(2, 0, 1, 3)[None],
        input_grad.reshape(clip_input.shape),
        g1,
        b1,
        part_qkv,
        gbq,
        jnp.moveaxis(gconv, 3, 0),
        gcomp,
        gt,
        gh,
        gw,
        part_proj,
        gbp,
        part_short,
        gbs,
        g2,
        b2,
        part_fc1,
        gb1,
        part_fc2,
        gb2,
    )


def solution(mesh):
    split = P("clip", "tm", "height", None, None)
    shared = P()
    weight = P("clip", ("tm", "height"))
    placed = (split, P("clip", None, None, "tm", "height", None, None), P("clip"), P("clip")) + (shared,) * 19 + (split,)
    outs = (split, split, shared, shared, weight) + (shared,) * 6 + (weight, shared, weight, shared, shared, shared, weight, shared, weight, shared)
    return jax.shard_map(body, mesh=mesh, in_specs=placed, out_specs=outs, check_vma=False)
```
